128 devices in a mesh: feat: 8 (over z, core), node: 16 (over y, x).
Axes of the slice: x: 4, y: 4, z: 4, core: 2. Of those that a mesh axis runs over, the one named last changes fastest.
Arguments:
- features: bfloat16 [8, 16384, 1024], P(None, 'node', 'feat'), may hold values from -6 to 6
- w_one: bfloat16 [1024, 512], P('feat'), may hold values from -0.1875 to 0.1875
- w_two: bfloat16 [256, 512], replicated, may hold values from -0.375 to 0.375
- b_one: float32 [256], replicated, may hold values from -3 to 3
- b_two: float32 [256], replicated, may hold values from -3 to 3
- owner_one: int32 [8, 8192, 8], P('feat', 'node'), may hold values from 0 to 15, all different within a row; in each aligned block of 512 rows (0 to 511, 512 to 1023, ..., all dimensions but the last counted through in order) at most 384 rows name the same one
- slot_one: int32 [8, 8192, 8], P('feat', 'node'), may hold values from 0 to 1023
- owner_two: int32 [8, 4096, 8], P('feat', 'node'), may hold values from 0 to 15, all different within a row; in each aligned block of 256 rows (0 to 255, 256 to 511, ..., all dimensions but the last counted through in order) at most 192 rows name the same one
- slot_two: int32 [8, 4096, 8], P('feat', 'node'), may hold values from 0 to 511
- cotangent: float32 [8, 4096, 256], P('feat', 'node'), may hold values from -0.3125 to 0.3125
Outputs:
- layer_out: bfloat16 [8, 4096, 256], P('feat', 'node')
- grad_w_one: float32 [1024, 512], P('feat')
- grad_w_two: float32 [256, 512], replicated
- grad_b_one: float32 [256], replicated
The draws below stay inside these ranges and needn't reach their ends.
Inputs may be any that keep to these rules, and one draw needn't show every extreme that they name: `owner_one`: each row names 8 different owners; within the rows of one device (aligned blocks of 512 rows, in order) no owner is named by more than 384 rows, a bound that some block reaches. `owner_two`: each row names 8 different owners; within the rows of one device (aligned blocks of 256 rows, in order) no owner is named by more than 192 rows, a bound that some block reaches.
All inputs are finite; a program needn't handle non-finite values.
Results may differ from the reference program's by a relative error of at most 0.02.
Values may be sent and summed in bfloat16 or wider, within the bound.
A program may use at most 128 MiB of HBM per device.

```python
import math
import jax
import jax.numpy as jnp
import numpy as np
from jax import lax

F = 1024
H = 256
K = 8
R1_DEV = 1024
R2_DEV = 512
R3_DEV = 256
CAP1 = 384
CAP2 = 192
M1 = 16384
M2 = 8192
M3 = 4096
N_FEAT = 8
N_NODE = 16


def set_ends(values, own_key, smallest, high):
    dims = values.shape
    index_at = [jax.random.randint(jax.random.fold_in(own_key, axis), (), 0, dims[axis]) for axis in range(len(dims))]
    values = values.at[tuple(index_at)].set(smallest)
    longest = dims.index(max(dims))
    index_at[longest] = (index_at[longest] + 1) % dims[longest]
    return values.at[tuple(index_at)].set(high)


def steps_of(own_key, extent, split, smallest, largest):
    def one(dim, blocks):
        steps = jax.random.uniform(jax.random.fold_in(jax.random.fold_in(own_key, 6), dim), (blocks,), jnp.float32, smallest / len(split), largest / len(split))
        return jnp.repeat(jnp.exp(steps), extent[dim] // blocks).reshape((-1,) + (1,) * (len(extent) - dim - 1))

    factor_of = one(*split[0])
    for cut in split[1:]:
        factor_of = factor_of * one(*cut)
    return factor_of


def deal_out(key, own, number, rows, number_of, top, limit, slope):
    ranking = jax.random.permutation(key, number_of)
    heavy_load, common = load_shares(number_of, rows * top, limit, slope, True), load_shares(number_of, rows * top, limit, slope, False)
    places = jnp.arange(number_of)

    def named(tallies, rotation):
        used = int((tallies > 0).sum())
        fixed = max(1, used // 4)
        moved = fixed + (places - fixed + rotation * (used - fixed)) % max(1, number_of - fixed)
        return jnp.zeros((number_of,), jnp.int32).at[ranking[jnp.where(places < fixed, places, moved)]].set(jnp.asarray(tallies, jnp.int32))

    tallies = jnp.where(number % 4 == 0, named(heavy_load, number // 4), named(common, number - number // 4 - 1))
    mixed = jax.random.permutation(jax.random.fold_in(own, 3), number_of)
    source_of, sink = mixed[0:number_of // 2 * 2:2], mixed[1:number_of // 2 * 2:2]
    room = jnp.minimum(tallies[source_of] - 1, limit - tallies[sink]) // 2
    room = jnp.where((source_of == ranking[0]) | (sink == ranking[0]) | (tallies[sink] == 0), 0, jnp.maximum(room, 0))
    moved = jax.random.randint(jax.random.fold_in(own, 4), (number_of // 2,), 0, 1 << 20) % (room + 1)
    tallies = tallies.at[source_of].add(-moved).at[sink].add(moved)
    members = jnp.searchsorted(jnp.cumsum(tallies), jnp.arange(rows * top), side="right").astype(jnp.int32)
    grid = members.reshape(top, rows).T
    grid = grid[jax.random.permutation(jax.random.fold_in(own, 1), rows)]
    rotation = jax.random.randint(jax.random.fold_in(own, 2), (rows, 1), 0, top)
    return jnp.take_along_axis(grid, (jnp.arange(top)[None, :] + rotation) % top, axis=1)


def load_shares(amount, total, limit, skew, full):
    loads = [(1 << 20) // math.isqrt(rank ** skew) + 1 for rank in range(1, amount + 1)]
    largest = limit if full else min(limit, max(-(-total // amount), total * loads[0] // sum(loads)))
    least = 1 if total - largest >= amount - 1 else 0
    given, surplus = [largest] + [least] * (amount - 1), total - largest - least * (amount - 1)
    while surplus > 0:
        candidates = [i for i in range(1, amount) if given[i] < largest] or [i for i in range(1, amount) if given[i] < limit]
        whole, left = sum([loads[i] for i in candidates]), surplus
        for i in candidates:
            more = min(limit - given[i], max(1, left * loads[i] // whole), surplus)
            given[i] = given[i] + more
            surplus = surplus - more
    return np.array(given)


def noise(own_key, dims, deviation, reach, pieces=(), kind=jnp.bfloat16):
    array = jax.random.normal(own_key, dims, jnp.float32) * deviation
    if len(pieces) > 0:
        array = steps_of(own_key, dims, pieces, -0.22, 0.18) * array
    return jnp.clip(array, min=-reach, max=reach).astype(kind)


def setup_inputs(seed: int = 0) -> dict:
    keys = jax.random.split(jax.random.key(seed), 11)
    features = noise(keys[0], (N_FEAT, M1, F), 1.0, 6.0, ((1, 16), (2, 8)))
    w_one = noise(keys[1], (F, 2 * H), F ** -0.5, 0.1875, ((0, 8),))
    w_two = noise(keys[2], (H, 2 * H), H ** -0.5, 0.375)
    b_one = noise(keys[3], (H,), 0.5, 3.0, (), jnp.float32)
    b_two = noise(keys[4], (H,), 0.5, 3.0, (), jnp.float32)
    owner_one_keys = jax.random.split(jax.random.fold_in(keys[5], 1), N_FEAT * M2 // R2_DEV)
    owner_one_turns = jax.random.permutation(jax.random.fold_in(keys[5], 3), N_FEAT * M2 // R2_DEV)
    owner_one = jax.vmap(lambda own, number: deal_out(jax.random.fold_in(keys[5], 2), own, number, R2_DEV, N_NODE, K, CAP1, 1))(owner_one_keys, owner_one_turns).reshape((N_FEAT, M2, K))
    slot_one = set_ends(jax.random.randint(keys[6], (N_FEAT, M2, K), 0, R1_DEV), jax.random.fold_in(keys[6], 1), 0, R1_DEV - 1).astype(jnp.int32)
    owner_two_keys = jax.random.split(jax.random.fold_in(keys[7], 1), N_FEAT * M3 // R3_DEV)
    owner_two_turns = jax.random.permutation(jax.random.fold_in(keys[7], 3), N_FEAT * M3 // R3_DEV)
    owner_two = jax.vmap(lambda own, number: deal_out(jax.random.fold_in(keys[7], 2), own, number, R3_DEV, N_NODE, K, CAP2, 1))(owner_two_keys, owner_two_turns).reshape((N_FEAT, M3, K))
    slot_two = set_ends(jax.random.randint(keys[8], (N_FEAT, M3, K), 0, R2_DEV), jax.random.fold_in(keys[8], 1), 0, R2_DEV - 1).astype(jnp.int32)
    cotangent = noise(keys[9], (N_FEAT, M3, H), 0.02, 0.3125, ((0, 8), (1, 16)), jnp.float32)
    return {"features": features, "w_one": w_one, "w_two": w_two, "b_one": b_one, "b_two": b_two, "owner_one": owner_one, "slot_one": slot_one, "owner_two": owner_two, "slot_two": slot_two, "cotangent": cotangent}


def silu_slope(linear):
    logistic = jax.nn.sigmoid(linear)
    return logistic * (1.0 + linear * (1.0 - logistic))


def spread_rows(target_rows, indices, message, fanout, hidden):
    edges = jnp.broadcast_to(message.astype(jnp.float32)[:, None, :], (message.shape[0], fanout, hidden))
    start_zero = jnp.zeros((target_rows, hidden), jnp.float32)
    return start_zero.at[indices.reshape(-1)].add(edges.reshape(-1, hidden))


def one_group(features_g, w_one, w_two, b_one, b_two, own_one, slo_one, own_two, slo_two, grad_out):
    columns = F // N_FEAT
    proj_one = jnp.zeros((M1, 2 * H), jnp.float32)
    for slice_index in range(N_FEAT):
        lower = slice_index * columns
        piece_prod = jnp.dot(features_g[:, lower:lower + columns], w_one[lower:lower + columns], preferred_element_type=jnp.float32)
        proj_one = proj_one + piece_prod.astype(jnp.bfloat16).astype(jnp.float32)
    table_one = proj_one[:, H:].astype(jnp.bfloat16)
    targets = jnp.arange(M2, dtype=jnp.int32)
    self_one = (targets // R2_DEV) * R1_DEV + targets % R2_DEV
    neighbour_one = own_one * R1_DEV + slo_one
    mean_one = jnp.sum(table_one[neighbour_one].astype(jnp.float32), axis=1) / K
    linear_one = proj_one[self_one, :H] + b_one + mean_one
    hidden_one = jax.nn.silu(linear_one).astype(jnp.bfloat16)
    proj_two = jnp.dot(hidden_one, w_two, preferred_element_type=jnp.float32)
    table_two = proj_two[:, H:].astype(jnp.bfloat16)
    seeds = jnp.arange(M3, dtype=jnp.int32)
    self_two = (seeds // R3_DEV) * R2_DEV + seeds % R3_DEV
    neighbour_two = own_two * R2_DEV + slo_two
    mean_two = jnp.sum(table_two[neighbour_two].astype(jnp.float32), axis=1) / K
    layer_out = (proj_two[self_two, :H] + b_two + mean_two).astype(jnp.bfloat16)
    message_two = (grad_out / K).astype(jnp.bfloat16)
    grad_table_two = spread_rows(M2, neighbour_two, message_two, K, H)
    grad_self_two = jnp.zeros((M2, H), jnp.float32).at[self_two].set(grad_out)
    grad_proj_two = jnp.concatenate([grad_self_two, grad_table_two], axis=1).astype(jnp.bfloat16)
    grad_w_two = jnp.dot(hidden_one.T, grad_proj_two, preferred_element_type=jnp.float32)
    grad_hidden_one = jnp.dot(grad_proj_two, w_two.T, preferred_element_type=jnp.float32)
    grad_linear_one = grad_hidden_one * silu_slope(linear_one)
    grad_b_one = jnp.sum(grad_linear_one, axis=0)
    message_one = (grad_linear_one / K).astype(jnp.bfloat16)
    grad_table_one = spread_rows(M1, neighbour_one, message_one, K, H)
    grad_self_one = jnp.zeros((M1, H), jnp.float32).at[self_one].set(grad_linear_one)
    grad_proj_one = jnp.concatenate([grad_self_one, grad_table_one], axis=1).astype(jnp.bfloat16)
    grad_w_one = jnp.dot(features_g.T, grad_proj_one, preferred_element_type=jnp.float32)
    return layer_out, grad_w_one, grad_w_two, grad_b_one


def reference(features, w_one, w_two, b_one, b_two, owner_one, slot_one, owner_two, slot_two, cotangent):
    def step_group(index):
        return one_group(features[index], w_one, w_two, b_one, b_two, owner_one[index], slot_one[index], owner_two[index], slot_two[index], cotangent[index])

    outputs, grads_w_one, grads_w_two, grads_b_one = lax.map(step_group, jnp.arange(N_FEAT, dtype=jnp.int32))
    return outputs, jnp.sum(grads_w_one, axis=0), jnp.sum(grads_w_two, axis=0), jnp.sum(grads_b_one, axis=0)
```

```python
import functools

import jax
import jax.numpy as jnp
from jax import lax
from jax.experimental import pallas as pl
from jax.experimental.pallas import tpu as pltpu
from jax.sharding import PartitionSpec as P

MESH = pl.DeviceIdType.MESH
CHUNKS = 4
FEATS = 8
SIDE = 4
BF = jnp.bfloat16
F32 = jnp.float32


def line_place(core, node):
    low, high = node % SIDE, node // SIDE
    return (1 - core) * low + core * high, (1 - core) * high + core * low


def node_at(core, u, v):
    return (1 - core) * (v * SIDE + u) + core * (u * SIDE + v)


def dot(a, b, dims=((1,), (0,))):
    return lax.dot_general(a, b, (dims, ((), ())), preferred_element_type=F32)


def step_kernel(
    feat_ref, w_one_ref, w_two_ref, b_one_ref, b_two_ref, asks_ref, cot_ref,
    out_ref, gw_one_ref, gw_two_ref, gb_ref,
    slab, w_parts, w_full, asks, asks_col, msg_two, gsum_two, gsend_two, grecv_two,
    gproj_two, ghid, table, self_one, ysum, ysend, yrecv, hidden, self_two,
    table_two, ysum_two, ysend_two, yrecv_two, glin, msg_one, gsum, gsend, grecv,
    w_out, w_in, w_mid, v_in, z_out, z_in, piece_all,
    ssem, rsem, lsem,
):
    f, n = lax.axis_index("feat"), lax.axis_index("node")
    core = f % 2
    u, v = line_place(core, n)
    rows_one = slab.shape[1]
    rows_two = asks_col.shape[1] * 2 // 3
    rows_three = rows_two // 2
    fan = 8.0
    part = rows_one // CHUNKS

    def feat_dev(i):
        return ((f + i + FEATS) % FEATS, n)

    def u_dev(d):
        return (f, node_at(core, (u + d + SIDE) % SIDE, v))

    def v_dev(e):
        return (f, node_at(core, u, (v + e + SIDE) % SIDE))

    used = [0]

    def send(src, dst, dev):
        k = used[0]
        used[0] += 1
        copy = pltpu.make_async_remote_copy(
            src_ref=src, dst_ref=dst, send_sem=ssem.at[k], recv_sem=rsem.at[k],
            device_id=dev, device_id_type=MESH,
        )
        copy.start()
        return copy

    started = []

    def keep(copy):
        started.append(copy)
        return copy

    barrier = pltpu.get_barrier_semaphore()
    partners = [feat_dev(i) for i in range(1, FEATS)]
    partners += [u_dev(d) for d in range(1, SIDE)] + [v_dev(e) for e in range(1, SIDE)]
    for dev in partners:
        pl.semaphore_signal(barrier, inc=1, device_id=dev, device_id_type=MESH)
    pl.semaphore_wait(barrier, len(partners))

    ask_copies = {
        e: keep(send(asks_ref.at[e], asks.at[e], v_dev(e))) for e in range(1, SIDE)
    }
    low, high = n % SIDE, n // SIDE
    w_copies = []
    for i in range(1, FEATS):
        their_core = (core + i) % 2
        their_u, their_v = line_place(their_core, n)
        w_copies.append(keep(send(
            w_one_ref.at[pl.ds(pl.multiple_of(high * 32, 32), 32),
                         pl.ds(pl.multiple_of(low * 128, 128), 128)],
            w_parts.at[i, their_u, their_v], feat_dev(i),
        )))
    msg_two[0] = (cot_ref[...] / fan).astype(BF)
    msg_two_copies = {
        e: keep(send(msg_two.at[0], msg_two.at[e], v_dev(e))) for e in range(1, SIDE)
    }
    own = pltpu.make_async_copy(feat_ref.at[f], slab.at[0], lsem)
    own.start()
    slab_copies = []
    for q in range(CHUNKS):
        rows = pl.ds(q * part, part)
        slab_copies.append([
            keep(send(feat_ref.at[(f + i) % FEATS, rows], slab.at[i, rows], feat_dev(i)))
            for i in (4, 5, 3, 2, 6, 7, 1)
        ])

    for copy in w_copies:
        copy.wait_recv()
    along_u = [
        keep(send(w_parts.at[pl.ds(1, FEATS - 1), u, v], w_parts.at[pl.ds(1, FEATS - 1), u, v],
                  u_dev(d)))
        for d in range(1, SIDE)
    ]

    asks[0] = asks_ref[0]
    for e in range(SIDE):
        if e > 0:
            ask_copies[e].wait_recv()
        asks_col[e] = jnp.transpose(asks[e].astype(F32)).astype(jnp.int32)

    def take_two(e, d):
        ids = lax.broadcasted_iota(jnp.int32, (rows_two, rows_three), 0)
        return (ids == asks[e, d:d + 1, rows_two:]).astype(BF)

    for e in range(1, SIDE):
        msg_two_copies[e].wait_recv()
    back_two = {}
    for d in (2, 1, 3, 0):
        total = jnp.zeros((rows_two, 256), F32)
        for e in range(SIDE):
            total += dot(take_two(e, d), msg_two[e])
        if d:
            gsend_two[d - 1] = total.astype(BF)
            back_two[d] = keep(send(gsend_two.at[d - 1], grecv_two.at[d - 1], u_dev(-d)))
        else:
            gsum_two[...] = total

    for copy in along_u:
        copy.wait_recv()
    along_v = [
        keep(send(w_parts.at[pl.ds(1, FEATS - 1), :, v], w_parts.at[pl.ds(1, FEATS - 1), :, v],
                  v_dev(e)))
        for e in range(1, SIDE)
    ]

    for d in range(1, SIDE):
        back_two[d].wait_recv()
    gtab_two = gsum_two[...]
    for d in range(1, SIDE):
        gtab_two += grecv_two[d - 1].astype(F32)
    gproj_two[:rows_three, :256] = cot_ref[...].astype(BF)
    gproj_two[rows_three:, :256] = jnp.zeros((rows_two - rows_three, 256), BF)
    gproj_two[:, 256:] = gtab_two.astype(BF)
    ghid[...] = dot(gproj_two[...], w_two_ref[...], ((1,), (1,)))

    for copy in along_v:
        copy.wait_recv()
    w_full[:128] = w_one_ref[...]
    for i in range(1, FEATS):
        for r in range(4):
            for q in range(4):
                a, b = (1 - core) * q + core * r, (1 - core) * r + core * q
                w_full[i * 128 + r * 32:i * 128 + r * 32 + 32, q * 128:q * 128 + 128] = (
                    w_parts[i, a, b]
                )

    own.wait()
    table_copies = {d: [] for d in range(1, SIDE)}
    for q in range(CHUNKS):
        for copy in slab_copies[q]:
            copy.wait_recv()
        lower = q * part
        block = jnp.concatenate([slab[i, lower:lower + part] for i in range(FEATS)], axis=1)
        if lower < rows_two:
            self_one[lower:lower + part] = dot(block, w_full[:, :256])
        table[0, lower:lower + part] = dot(block, w_full[:, 256:]).astype(BF)
        rows = pl.ds(lower, part)
        for d in (2, 1, 3):
            table_copies[d].append(
                keep(send(table.at[0, rows], table.at[d, rows], u_dev(d)))
            )

    def pick_one(e, d):
        ids = lax.broadcasted_iota(jnp.int32, (rows_two, rows_one), 1)
        return (ids == asks_col[e, :rows_two, d:d + 1]).astype(BF)

    for d in (0, 1, 3):
        if d:
            for copy in table_copies[d]:
                copy.wait_recv()

        def add_line(e, carry, d=d):
            value = dot(pick_one(e, d), table[d])
            ysum[e] = value if d == 0 else ysum[e] + value
            return carry

        lax.fori_loop(0, SIDE, add_line, 0)
    for copy in table_copies[2]:
        copy.wait_recv()
    y_copies = {}
    for e in (2, 1, 3, 0):
        value = ysum[e] + dot(pick_one(e, 2), table[2])
        if e:
            ysend[e - 1] = value.astype(BF)
            y_copies[e] = keep(send(ysend.at[e - 1], yrecv.at[e - 1], v_dev(-e)))
        else:
            ysum[0] = value
    for e in range(1, SIDE):
        y_copies[e].wait_recv()
    total = ysum[0]
    for e in range(1, SIDE):
        total += yrecv[e - 1].astype(F32)
    linear = self_one[...] + b_one_ref[...] + total / fan
    logistic = 1.0 / (1.0 + jnp.exp(-linear))
    hidden[...] = (linear * logistic).astype(BF)
    grad = ghid[...] * (logistic * (1.0 + linear * (1.0 - logistic)))
    glin[...] = grad.astype(BF)
    msg_one[0] = (grad / fan).astype(BF)
    msg_copies = {
        e: keep(send(msg_one.at[0], msg_one.at[e], v_dev(e))) for e in (2, 1, 3)
    }
    bias = jnp.sum(grad, axis=0, keepdims=True)

    proj = dot(hidden[...], w_two_ref[...])
    self_two[...] = proj[:rows_three, :256]
    table_two[0] = proj[:, 256:].astype(BF)
    table_two_copies = {
        d: keep(send(table_two.at[0], table_two.at[d], u_dev(d))) for d in (2, 1, 3)
    }
    gw_two = dot(hidden[...], gproj_two[...], ((0,), (0,))).astype(BF)
    for r in range(4):
        for q in range(4):
            a, b = (1 - core) * q + core * r, (1 - core) * r + core * q
            w_out[a, b, 256:320] = gw_two[r * 64:r * 64 + 64, q * 128:q * 128 + 128]
            if r == 0 and q < 2:
                w_out[a, b, 320:336] = jnp.broadcast_to(
                    bias[:, q * 128:q * 128 + 128], (16, 128)
                ).astype(BF)
            else:
                w_out[a, b, 320:336] = jnp.zeros((16, 128), BF)

    def take_one(e, d):
        ids = lax.broadcasted_iota(jnp.int32, (rows_one, rows_two), 0)
        return (ids == asks[e, pl.ds(d, 1), :rows_two]).astype(BF)

    for e in (0, 1, 3):
        if e:
            msg_copies[e].wait_recv()

        def add_back(d, carry, e=e):
            value = dot(take_one(e, d), msg_one[e])
            gsum[d] = value if e == 0 else gsum[d] + value
            return carry

        lax.fori_loop(0, SIDE, add_back, 0)
    msg_copies[2].wait_recv()
    back_one = {}
    for d in (2, 1, 3, 0):
        value = gsum[d] + dot(take_one(2, d), msg_one[2])
        if d:
            gsend[d - 1] = value.astype(BF)
            back_one[d] = keep(send(gsend.at[d - 1], grecv.at[d - 1], u_dev(-d)))
        else:
            gsum[0] = value

    def pick_two(e, d):
        ids = lax.broadcasted_iota(jnp.int32, (rows_three, rows_two), 1)
        return (ids == asks_col[e, rows_two:, d:d + 1]).astype(BF)

    for d in range(1, SIDE):
        table_two_copies[d].wait_recv()
    y_two = {}
    for e in (2, 1, 3, 0):
        value = jnp.zeros((rows_three, 256), F32)
        for d in range(SIDE):
            value += dot(pick_two(e, d), table_two[d])
        if e:
            ysend_two[e - 1] = value.astype(BF)
            y_two[e] = keep(send(ysend_two.at[e - 1], yrecv_two.at[e - 1], v_dev(-e)))
        else:
            ysum_two[...] = value

    for d in range(1, SIDE):
        back_one[d].wait_recv()
    total = gsum[0]
    for d in range(1, SIDE):
        total += grecv[d - 1].astype(F32)
    gtab = total.astype(BF)
    for half in range(2):
        block = jnp.concatenate([slab[half * 4 + i] for i in range(4)], axis=1)
        left = dot(block[:rows_two], glin[...], ((0,), (0,))).astype(BF)
        right = dot(block, gtab, ((0,), (0,))).astype(BF)
        for i in range(4):
            for r in range(4):
                for q in range(4):
                    a, b = (1 - core) * q + core * r, (1 - core) * r + core * q
                    side = left if q < 2 else right
                    w_out[a, b, (half * 4 + i) * 32:(half * 4 + i) * 32 + 32] = side[
                        i * 128 + r * 32:i * 128 + r * 32 + 32,
                        (q % 2) * 128:(q % 2) * 128 + 128]

    sums = [
        keep(send(w_out.at[(u + d) % SIDE], w_in.at[d - 1], u_dev(d))) for d in (2, 1, 3)
    ]
    for e in range(1, SIDE):
        y_two[e].wait_recv()
    total = ysum_two[...]
    for e in range(1, SIDE):
        total += yrecv_two[e - 1].astype(F32)
    out_ref[...] = (self_two[...] + b_two_ref[...] + total / fan).astype(BF)
    for copy in sums:
        copy.wait_recv()
    total = w_out[u].astype(F32)
    for d in range(1, SIDE):
        total += w_in[d - 1].astype(F32)
    w_mid[...] = total.astype(BF)
    sums = [
        keep(send(w_mid.at[(v + e) % SIDE], v_in.at[e - 1], v_dev(e))) for e in (2, 1, 3)
    ]
    for copy in sums:
        copy.wait_recv()
    total = w_mid[v].astype(F32)
    for e in range(1, SIDE):
        total += v_in[e - 1].astype(F32)
    total = total.astype(BF)
    for i in range(FEATS):
        z_out[i, :32] = total[i * 32:i * 32 + 32]
        z_out[i, 32:] = total[256:]
    sums = [keep(send(z_out.at[i], z_in.at[i - 1], feat_dev(-i))) for i in range(1, FEATS)]
    for copy in sums:
        copy.wait_recv()
    total = z_out[0].astype(F32)
    for i in range(1, FEATS):
        total += z_in[i - 1].astype(F32)
    piece_all[u, v] = total.astype(BF)
    sums = [
        keep(send(piece_all.at[u, v], piece_all.at[u, v], v_dev(e))) for e in range(1, SIDE)
    ]
    for copy in sums:
        copy.wait_recv()
    sums = [keep(send(piece_all.at[u], piece_all.at[u], u_dev(d))) for d in range(1, SIDE)]
    for copy in sums:
        copy.wait_recv()
    for r in range(4):
        for q in range(4):
            a, b = (1 - core) * q + core * r, (1 - core) * r + core * q
            piece = piece_all[a, b].astype(F32)
            gw_one_ref[r * 32:r * 32 + 32, q * 128:q * 128 + 128] = piece[:32]
            gw_two_ref[r * 64:r * 64 + 64, q * 128:q * 128 + 128] = piece[32:96]
            if r == 0 and q < 2:
                gb_ref[:, q * 128:q * 128 + 128] = piece[96:97]
    for copy in started:
        copy.wait_send()


N_COPIES = 3 + 7 + 3 + 7 * CHUNKS + 3 + 3 + 3 + 3 * CHUNKS + 3 * 6 + 3 + 7 + 3 + 3 + 3


def line_asks(owner, slot, core, u, v):
    ids = jnp.stack([
        jnp.stack([node_at(core, (u - d + SIDE) % SIDE, (v + e) % SIDE) for d in range(SIDE)]
                  + [jnp.int32(-1)] * 4)
        for e in range(SIDE)
    ])
    owner_t, slot_t = owner.T, slot.T
    same = owner_t[:, None, None, :] == ids[None, :, :, None]
    return jnp.max(jnp.where(same, slot_t[:, None, None, :], -1), axis=0)


def on_device(
    features, w_one, w_two, b_one, b_two, owner_one, slot_one, owner_two, slot_two, cotangent
):
    f, n = lax.axis_index("feat"), lax.axis_index("node")
    core = f % 2
    u, v = line_place(core, n)
    asks = jnp.concatenate([
        line_asks(owner_one[0], slot_one[0], core, u, v),
        line_asks(owner_two[0], slot_two[0], core, u, v),
    ], axis=2)
    r1, r2, r3 = features.shape[1], owner_one.shape[1], owner_two.shape[1]
    vm = pl.BlockSpec(memory_space=pltpu.VMEM)
    scratch = [
        ((FEATS, r1, 128), BF), ((FEATS, 4, 4, 32, 128), BF), ((1024, 512), BF),
        ((SIDE, 8, r2 + r3), jnp.int32), ((SIDE, r2 + r3, 8), jnp.int32),
        ((SIDE, r3, 256), BF), ((r2, 256), F32), ((3, r2, 256), BF), ((3, r2, 256), BF),
        ((r2, 512), BF), ((r2, 256), F32), ((SIDE, r1, 256), BF), ((r2, 256), F32),
        ((SIDE, r2, 256), F32), ((3, r2, 256), BF), ((3, r2, 256), BF), ((r2, 256), BF),
        ((r3, 256), F32), ((SIDE, r2, 256), BF), ((r3, 256), F32), ((3, r3, 256), BF),
        ((3, r3, 256), BF), ((r2, 256), BF), ((SIDE, r2, 256), BF), ((SIDE, r1, 256), F32),
        ((3, r1, 256), BF), ((3, r1, 256), BF), ((4, 4, 336, 128), BF), ((3, 4, 336, 128), BF),
        ((4, 336, 128), BF), ((3, 336, 128), BF), ((FEATS, 112, 128), BF),
        ((FEATS - 1, 112, 128), BF), ((4, 4, 112, 128), BF),
    ]
    layer_out, gw_one, gw_two, gb = pl.pallas_call(
        step_kernel,
        out_shape=[
            jax.ShapeDtypeStruct((r3, 256), BF), jax.ShapeDtypeStruct((128, 512), F32),
            jax.ShapeDtypeStruct((256, 512), F32), jax.ShapeDtypeStruct((1, 256), F32),
        ],
        in_specs=[pl.BlockSpec(memory_space=pl.ANY)] + [vm] * 6,
        out_specs=[vm] * 4,
        scratch_shapes=[pltpu.VMEM(s, t) for s, t in scratch] + [
            pltpu.SemaphoreType.DMA((N_COPIES,)), pltpu.SemaphoreType.DMA((N_COPIES,)),
            pltpu.SemaphoreType.DMA,
        ],
        compiler_params=pltpu.CompilerParams(
            collective_id=0, has_side_effects=True, vmem_limit_bytes=52 * 2**20
        ),
        cost_estimate=pl.CostEstimate(
            flops=14 * 10**9, bytes_accessed=8 * 2**20, transcendentals=512 * 256
        ),
        name="sage_step",
    )(features, w_one, w_two, b_one[None], b_two[None], asks, cotangent[0])
    return layer_out[None], gw_one, gw_two, gb[0]


def solution(mesh):
    placed = (
        P(None, "node", "feat"),
        P("feat", None),
        P(),
        P(),
        P(),
        P("feat", "node", None),
        P("feat", "node", None),
        P("feat", "node", None),
        P("feat", "node", None),
        P("feat", "node", None),
    )
    return jax.shard_map(
        on_device,
        mesh=mesh,
        in_specs=placed,
        out_specs=(P("feat", "node", None), P("feat", None), P(), P()),
        check_vma=False,
    )
```

```python
import jax
import jax.numpy as jnp
from jax import lax
from jax.experimental import pallas as pl
from jax.experimental.pallas import tpu as pltpu
from jax.sharding import PartitionSpec as P

MESH = pl.DeviceIdType.MESH
CHUNKS = 4
HALVES = 2
FEATS = 8
SIDE = 4
FAN = 8
BF = jnp.bfloat16
F32 = jnp.float32
I32 = jnp.int32


def line_place(core, node):
    low, high = node % SIDE, node // SIDE
    return (1 - core) * low + core * high, (1 - core) * high + core * low


def node_at(core, u, v):
    return (1 - core) * (v * SIDE + u) + core * (u * SIDE + v)


def dot(a, b, dims=((1,), (0,))):
    return lax.dot_general(a, b, (dims, ((), ())), preferred_element_type=F32)


def add_up(first, others):
    total = first
    for other in others:
        total += other.astype(F32)
    return total


def step_kernel(
    feat_ref, w_one_ref, w_two_ref, b_one_ref, b_two_ref, owner_one_ref, slot_one_ref,
    owner_two_ref, slot_two_ref, cot_ref,
    out_ref, gw_one_ref, gw_two_ref, gb_ref,
    slab, w_parts, w_full, w_two, b_one, b_two, own_one, slo_one, own_two, slo_two, cot,
    asks_out, asks, asks_col, msg_two, gsum_two, gsend_two, grecv_two,
    gproj_two, ghid, table, self_one, ysum, ysend, yrecv, hidden, self_two,
    table_two, ysum_two, ysend_two, yrecv_two, glin, msg_one, gsum, gsend, grecv,
    two_out, two_in, two_mid, two_u, two_z, two_all,
    pair_out, pair_in, w_out, w_in, w_mid, v_in, z_out, z_in, piece_all,
    ssem, rsem, lsem,
):
    f, n = lax.axis_index("feat"), lax.axis_index("node")
    z, core = f // 2, f % 2
    u, v = line_place(core, n)
    rows_one = slab.shape[1]
    rows_two = own_one.shape[0]
    rows_three = own_two.shape[0]
    part = rows_one // CHUNKS
    half = rows_two // HALVES
    slots = [(dz, dc) for dz in range(4) for dc in range(2)]
    by_far = (2, 1, 3)

    def feat_dev(dz, dc):
        return (((z + dz + 4) % 4) * 2 + (core + dc) % 2, n)

    def u_dev(d):
        return (f, node_at(core, (u + d + SIDE) % SIDE, v))

    def v_dev(e):
        return (f, node_at(core, u, (v + e + SIDE) % SIDE))

    def place(r, q):
        return (1 - core) * q + core * r, (1 - core) * r + core * q

    started = []

    def send(src, dst, dev):
        k = len(started)
        copy = pltpu.make_async_remote_copy(
            src_ref=src, dst_ref=dst, send_sem=ssem.at[k], recv_sem=rsem.at[k],
            device_id=dev, device_id_type=MESH,
        )
        copy.start()
        started.append(copy)
        return copy

    barrier = pltpu.get_barrier_semaphore()
    partners = [feat_dev(*s) for s in slots[1:]]
    partners += [u_dev(d) for d in range(1, SIDE)] + [v_dev(e) for e in range(1, SIDE)]
    for dev in partners:
        pl.semaphore_signal(barrier, inc=1, device_id=dev, device_id_type=MESH)

    loads = []

    def load(src, dst):
        copy = pltpu.make_async_copy(src, dst, lsem.at[len(loads)])
        copy.start()
        loads.append(copy)
        return copy

    index_loads = [
        load(owner_one_ref, own_one), load(slot_one_ref, slo_one),
        load(owner_two_ref, own_two), load(slot_two_ref, slo_two),
    ]
    cot_load = load(cot_ref, cot)
    w_one_load = load(w_one_ref, w_full.at[pl.ds(0, 128)])
    own_load = load(feat_ref.at[f], slab.at[0])
    small_loads = [load(w_two_ref, w_two), load(b_one_ref, b_one), load(b_two_ref, b_two)]

    for copy in index_loads:
        copy.wait()
    for own, slo, lower in ((own_one, slo_one, 0), (own_two, slo_two, rows_two)):
        owner_t = jnp.transpose(own[...].astype(F32))
        slot_t = jnp.transpose(slo[...].astype(F32))
        for e in range(SIDE):
            for d in range(SIDE):
                at = node_at(core, (u - d + SIDE) % SIDE, (v + e) % SIDE)
                found = jnp.max(
                    jnp.where(owner_t == at.astype(F32), slot_t, -1.0), axis=0, keepdims=True
                )
                asks_out[e, d:d + 1, lower:lower + own.shape[0]] = found.astype(I32)
    for e in range(SIDE):
        asks_out[e, SIDE:] = jnp.full((8 - SIDE, rows_two + rows_three), -1, I32)
    cot_load.wait()
    msg_two[0] = (cot[...] / FAN).astype(BF)

    pl.semaphore_wait(barrier, len(partners))

    low, high = n % SIDE, n // SIDE
    w_copies = []
    for i, (dz, dc) in enumerate(slots):
        if i:
            their_u, their_v = line_place((core + dc) % 2, n)
            w_copies.append(send(
                w_one_ref.at[pl.ds(pl.multiple_of(high * 32, 32), 32),
                             pl.ds(pl.multiple_of(low * 128, 128), 128)],
                w_parts.at[i, their_u, their_v], feat_dev(dz, dc),
            ))
    ask_copies = [send(asks_out.at[e], asks.at[e], v_dev(e)) for e in range(1, SIDE)]
    msg_two_copies = [send(msg_two.at[0], msg_two.at[e], v_dev(e)) for e in range(1, SIDE)]
    slab_copies = []
    for c in range(CHUNKS):
        rows = pl.ds(c * part, part)
        slab_copies.append([])
        for i in (4, 5, 2, 3, 6, 7, 1):
            dev = feat_dev(*slots[i])
            slab_copies[c].append(send(feat_ref.at[dev[0], rows], slab.at[i, rows], dev))

    for copy in w_copies:
        copy.wait_recv()
    mine = w_parts.at[pl.ds(1, FEATS - 1), u, v]
    along_u = [send(mine, mine, u_dev(d)) for d in range(1, SIDE)]
    asks[0] = asks_out[0]
    for copy in ask_copies:
        copy.wait_recv()
    for e in range(SIDE):
        asks_col[e] = jnp.transpose(asks[e].astype(F32)).astype(I32)
    for copy in along_u:
        copy.wait_recv()
    mine = w_parts.at[pl.ds(1, FEATS - 1), :, v]
    along_v = [send(mine, mine, v_dev(e)) for e in range(1, SIDE)]

    for copy in msg_two_copies:
        copy.wait_recv()
    msgs = jnp.concatenate([msg_two[e] for e in range(SIDE)], axis=0)
    back_two = []
    for d in (2, 1, 3, 0):
        ids = lax.broadcasted_iota(I32, (rows_two, rows_three), 0)
        picks = jnp.concatenate(
            [(ids == asks[e, d:d + 1, rows_two:]).astype(BF) for e in range(SIDE)], axis=1
        )
        total = dot(picks, msgs)
        if d:
            gsend_two[d - 1] = total.astype(BF)
            back_two.append(send(gsend_two.at[d - 1], grecv_two.at[d - 1], u_dev(-d)))
        else:
            gsum_two[...] = total

    for copy in along_v:
        copy.wait_recv()
    w_one_load.wait()
    for i in range(1, FEATS):
        for r in range(4):
            for q in range(4):
                a, b = place(r, q)
                w_full[i * 128 + r * 32:i * 128 + r * 32 + 32, q * 128:q * 128 + 128] = (
                    w_parts[i, a, b]
                )

    table_copies = []

    def project(c):
        for copy in slab_copies[c]:
            copy.wait_recv()
        lower = c * part
        block = jnp.concatenate([slab[i, lower:lower + part] for i in range(FEATS)], axis=1)
        table[0, lower:lower + part] = dot(block, w_full[:, 256:]).astype(BF)
        rows = pl.ds(lower, part)
        table_copies.append(
            [send(table.at[0, rows], table.at[d, rows], u_dev(d)) for d in by_far]
        )
        if lower < rows_two:
            self_one[lower:lower + part] = dot(block, w_full[:, :256])

    def line_sums(c, e, lower, count):
        ids = lax.broadcasted_iota(I32, (count, part), 1) + c * part
        picks = jnp.concatenate(
            [(ids == asks_col[e, lower:lower + count, d:d + 1]).astype(BF)
             for d in range(SIDE)], axis=1
        )
        rows = jnp.concatenate(
            [table[d, c * part:c * part + part] for d in range(SIDE)], axis=0
        )
        return dot(picks, rows)

    def add_lines(c):
        for copy in table_copies[c]:
            copy.wait_recv()

        def one(e, carry):
            value = line_sums(c, e, 0, rows_two)
            ysum[e] = value if c == 0 else ysum[e] + value
            return carry

        lax.fori_loop(0, SIDE, one, 0)

    own_load.wait()
    for c in range(CHUNKS):
        project(c)
        if c:
            add_lines(c - 1)
        if c == 1:
            for copy in back_two:
                copy.wait_recv()
            for copy in small_loads:
                copy.wait()
            gtab_two = add_up(gsum_two[...], [grecv_two[d] for d in range(SIDE - 1)])
            gproj_two[:rows_three, :256] = cot[...].astype(BF)
            gproj_two[rows_three:, :256] = jnp.zeros((rows_two - rows_three, 256), BF)
            gproj_two[:, 256:] = gtab_two.astype(BF)
            ghid[...] = dot(gproj_two[...], w_two[...], ((1,), (1,)))
    last = CHUNKS - 1
    for copy in table_copies[last]:
        copy.wait_recv()
    y_copies = []
    for h in range(HALVES):
        rows = pl.ds(h * half, half)
        y_copies.append([])
        for e in (2, 1, 3, 0):
            value = ysum[e, h * half:h * half + half] + line_sums(last, e, h * half, half)
            if e:
                ysend[e - 1, h * half:h * half + half] = value.astype(BF)
                y_copies[h].append(
                    send(ysend.at[e - 1, rows], yrecv.at[e - 1, rows], v_dev(-e))
                )
            else:
                ysum[0, h * half:h * half + half] = value
    msg_copies = []
    bias = jnp.zeros((1, 256), F32)
    for h in range(HALVES):
        for copy in y_copies[h]:
            copy.wait_recv()
        rows = slice(h * half, h * half + half)
        total = add_up(ysum[0, rows], [yrecv[e, rows] for e in range(SIDE - 1)])
        linear = self_one[rows] + b_one[...] + total / FAN
        logistic = 1.0 / (1.0 + jnp.exp(-linear))
        grad = ghid[rows] * (logistic * (1.0 + linear * (1.0 - logistic)))
        msg_one[0, rows] = (grad / FAN).astype(BF)
        there = pl.ds(h * half, half)
        msg_copies.append([
            send(msg_one.at[0, there], msg_one.at[e, there], v_dev(e)) for e in by_far
        ])
        glin[rows] = grad.astype(BF)
        hidden[rows] = (linear * logistic).astype(BF)
        bias += jnp.sum(grad, axis=0, keepdims=True)

    proj = dot(hidden[...], w_two[...])
    table_two[0] = proj[:, 256:].astype(BF)
    table_two_copies = [send(table_two.at[0], table_two.at[d], u_dev(d)) for d in by_far]
    self_two[...] = proj[:rows_three, :256]
    gw_two = dot(hidden[...], gproj_two[...], ((0,), (0,))).astype(BF)
    for r in range(4):
        for q in range(4):
            a, b = place(r, q)
            two_out[a, b, :64] = gw_two[r * 64:r * 64 + 64, q * 128:q * 128 + 128]
            if r == 0 and q < 2:
                two_out[a, b, 64:] = jnp.broadcast_to(
                    bias[:, q * 128:q * 128 + 128], (16, 128)
                ).astype(BF)
            else:
                two_out[a, b, 64:] = jnp.zeros((16, 128), BF)
    two_copies = [
        send(two_out.at[:, (v + e) % SIDE], two_in.at[e - 1], v_dev(e)) for e in by_far
    ]

    def line_grads(h, d):
        ids = lax.broadcasted_iota(I32, (rows_one, half), 0)
        picks = jnp.concatenate(
            [(ids == asks[e, pl.ds(d, 1), h * half:h * half + half]).astype(BF)
             for e in range(SIDE)], axis=1
        )
        rows = jnp.concatenate(
            [msg_one[e, h * half:h * half + half] for e in range(SIDE)], axis=0
        )
        return dot(picks, rows)

    for h in range(HALVES - 1):
        for copy in msg_copies[h]:
            copy.wait_recv()

        def add_back(d, carry, h=h):
            value = line_grads(h, d)
            gsum[d] = value if h == 0 else gsum[d] + value
            return carry

        lax.fori_loop(0, SIDE, add_back, 0)
    for copy in msg_copies[HALVES - 1]:
        copy.wait_recv()
    back_one = []
    for d in (2, 1, 3, 0):
        value = gsum[d] + line_grads(HALVES - 1, d)
        if d:
            gsend[d - 1] = value.astype(BF)
            back_one.append(send(gsend.at[d - 1], grecv.at[d - 1], u_dev(-d)))
        else:
            gsum[0] = value

    for copy in two_copies:
        copy.wait_recv()
    for a in range(SIDE):
        two_mid[a] = add_up(
            two_out[a, v].astype(F32), [two_in[e, a] for e in range(SIDE - 1)]
        ).astype(BF)
    two_copies = [
        send(two_mid.at[(u + d) % SIDE], two_u.at[d - 1], u_dev(d)) for d in by_far
    ]

    for copy in table_two_copies:
        copy.wait_recv()
    y_two = []
    rows = jnp.concatenate([table_two[d] for d in range(SIDE)], axis=0)
    for e in (2, 1, 3, 0):
        ids = lax.broadcasted_iota(I32, (rows_three, rows_two), 1)
        picks = jnp.concatenate(
            [(ids == asks_col[e, rows_two:, d:d + 1]).astype(BF) for d in range(SIDE)], axis=1
        )
        value = dot(picks, rows)
        if e:
            ysend_two[e - 1] = value.astype(BF)
            y_two.append(send(ysend_two.at[e - 1], yrecv_two.at[e - 1], v_dev(-e)))
        else:
            ysum_two[...] = value

    for copy in two_copies:
        copy.wait_recv()
    two_z[0] = add_up(two_mid[u].astype(F32), [two_u[d] for d in range(SIDE - 1)]).astype(BF)
    two_copies = [send(two_z.at[0], two_z.at[i], feat_dev(*slots[i])) for i in range(1, FEATS)]

    for copy in y_two:
        copy.wait_recv()
    total = add_up(ysum_two[...], [yrecv_two[e] for e in range(SIDE - 1)])
    out_ref[...] = (self_two[...] + b_two[...] + total / FAN).astype(BF)

    for copy in two_copies:
        copy.wait_recv()
    two_all[u, v] = add_up(
        two_z[0].astype(F32), [two_z[i] for i in range(1, FEATS)]
    ).astype(BF)
    two_copies = [send(two_all.at[u, v], two_all.at[u, v], v_dev(e)) for e in by_far]

    for copy in back_one:
        copy.wait_recv()
    gtab = add_up(gsum[0], [grecv[d] for d in range(SIDE - 1)]).astype(BF)

    def outer(dc):
        block = jnp.concatenate([slab[2 * dz + dc] for dz in range(4)], axis=1)
        return (dot(block[:rows_two], glin[...], ((0,), (0,))),
                dot(block, gtab, ((0,), (0,))))

    left, right = outer(1)
    pair_out[:, :256] = left.astype(BF)
    pair_out[:, 256:] = right.astype(BF)
    pair = send(pair_out, pair_in, feat_dev(0, 1))
    left, right = outer(0)
    for copy in two_copies:
        copy.wait_recv()
    two_copies = [send(two_all.at[u], two_all.at[u], u_dev(d)) for d in by_far]
    pair.wait_recv()
    left = (left + pair_in[:, :256].astype(F32)).astype(BF)
    right = (right + pair_in[:, 256:].astype(F32)).astype(BF)
    for dz in range(4):
        for r in range(4):
            for q in range(4):
                a, b = place(r, q)
                side = left if q < 2 else right
                w_out[a, b, dz * 32:dz * 32 + 32] = side[
                    dz * 128 + r * 32:dz * 128 + r * 32 + 32,
                    (q % 2) * 128:(q % 2) * 128 + 128]

    sums = [send(w_out.at[(u + d) % SIDE], w_in.at[d - 1], u_dev(d)) for d in by_far]
    for copy in two_copies:
        copy.wait_recv()
    for r in range(4):
        for q in range(4):
            a, b = place(r, q)
            piece = two_all[a, b].astype(F32)
            gw_two_ref[r * 64:r * 64 + 64, q * 128:q * 128 + 128] = piece[:64]
            if r == 0 and q < 2:
                gb_ref[:, q * 128:q * 128 + 128] = piece[64:65]
    for copy in sums:
        copy.wait_recv()
    for b in range(SIDE):
        w_mid[b] = add_up(
            w_out[u, b].astype(F32), [w_in[d, b] for d in range(SIDE - 1)]
        ).astype(BF)
    sums = [send(w_mid.at[(v + e) % SIDE], v_in.at[e - 1], v_dev(e)) for e in by_far]
    for copy in sums:
        copy.wait_recv()
    z_out[...] = add_up(w_mid[v].astype(F32), [v_in[e] for e in range(SIDE - 1)]).astype(BF)
    sums = [
        send(z_out.at[pl.ds(dz * 32, 32)], z_in.at[dz - 1], feat_dev(-dz, 0)) for dz in by_far
    ]
    for copy in sums:
        copy.wait_recv()
    piece_all[u, v] = add_up(
        z_out[:32].astype(F32), [z_in[dz] for dz in range(3)]
    ).astype(BF)
    sums = [send(piece_all.at[u, v], piece_all.at[u, v], v_dev(e)) for e in by_far]
    for copy in sums:
        copy.wait_recv()
    sums = [send(piece_all.at[u], piece_all.at[u], u_dev(d)) for d in by_far]
    for copy in sums:
        copy.wait_recv()
    for r in range(4):
        for q in range(4):
            a, b = place(r, q)
            gw_one_ref[r * 32:r * 32 + 32, q * 128:q * 128 + 128] = piece_all[a, b].astype(F32)
    for copy in started:
        copy.wait_send()


N_COPIES = 7 * (3 + CHUNKS) + 3 * (CHUNKS + 2 * HALVES) + 3 * 18


def on_device(
    features, w_one, w_two, b_one, b_two, owner_one, slot_one, owner_two, slot_two, cotangent
):
    r1, r2, r3 = features.shape[1], owner_one.shape[1], owner_two.shape[1]
    vm = pl.BlockSpec(memory_space=pltpu.VMEM)
    scratch = [
        ((FEATS, r1, 128), BF), ((FEATS, 4, 4, 32, 128), BF), ((1024, 512), BF),
        ((256, 512), BF), ((1, 256), F32), ((1, 256), F32),
        ((r2, FAN), I32), ((r2, FAN), I32), ((r3, FAN), I32), ((r3, FAN), I32),
        ((r3, 256), F32), ((SIDE, 8, r2 + r3), I32),
        ((SIDE, 8, r2 + r3), I32), ((SIDE, r2 + r3, 8), I32),
        ((SIDE, r3, 256), BF), ((r2, 256), F32), ((3, r2, 256), BF), ((3, r2, 256), BF),
        ((r2, 512), BF), ((r2, 256), F32), ((SIDE, r1, 256), BF), ((r2, 256), F32),
        ((SIDE, r2, 256), F32), ((3, r2, 256), BF), ((3, r2, 256), BF), ((r2, 256), BF),
        ((r3, 256), F32), ((SIDE, r2, 256), BF), ((r3, 256), F32), ((3, r3, 256), BF),
        ((3, r3, 256), BF), ((r2, 256), BF), ((SIDE, r2, 256), BF), ((SIDE, r1, 256), F32),
        ((3, r1, 256), BF), ((3, r1, 256), BF),
        ((4, 4, 80, 128), BF), ((3, 4, 80, 128), BF), ((4, 80, 128), BF), ((3, 80, 128), BF),
        ((FEATS, 80, 128), BF), ((4, 4, 80, 128), BF),
        ((512, 512), BF), ((512, 512), BF), ((4, 4, 128, 128), BF), ((3, 4, 128, 128), BF),
        ((4, 128, 128), BF), ((3, 128, 128), BF), ((128, 128), BF), ((3, 32, 128), BF),
        ((4, 4, 32, 128), BF),
    ]
    layer_out, gw_one, gw_two, gb = pl.pallas_call(
        step_kernel,
        out_shape=[
            jax.ShapeDtypeStruct((r3, 256), BF), jax.ShapeDtypeStruct((128, 512), F32),
            jax.ShapeDtypeStruct((256, 512), F32), jax.ShapeDtypeStruct((1, 256), F32),
        ],
        in_specs=[pl.BlockSpec(memory_space=pl.ANY)] * 10,
        out_specs=[vm] * 4,
        scratch_shapes=[pltpu.VMEM(s, t) for s, t in scratch] + [
            pltpu.SemaphoreType.DMA((N_COPIES,)), pltpu.SemaphoreType.DMA((N_COPIES,)),
            pltpu.SemaphoreType.DMA((10,)),
        ],
        compiler_params=pltpu.CompilerParams(
            collective_id=0, has_side_effects=True, vmem_limit_bytes=56 * 2**20
        ),
        cost_estimate=pl.CostEstimate(
            flops=14 * 10**9, bytes_accessed=8 * 2**20, transcendentals=512 * 256
        ),
        name="sage_step",
    )(features, w_one, w_two, b_one[None], b_two[None], owner_one[0], slot_one[0],
      owner_two[0], slot_two[0], cotangent[0])
    return layer_out[None], gw_one, gw_two, gb[0]


def solution(mesh):
    placed = (
        P(None, "node", "feat"),
        P("feat", None),
        P(),
        P(),
        P(),
        P("feat", "node", None),
        P("feat", "node", None),
        P("feat", "node", None),
        P("feat", "node", None),
        P("feat", "node", None),
    )
    return jax.shard_map(
        on_device,
        mesh=mesh,
        in_specs=placed,
        out_specs=(P("feat", "node", None), P("feat", None), P(), P()),
        check_vma=False,
    )
```

```python
import jax
import jax.numpy as jnp
from jax import lax
from jax.experimental import pallas as pl
from jax.experimental.pallas import tpu as pltpu
from jax.sharding import PartitionSpec as P

MESH = pl.DeviceIdType.MESH
CHUNKS = (256, 256, 256, 128, 128)
HALVES = 2
FEATS = 8
SIDE = 4
FAN = 8
BF = jnp.bfloat16
F32 = jnp.float32
I32 = jnp.int32


def line_place(core, node):
    low, high = node % SIDE, node // SIDE
    return (1 - core) * low + core * high, (1 - core) * high + core * low


def node_at(core, u, v):
    return (1 - core) * (v * SIDE + u) + core * (u * SIDE + v)


def dot(a, b, dims=((1,), (0,))):
    return lax.dot_general(a, b, (dims, ((), ())), preferred_element_type=F32)


def add_up(first, others):
    total = first
    for other in others:
        total += other.astype(F32)
    return total


def step_kernel(
    feat_ref, w_one_ref, w_two_ref, b_one_ref, b_two_ref, owner_one_ref, slot_one_ref,
    owner_two_ref, slot_two_ref, cot_ref,
    out_ref, gw_one_ref, gw_two_ref, gb_ref,
    slab, w_parts, w_full, w_two, b_one, b_two, own_one, slo_one, own_two, slo_two, cot,
    asks_out, asks, asks_col, msg_two, gsum_two, gsend_two, grecv_two,
    gproj_two, ghid, table, self_one, ysum, ysend, yrecv, hidden, self_two,
    table_two, ysum_two, ysend_two, yrecv_two, glin, msg_one, gsum, gsend, grecv,
    two_out, two_in, two_mid, two_u, two_z, two_all,
    pair_out, pair_in, w_out, w_in, w_mid, v_in, z_out, z_in, piece_all,
    ssem, rsem, lsem,
):
    f, n = lax.axis_index("feat"), lax.axis_index("node")
    z, core = f // 2, f % 2
    u, v = line_place(core, n)
    rows_one = slab.shape[1]
    rows_two = own_one.shape[1]
    rows_three = own_two.shape[1]
    starts = [sum(CHUNKS[:c]) for c in range(len(CHUNKS))]
    half = rows_two // HALVES
    slots = [(dz, dc) for dz in range(4) for dc in range(2)]
    by_far = (2, 1, 3)

    def feat_dev(dz, dc):
        return (((z + dz + 4) % 4) * 2 + (core + dc) % 2, n)

    def u_dev(d):
        return (f, node_at(core, (u + d + SIDE) % SIDE, v))

    def v_dev(e):
        return (f, node_at(core, u, (v + e + SIDE) % SIDE))

    def place(r, q):
        return (1 - core) * q + core * r, (1 - core) * r + core * q

    started = []

    def send(src, dst, dev):
        k = len(started)
        copy = pltpu.make_async_remote_copy(
            src_ref=src, dst_ref=dst, send_sem=ssem.at[k], recv_sem=rsem.at[k],
            device_id=dev, device_id_type=MESH,
        )
        copy.start()
        started.append(copy)
        return copy

    barrier = pltpu.get_barrier_semaphore()
    partners = [feat_dev(*s) for s in slots[1:]]
    partners += [u_dev(d) for d in range(1, SIDE)] + [v_dev(e) for e in range(1, SIDE)]
    for dev in partners:
        pl.semaphore_signal(barrier, inc=1, device_id=dev, device_id_type=MESH)

    loads = []

    def load(src, dst):
        copy = pltpu.make_async_copy(src, dst, lsem.at[len(loads)])
        copy.start()
        loads.append(copy)
        return copy

    index_loads = [
        load(owner_one_ref, own_one), load(slot_one_ref, slo_one),
        load(owner_two_ref, own_two), load(slot_two_ref, slo_two),
    ]
    cot_load = load(cot_ref, cot)
    w_one_load = load(w_one_ref, w_full.at[pl.ds(0, 128)])
    own_load = load(feat_ref.at[f], slab.at[0])
    small_loads = [load(w_two_ref, w_two), load(b_one_ref, b_one), load(b_two_ref, b_two)]

    for copy in index_loads:
        copy.wait()
    for own, slo, lower in ((own_one, slo_one, 0), (own_two, slo_two, rows_two)):
        owner_t, slot_t = own[...], slo[...]
        for e in range(SIDE):
            for d in range(SIDE):
                at = node_at(core, (u - d + SIDE) % SIDE, (v + e) % SIDE)
                found = jnp.max(
                    jnp.where(owner_t == at, slot_t, -1), axis=0, keepdims=True
                )
                asks_out[e, d:d + 1, lower:lower + own.shape[1]] = found
    for e in range(SIDE):
        asks_out[e, SIDE:] = jnp.full((8 - SIDE, rows_two + rows_three), -1, I32)
    cot_load.wait()
    msg_two[0] = (cot[...] / FAN).astype(BF)

    pl.semaphore_wait(barrier, len(partners))

    def send_chunk(c):
        rows = pl.ds(starts[c], CHUNKS[c])
        copies = []
        for i in (4, 5, 2, 3, 6, 7, 1):
            dev = feat_dev(*slots[i])
            copies.append(send(feat_ref.at[dev[0], rows], slab.at[i, rows], dev))
        return copies

    low, high = n % SIDE, n // SIDE
    w_copies = []
    for i, (dz, dc) in enumerate(slots):
        if i:
            their_u, their_v = line_place((core + dc) % 2, n)
            w_copies.append(send(
                w_one_ref.at[pl.ds(pl.multiple_of(high * 32, 32), 32),
                             pl.ds(pl.multiple_of(low * 128, 128), 128)],
                w_parts.at[i, their_u, their_v], feat_dev(dz, dc),
            ))
    first_chunk = send_chunk(0)
    ask_copies = [send(asks_out.at[e], asks.at[e], v_dev(e)) for e in range(1, SIDE)]
    msg_two_copies = [send(msg_two.at[0], msg_two.at[e], v_dev(e)) for e in range(1, SIDE)]
    slab_copies = [first_chunk] + [send_chunk(c) for c in range(1, len(CHUNKS))]

    for copy in w_copies:
        copy.wait_recv()
    mine = w_parts.at[pl.ds(1, FEATS - 1), u, v]
    along_u = [send(mine, mine, u_dev(d)) for d in range(1, SIDE)]
    asks[0] = asks_out[0]
    for copy in ask_copies:
        copy.wait_recv()
    for e in range(SIDE):
        asks_col[e] = jnp.transpose(asks[e].astype(F32)).astype(I32)
    for copy in msg_two_copies:
        copy.wait_recv()
    msgs = jnp.concatenate([msg_two[e] for e in range(SIDE)], axis=0)
    back_two = []
    for d in (2, 1, 3, 0):
        ids = lax.broadcasted_iota(I32, (rows_two, rows_three), 0)
        picks = jnp.concatenate(
            [(ids == asks[e, d:d + 1, rows_two:]).astype(BF) for e in range(SIDE)], axis=1
        )
        total = dot(picks, msgs)
        if d:
            gsend_two[d - 1] = total.astype(BF)
            back_two.append(send(gsend_two.at[d - 1], grecv_two.at[d - 1], u_dev(-d)))
        else:
            gsum_two[...] = total

    for copy in along_u:
        copy.wait_recv()
    mine = w_parts.at[pl.ds(1, FEATS - 1), :, v]
    along_v = [send(mine, mine, v_dev(e)) for e in range(1, SIDE)]

    for copy in back_two:
        copy.wait_recv()
    for copy in small_loads:
        copy.wait()
    gtab_two = add_up(gsum_two[...], [grecv_two[d] for d in range(SIDE - 1)])
    gproj_two[:rows_three, :256] = cot[...].astype(BF)
    gproj_two[rows_three:, :256] = jnp.zeros((rows_two - rows_three, 256), BF)
    gproj_two[:, 256:] = gtab_two.astype(BF)
    ghid[...] = dot(gproj_two[...], w_two[...], ((1,), (1,)))

    for copy in along_v:
        copy.wait_recv()
    w_one_load.wait()
    for i in range(1, FEATS):
        for r in range(4):
            for q in range(4):
                a, b = place(r, q)
                w_full[i * 128 + r * 32:i * 128 + r * 32 + 32, q * 128:q * 128 + 128] = (
                    w_parts[i, a, b]
                )

    table_copies = []

    def project(c):
        for copy in slab_copies[c]:
            copy.wait_recv()
        lower, part = starts[c], CHUNKS[c]
        block = jnp.concatenate([slab[i, lower:lower + part] for i in range(FEATS)], axis=1)
        table[0, lower:lower + part] = dot(block, w_full[:, 256:]).astype(BF)
        rows = pl.ds(lower, part)
        table_copies.append(
            [send(table.at[0, rows], table.at[d, rows], u_dev(d)) for d in by_far]
        )
        if lower < rows_two:
            self_one[lower:lower + part] = dot(block, w_full[:, :256])

    def line_sums(c, e, lower, count):
        start, part = starts[c], CHUNKS[c]
        ids = lax.broadcasted_iota(I32, (count, part), 1) + start
        picks = jnp.concatenate(
            [(ids == asks_col[e, lower:lower + count, d:d + 1]).astype(BF)
             for d in range(SIDE)], axis=1
        )
        rows = jnp.concatenate(
            [table[d, start:start + part] for d in range(SIDE)], axis=0
        )
        return dot(picks, rows)

    def add_lines(c):
        for copy in table_copies[c]:
            copy.wait_recv()

        def one(e, carry):
            value = line_sums(c, e, 0, rows_two)
            ysum[e] = value if c == 0 else ysum[e] + value
            return carry

        lax.fori_loop(0, SIDE, one, 0)

    own_load.wait()
    for c in range(len(CHUNKS)):
        project(c)
        if c:
            add_lines(c - 1)
    last = len(CHUNKS) - 1
    for copy in table_copies[last]:
        copy.wait_recv()
    y_copies = []
    for h in range(HALVES):
        rows = pl.ds(h * half, half)
        y_copies.append([])
        for e in (2, 1, 3, 0):
            value = ysum[e, h * half:h * half + half] + line_sums(last, e, h * half, half)
            if e:
                ysend[e - 1, h * half:h * half + half] = value.astype(BF)
                y_copies[h].append(
                    send(ysend.at[e - 1, rows], yrecv.at[e - 1, rows], v_dev(-e))
                )
            else:
                ysum[0, h * half:h * half + half] = value
    msg_copies = []
    bias = jnp.zeros((1, 256), F32)
    for h in range(HALVES):
        for copy in y_copies[h]:
            copy.wait_recv()
        rows = slice(h * half, h * half + half)
        total = add_up(ysum[0, rows], [yrecv[e, rows] for e in range(SIDE - 1)])
        linear = self_one[rows] + b_one[...] + total / FAN
        logistic = 1.0 / (1.0 + jnp.exp(-linear))
        grad = ghid[rows] * (logistic * (1.0 + linear * (1.0 - logistic)))
        msg_one[0, rows] = (grad / FAN).astype(BF)
        there = pl.ds(h * half, half)
        msg_copies.append([
            send(msg_one.at[0, there], msg_one.at[e, there], v_dev(e)) for e in by_far
        ])
        glin[rows] = grad.astype(BF)
        hidden[rows] = (linear * logistic).astype(BF)
        bias += jnp.sum(grad, axis=0, keepdims=True)

    proj = dot(hidden[...], w_two[...])
    table_two[0] = proj[:, 256:].astype(BF)
    table_two_copies = [send(table_two.at[0], table_two.at[d], u_dev(d)) for d in by_far]
    self_two[...] = proj[:rows_three, :256]
    gw_two = dot(hidden[...], gproj_two[...], ((0,), (0,))).astype(BF)
    for r in range(4):
        for q in range(4):
            a, b = place(r, q)
            two_out[a, b, :64] = gw_two[r * 64:r * 64 + 64, q * 128:q * 128 + 128]
            if r == 0 and q < 2:
                two_out[a, b, 64:] = jnp.broadcast_to(
                    bias[:, q * 128:q * 128 + 128], (16, 128)
                ).astype(BF)
            else:
                two_out[a, b, 64:] = jnp.zeros((16, 128), BF)
    two_copies = [
        send(two_out.at[:, (v + e) % SIDE], two_in.at[e - 1], v_dev(e)) for e in by_far
    ]

    def line_grads(h, d):
        ids = lax.broadcasted_iota(I32, (rows_one, half), 0)
        picks = jnp.concatenate(
            [(ids == asks[e, pl.ds(d, 1), h * half:h * half + half]).astype(BF)
             for e in range(SIDE)], axis=1
        )
        rows = jnp.concatenate(
            [msg_one[e, h * half:h * half + half] for e in range(SIDE)], axis=0
        )
        return dot(picks, rows)

    for h in range(HALVES - 1):
        for copy in msg_copies[h]:
            copy.wait_recv()

        def add_back(d, carry, h=h):
            value = line_grads(h, d)
            gsum[d] = value if h == 0 else gsum[d] + value
            return carry

        lax.fori_loop(0, SIDE, add_back, 0)
    for copy in two_copies:
        copy.wait_recv()
    for a in range(SIDE):
        two_mid[a] = add_up(
            two_out[a, v].astype(F32), [two_in[e, a] for e in range(SIDE - 1)]
        ).astype(BF)
    two_copies = [
        send(two_mid.at[(u + d) % SIDE], two_u.at[d - 1], u_dev(d)) for d in by_far
    ]

    for copy in msg_copies[HALVES - 1]:
        copy.wait_recv()
    back_one = []
    for d in (2, 1, 3, 0):
        value = gsum[d] + line_grads(HALVES - 1, d)
        if d:
            gsend[d - 1] = value.astype(BF)
            back_one.append(send(gsend.at[d - 1], grecv.at[d - 1], u_dev(-d)))
        else:
            gsum[0] = value

    for copy in two_copies:
        copy.wait_recv()
    two_z[0] = add_up(two_mid[u].astype(F32), [two_u[d] for d in range(SIDE - 1)]).astype(BF)
    two_copies = [send(two_z.at[0], two_z.at[i], feat_dev(*slots[i])) for i in range(1, FEATS)]

    for copy in table_two_copies:
        copy.wait_recv()
    y_two = []
    rows = jnp.concatenate([table_two[d] for d in range(SIDE)], axis=0)
    for e in (2, 1, 3, 0):
        ids = lax.broadcasted_iota(I32, (rows_three, rows_two), 1)
        picks = jnp.concatenate(
            [(ids == asks_col[e, rows_two:, d:d + 1]).astype(BF) for d in range(SIDE)], axis=1
        )
        value = dot(picks, rows)
        if e:
            ysend_two[e - 1] = value.astype(BF)
            y_two.append(send(ysend_two.at[e - 1], yrecv_two.at[e - 1], v_dev(-e)))
        else:
            ysum_two[...] = value

    for copy in two_copies:
        copy.wait_recv()
    two_all[u, v] = add_up(
        two_z[0].astype(F32), [two_z[i] for i in range(1, FEATS)]
    ).astype(BF)
    two_copies = [send(two_all.at[u, v], two_all.at[u, v], v_dev(e)) for e in by_far]

    for copy in y_two:
        copy.wait_recv()
    total = add_up(ysum_two[...], [yrecv_two[e] for e in range(SIDE - 1)])
    out_ref[...] = (self_two[...] + b_two[...] + total / FAN).astype(BF)

    for copy in two_copies:
        copy.wait_recv()
    two_copies = [send(two_all.at[u], two_all.at[u], u_dev(d)) for d in by_far]

    for copy in back_one:
        copy.wait_recv()
    gtab = add_up(gsum[0], [grecv[d] for d in range(SIDE - 1)]).astype(BF)

    def outer(dc):
        block = jnp.concatenate([slab[2 * dz + dc] for dz in range(4)], axis=1)
        return (dot(block[:rows_two], glin[...], ((0,), (0,))),
                dot(block, gtab, ((0,), (0,))))

    left, right = outer(1)
    pair_out[:, :256] = left.astype(BF)
    pair_out[:, 256:] = right.astype(BF)
    pair = send(pair_out, pair_in, feat_dev(0, 1))
    left, right = outer(0)
    pair.wait_recv()
    left = (left + pair_in[:, :256].astype(F32)).astype(BF)
    right = (right + pair_in[:, 256:].astype(F32)).astype(BF)
    for dz in range(4):
        for r in range(4):
            for q in range(4):
                a, b = place(r, q)
                side = left if q < 2 else right
                w_out[a, b, dz * 32:dz * 32 + 32] = side[
                    dz * 128 + r * 32:dz * 128 + r * 32 + 32,
                    (q % 2) * 128:(q % 2) * 128 + 128]

    sums = [send(w_out.at[(u + d) % SIDE], w_in.at[d - 1], u_dev(d)) for d in by_far]
    for copy in two_copies:
        copy.wait_recv()
    for r in range(4):
        for q in range(4):
            a, b = place(r, q)
            piece = two_all[a, b].astype(F32)
            gw_two_ref[r * 64:r * 64 + 64, q * 128:q * 128 + 128] = piece[:64]
            if r == 0 and q < 2:
                gb_ref[:, q * 128:q * 128 + 128] = piece[64:65]
    for copy in sums:
        copy.wait_recv()
    for b in range(SIDE):
        w_mid[b] = add_up(
            w_out[u, b].astype(F32), [w_in[d, b] for d in range(SIDE - 1)]
        ).astype(BF)
    sums = [send(w_mid.at[(v + e) % SIDE], v_in.at[e - 1], v_dev(e)) for e in by_far]
    for copy in sums:
        copy.wait_recv()
    z_out[...] = add_up(w_mid[v].astype(F32), [v_in[e] for e in range(SIDE - 1)]).astype(BF)
    sums = [
        send(z_out.at[pl.ds(dz * 32, 32)], z_in.at[dz - 1], feat_dev(-dz, 0)) for dz in by_far
    ]
    for copy in sums:
        copy.wait_recv()
    piece_all[u, v] = add_up(
        z_out[:32].astype(F32), [z_in[dz] for dz in range(3)]
    ).astype(BF)
    sums = [send(piece_all.at[u, v], piece_all.at[u, v], v_dev(e)) for e in by_far]
    for copy in sums:
        copy.wait_recv()
    sums = [send(piece_all.at[u], piece_all.at[u], u_dev(d)) for d in by_far]
    for copy in sums:
        copy.wait_recv()
    for r in range(4):
        for q in range(4):
            a, b = place(r, q)
            gw_one_ref[r * 32:r * 32 + 32, q * 128:q * 128 + 128] = piece_all[a, b].astype(F32)
    for copy in started:
        copy.wait_send()


N_COPIES = 7 * (3 + len(CHUNKS)) + 3 * (len(CHUNKS) + 2 * HALVES) + 3 * 18


def on_device(
    features, w_one, w_two, b_one, b_two, owner_one, slot_one, owner_two, slot_two, cotangent
):
    r1, r2, r3 = features.shape[1], owner_one.shape[1], owner_two.shape[1]
    vm = pl.BlockSpec(memory_space=pltpu.VMEM)
    scratch = [
        ((FEATS, r1, 128), BF), ((FEATS, 4, 4, 32, 128), BF), ((1024, 512), BF),
        ((256, 512), BF), ((1, 256), F32), ((1, 256), F32),
        ((FAN, r2), I32), ((FAN, r2), I32), ((FAN, r3), I32), ((FAN, r3), I32),
        ((r3, 256), F32), ((SIDE, 8, r2 + r3), I32),
        ((SIDE, 8, r2 + r3), I32), ((SIDE, r2 + r3, 8), I32),
        ((SIDE, r3, 256), BF), ((r2, 256), F32), ((3, r2, 256), BF), ((3, r2, 256), BF),
        ((r2, 512), BF), ((r2, 256), F32), ((SIDE, r1, 256), BF), ((r2, 256), F32),
        ((SIDE, r2, 256), F32), ((3, r2, 256), BF), ((3, r2, 256), BF), ((r2, 256), BF),
        ((r3, 256), F32), ((SIDE, r2, 256), BF), ((r3, 256), F32), ((3, r3, 256), BF),
        ((3, r3, 256), BF), ((r2, 256), BF), ((SIDE, r2, 256), BF), ((SIDE, r1, 256), F32),
        ((3, r1, 256), BF), ((3, r1, 256), BF),
        ((4, 4, 80, 128), BF), ((3, 4, 80, 128), BF), ((4, 80, 128), BF), ((3, 80, 128), BF),
        ((FEATS, 80, 128), BF), ((4, 4, 80, 128), BF),
        ((512, 512), BF), ((512, 512), BF), ((4, 4, 128, 128), BF), ((3, 4, 128, 128), BF),
        ((4, 128, 128), BF), ((3, 128, 128), BF), ((128, 128), BF), ((3, 32, 128), BF),
        ((4, 4, 32, 128), BF),
    ]
    layer_out, gw_one, gw_two, gb = pl.pallas_call(
        step_kernel,
        out_shape=[
            jax.ShapeDtypeStruct((r3, 256), BF), jax.ShapeDtypeStruct((128, 512), F32),
            jax.ShapeDtypeStruct((256, 512), F32), jax.ShapeDtypeStruct((1, 256), F32),
        ],
        in_specs=[pl.BlockSpec(memory_space=pltpu.HBM)] * 10,
        out_specs=[vm] * 4,
        scratch_shapes=[pltpu.VMEM(s, t) for s, t in scratch] + [
            pltpu.SemaphoreType.DMA((N_COPIES,)), pltpu.SemaphoreType.DMA((N_COPIES,)),
            pltpu.SemaphoreType.DMA((10,)),
        ],
        compiler_params=pltpu.CompilerParams(
            collective_id=0, has_side_effects=True, vmem_limit_bytes=36 * 2**20
        ),
        cost_estimate=pl.CostEstimate(
            flops=14 * 10**9, bytes_accessed=8 * 2**20, transcendentals=512 * 256
        ),
        name="sage_step",
    )(features, w_one, w_two, b_one[None], b_two[None], owner_one[0].T, slot_one[0].T,
      owner_two[0].T, slot_two[0].T, cotangent[0])
    return layer_out[None], gw_one, gw_two, gb[0]


def solution(mesh):
    placed = (
        P(None, "node", "feat"),
        P("feat", None),
        P(),
        P(),
        P(),
        P("feat", "node", None),
        P("feat", "node", None),
        P("feat", "node", None),
        P("feat", "node", None),
        P("feat", "node", None),
    )
    return jax.shard_map(
        on_device,
        mesh=mesh,
        in_specs=placed,
        out_specs=(P("feat", "node", None), P("feat", None), P(), P()),
        check_vma=False,
    )
```

```python
import jax
import jax.numpy as jnp
from jax import lax
from jax.experimental import pallas as pl
from jax.experimental.pallas import tpu as pltpu
from jax.sharding import PartitionSpec as P

MESH = pl.DeviceIdType.MESH
PART = 256
FEATS = 8
SIDE = 4
FAN = 8
BF = jnp.bfloat16
F32 = jnp.float32
I32 = jnp.int32


def line_place(core, node):
    low, high = node % SIDE, node // SIDE
    return (1 - core) * low + core * high, (1 - core) * high + core * low


def node_at(core, u, v):
    return (1 - core) * (v * SIDE + u) + core * (u * SIDE + v)


def dot(a, b, dims=((1,), (0,))):
    return lax.dot_general(a, b, (dims, ((), ())), preferred_element_type=F32)


def add_up(first, others):
    total = first
    for other in others:
        total += other.astype(F32)
    return total


def step_kernel(
    feat_ref, w_one_ref, w_two_ref, b_one_ref, b_two_ref, owner_one_ref, slot_one_ref,
    owner_two_ref, slot_two_ref, cot_ref,
    out_ref, gw_one_ref, gw_two_ref, gb_ref,
    slab, w_parts, w_full, w_two, b_one, b_two, own_one, slo_one, own_two, slo_two, cot,
    asks_out, asks, asks_col, msg_two, gsum_two, gsend_two, grecv_two,
    gproj_two, ghid, table, self_one, ysum, ysend, yrecv, hidden, self_two,
    table_two, ysum_two, ysend_two, yrecv_two, glin, msg_one, gsum, gsend, grecv, bias,
    two_out, two_in, two_mid, two_v, two_z, two_all,
    wall, gtab, pair_out, pair_in, w_out, w_in, w_mid, v_in, z_out, z_in, piece_all,
    ssem, rsem, lsem,
):
    f, n = lax.axis_index("feat"), lax.axis_index("node")
    z, core = f // 2, f % 2
    u, v = line_place(core, n)
    rows_one = slab.shape[1]
    rows_two = own_one.shape[1]
    rows_three = own_two.shape[1]
    chunks = rows_one // PART
    tiles = rows_two // PART
    slots = [(dz, dc) for dz in range(4) for dc in range(2)]
    others = (2, 1, 3)

    def feat_dev(dz, dc):
        return (((z + dz + 4) % 4) * 2 + (core + dc) % 2, n)

    def u_dev(d):
        return (f, node_at(core, (u + d + SIDE) % SIDE, v))

    def v_dev(e):
        return (f, node_at(core, u, (v + e + SIDE) % SIDE))

    def place(r, q):
        return (1 - core) * q + core * r, (1 - core) * r + core * q

    def tile(j, size=PART):
        return pl.ds(pl.multiple_of(j * size, size), size)

    used = [0]
    groups = []

    def group(count):
        first = used[0]
        used[0] += count
        return first

    def describe(k, src, dst, dev):
        return pltpu.make_async_remote_copy(
            src_ref=src, dst_ref=dst, send_sem=ssem.at[k], recv_sem=rsem.at[k],
            device_id=dev, device_id_type=MESH,
        )

    def send(src, dst, dev):
        copy = describe(group(1), src, dst, dev)
        copy.start()
        groups.append(copy)
        return copy

    def arrived(copies):
        for copy in copies:
            copy.wait_recv()

    barrier = pltpu.get_barrier_semaphore()
    partners = [feat_dev(*s) for s in slots[1:]]
    partners += [u_dev(d) for d in range(1, SIDE)] + [v_dev(e) for e in range(1, SIDE)]
    for dev in partners:
        pl.semaphore_signal(barrier, inc=1, device_id=dev, device_id_type=MESH)

    loads = []

    def load(src, dst):
        copy = pltpu.make_async_copy(src, dst, lsem.at[len(loads)])
        copy.start()
        loads.append(copy)
        return copy

    index_loads = [
        load(owner_one_ref, own_one), load(slot_one_ref, slo_one),
        load(owner_two_ref, own_two), load(slot_two_ref, slo_two),
    ]
    cot_load = load(cot_ref, cot)
    w_one_load = load(w_one_ref, w_full.at[pl.ds(0, 128)])
    own_load = load(feat_ref.at[f], slab.at[0])
    small_loads = [load(w_two_ref, w_two), load(b_one_ref, b_one), load(b_two_ref, b_two)]

    for copy in index_loads:
        copy.wait()

    def ask_line(e, carry):
        for own, slo, lower in ((own_one, slo_one, 0), (own_two, slo_two, rows_two)):
            owner, slot = own[...], slo[...]
            found = []
            for d in range(SIDE):
                at = node_at(core, (u - d + SIDE) % SIDE, (v + e) % SIDE)
                found.append(jnp.max(jnp.where(owner == at, slot, -1), axis=0, keepdims=True))
            found.append(jnp.full((8 - SIDE, own.shape[1]), -1, I32))
            asks_out[e, :, lower:lower + own.shape[1]] = jnp.concatenate(found, axis=0)
        return carry

    lax.fori_loop(0, SIDE, ask_line, 0)
    cot_load.wait()
    msg_two[0] = (cot[...] / FAN).astype(BF)

    def clear(j, carry):
        ysum[j] = jnp.zeros((rows_two, 256), F32)
        gsum[j] = jnp.zeros((rows_one, 256), F32)
        return carry

    lax.fori_loop(0, SIDE, clear, 0)
    bias[...] = jnp.zeros((1, 256), F32)

    pl.semaphore_wait(barrier, len(partners))

    low, high = n % SIDE, n // SIDE
    w_copies = []
    for i, (dz, dc) in enumerate(slots):
        if i:
            their_u, their_v = line_place((core + dc) % 2, n)
            w_copies.append(send(
                w_one_ref.at[pl.ds(pl.multiple_of(high * 32, 32), 32),
                             pl.ds(pl.multiple_of(low * 128, 128), 128)],
                w_parts.at[i, their_u, their_v], feat_dev(dz, dc),
            ))
    slab_at = group(7 * chunks)

    def slab_copy(c, i):
        dev = feat_dev(*slots[i])
        return describe(slab_at + c * 7 + i - 1, feat_ref.at[dev[0], tile(c)],
                        slab.at[i, tile(c)], dev)

    def send_chunk(c, carry):
        for i in (4, 5, 2, 3, 6, 7, 1):
            slab_copy(c, i).start()
        return carry

    send_chunk(0, 0)
    ask_copies = [send(asks_out.at[e], asks.at[e], v_dev(e)) for e in range(1, SIDE)]
    msg_two_copies = [send(msg_two.at[0], msg_two.at[e], v_dev(e)) for e in range(1, SIDE)]
    lax.fori_loop(1, chunks, send_chunk, 0)

    arrived(w_copies)
    mine = w_parts.at[pl.ds(1, FEATS - 1), u, v]
    along_u = [send(mine, mine, u_dev(d)) for d in range(1, SIDE)]
    asks[0] = asks_out[0]
    arrived(ask_copies)

    def turn(e, carry):
        asks_col[e] = jnp.transpose(asks[e].astype(F32)).astype(I32)
        return carry

    lax.fori_loop(0, SIDE, turn, 0)

    arrived(msg_two_copies)
    back_two_at = group(3 * tiles)

    def back_two(d, t):
        return describe(back_two_at + (d - 1) * tiles + t, gsend_two.at[d - 1, tile(t)],
                        grecv_two.at[d - 1, tile(t)], u_dev(-d))

    def back_two_step(j, carry):
        d, t = (j // tiles + 1) % SIDE, j % tiles
        ids = lax.broadcasted_iota(I32, (PART, rows_three), 0) + t * PART
        picks = jnp.concatenate(
            [(ids == asks[e, pl.ds(d, 1), rows_two:]).astype(BF) for e in range(SIDE)], axis=1
        )
        value = dot(picks, jnp.concatenate([msg_two[e] for e in range(SIDE)], axis=0))

        @pl.when(d > 0)
        def _():
            gsend_two[d - 1, tile(t)] = value.astype(BF)
            back_two(d, t).start()

        @pl.when(d == 0)
        def _():
            gsum_two[tile(t)] = value

        return carry

    lax.fori_loop(0, SIDE * tiles, back_two_step, 0)
    arrived(along_u)
    mine = w_parts.at[pl.ds(1, FEATS - 1), :, v]
    along_v = [send(mine, mine, v_dev(e)) for e in range(1, SIDE)]

    for copy in small_loads:
        copy.wait()
    arrived([back_two(d, t) for d in range(1, SIDE) for t in range(tiles)])
    gproj_two[:rows_three, :256] = cot[...].astype(BF)
    gproj_two[rows_three:, :256] = jnp.zeros((rows_two - rows_three, 256), BF)

    def ghid_step(t, carry):
        total = add_up(gsum_two[tile(t, 128)], [grecv_two[d, tile(t, 128)] for d in range(3)])
        gproj_two[tile(t, 128), 256:] = total.astype(BF)
        ghid[tile(t, 128)] = dot(gproj_two[tile(t, 128)], w_two[...], ((1,), (1,)))
        return carry

    lax.fori_loop(0, rows_two // 128, ghid_step, 0)

    arrived(along_v)
    w_one_load.wait()

    def lay_w(i, carry):
        for r in range(4):
            for q in range(4):
                a, b = place(r, q)
                w_full[pl.ds(pl.multiple_of(i * 128 + r * 32, 32), 32),
                       q * 128:q * 128 + 128] = w_parts[i, a, b]
        return carry

    lax.fori_loop(1, FEATS, lay_w, 0)
    own_load.wait()

    table_at = group(3 * chunks)
    y_at = group(3 * tiles)

    def table_copy(c, d):
        return describe(table_at + c * 3 + d - 1, table.at[0, tile(c)], table.at[d, tile(c)],
                        u_dev(d))

    def y_copy(e, h):
        return describe(y_at + h * 3 + e - 1, ysend.at[e - 1, tile(h)], yrecv.at[e - 1, tile(h)],
                        v_dev(-e))

    def chunk_step(c, carry):
        @pl.when(c < chunks)
        def _():
            arrived([slab_copy(c, i) for i in range(1, FEATS)])
            block = jnp.concatenate([slab[i, tile(c)] for i in range(FEATS)], axis=1)
            table[0, tile(c)] = dot(block, w_full[:, 256:]).astype(BF)
            for d in others:
                table_copy(c, d).start()

            @pl.when(c < tiles)
            def _():
                self_one[tile(c)] = dot(block, w_full[:, :256])

        @pl.when(c > 0)
        def _():
            arrived([table_copy(c - 1, d) for d in others])

            def sum_step(j, inner):
                h, e = j // SIDE, (j + 1) % SIDE
                ids = lax.broadcasted_iota(I32, (PART, PART), 1) + (c - 1) * PART
                picks = jnp.concatenate(
                    [(ids == asks_col[e, tile(h), d:d + 1]).astype(BF) for d in range(SIDE)],
                    axis=1,
                )
                rows = jnp.concatenate([table[d, tile(c - 1)] for d in range(SIDE)], axis=0)
                value = ysum[e, tile(h)] + dot(picks, rows)
                ysum[e, tile(h)] = value

                @pl.when((c == chunks) & (e > 0))
                def _():
                    ysend[e - 1, tile(h)] = value.astype(BF)
                    y_copy(e, h).start()

                return inner

            lax.fori_loop(0, SIDE * tiles, sum_step, 0)

        return carry

    lax.fori_loop(0, chunks + 1, chunk_step, 0)

    msg_at = group(3 * tiles)

    def msg_copy(h, e):
        return describe(msg_at + h * 3 + e - 1, msg_one.at[0, tile(h)], msg_one.at[e, tile(h)],
                        v_dev(e))

    def act_step(h, carry):
        arrived([y_copy(e, h) for e in others])

        def rows_step(t, inner):
            rows = pl.ds(pl.multiple_of(h * PART + t * 64, 64), 64)
            total = add_up(ysum[0, rows], [yrecv[e, rows] for e in range(SIDE - 1)])
            linear = self_one[rows] + b_one[...] + total / FAN
            logistic = 1.0 / (1.0 + jnp.exp(-linear))
            grad = ghid[rows] * (logistic * (1.0 + linear * (1.0 - logistic)))
            msg_one[0, rows] = (grad / FAN).astype(BF)
            glin[rows] = grad.astype(BF)
            hidden[rows] = (linear * logistic).astype(BF)
            bias[...] += jnp.sum(grad, axis=0, keepdims=True)
            return inner

        lax.fori_loop(0, PART // 64, rows_step, 0)
        for e in others:
            msg_copy(h, e).start()
        return carry

    lax.fori_loop(0, tiles, act_step, 0)

    def gw_two_step(k, carry):
        value = dot(hidden[:, tile(k, 128)], gproj_two[...], ((0,), (0,))).astype(BF)
        for r in range(2):
            for q in range(4):
                a, b = place(2 * k + r, q)
                two_out[a, b, :64] = value[r * 64:r * 64 + 64, q * 128:q * 128 + 128]
                two_out[a, b, 64:] = jnp.zeros((16, 128), BF)
        return carry

    lax.fori_loop(0, 2, gw_two_step, 0)
    for q in range(2):
        a, b = place(0, q)
        two_out[a, b, 64:] = jnp.broadcast_to(bias[:, q * 128:q * 128 + 128], (16, 128)).astype(BF)
    two_u_copies = [
        send(two_out.at[(u + d) % SIDE], two_in.at[d - 1], u_dev(d)) for d in others
    ]

    def proj_two_step(t, carry):
        proj = dot(hidden[tile(t, 128)], w_two[...])
        table_two[0, tile(t, 128)] = proj[:, 256:].astype(BF)

        @pl.when(t < rows_three // 128)
        def _():
            self_two[tile(t, 128)] = proj[:, :256]

        return carry

    lax.fori_loop(0, rows_two // 128, proj_two_step, 0)
    table_two_copies = [send(table_two.at[0], table_two.at[d], u_dev(d)) for d in others]

    two_v_at = group(3)
    back_at = group(3 * chunks)

    def two_v_copy(e):
        return describe(two_v_at + e - 1, two_mid.at[(v + e) % SIDE], two_v.at[e - 1], v_dev(e))

    def back_copy(d, t):
        return describe(back_at + (d - 1) * chunks + t, gsend.at[d - 1, tile(t)],
                        grecv.at[d - 1, tile(t)], u_dev(-d))

    def back_step(h, carry):
        @pl.when(h == tiles - 1)
        def _():
            arrived(two_u_copies)
            for b in range(SIDE):
                two_mid[b] = add_up(
                    two_out[u, b].astype(F32), [two_in[d, b] for d in range(SIDE - 1)]
                ).astype(BF)
            for e in others:
                two_v_copy(e).start()

        arrived([msg_copy(h, e) for e in others])

        def grad_step(j, inner):
            d, t = (j // chunks + 1) % SIDE, j % chunks
            ids = lax.broadcasted_iota(I32, (PART, PART), 0) + t * PART
            picks = jnp.concatenate(
                [(ids == asks[e, pl.ds(d, 1), tile(h)]).astype(BF) for e in range(SIDE)], axis=1
            )
            rows = jnp.concatenate([msg_one[e, tile(h)] for e in range(SIDE)], axis=0)
            value = gsum[d, tile(t)] + dot(picks, rows)
            gsum[d, tile(t)] = value

            @pl.when((h == tiles - 1) & (d > 0))
            def _():
                gsend[d - 1, tile(t)] = value.astype(BF)
                back_copy(d, t).start()

            return inner

        lax.fori_loop(0, SIDE * chunks, grad_step, 0)
        return carry

    lax.fori_loop(0, tiles, back_step, 0)
    arrived([two_v_copy(e) for e in others])
    two_z[0] = add_up(two_mid[v].astype(F32), [two_v[e] for e in range(SIDE - 1)]).astype(BF)
    two_z_copies = [
        send(two_z.at[0], two_z.at[i], feat_dev(*slots[i])) for i in range(1, FEATS)
    ]

    arrived(table_two_copies)
    y_two_at = group(6)

    def y_two_copy(e, h):
        return describe(y_two_at + h * 3 + e - 1, ysend_two.at[e - 1, tile(h, 128)],
                        yrecv_two.at[e - 1, tile(h, 128)], v_dev(-e))

    def y_two_step(j, carry):
        e, h = (j // 2 + 1) % SIDE, j % 2
        ids = lax.broadcasted_iota(I32, (128, rows_two), 1)
        lower = pl.ds(pl.multiple_of(rows_two + h * 128, 128), 128)
        picks = jnp.concatenate(
            [(ids == asks_col[e, lower, d:d + 1]).astype(BF) for d in range(SIDE)], axis=1
        )
        value = dot(picks, jnp.concatenate([table_two[d] for d in range(SIDE)], axis=0))

        @pl.when(e > 0)
        def _():
            ysend_two[e - 1, tile(h, 128)] = value.astype(BF)
            y_two_copy(e, h).start()

        @pl.when(e == 0)
        def _():
            ysum_two[tile(h, 128)] = value

        return carry

    lax.fori_loop(0, 2 * SIDE, y_two_step, 0)

    arrived(two_z_copies)
    two_all[u, v] = add_up(
        two_z[0].astype(F32), [two_z[i] for i in range(1, FEATS)]
    ).astype(BF)
    two_copies = [send(two_all.at[u, v], two_all.at[u, v], v_dev(e)) for e in others]
    arrived([y_two_copy(e, h) for e in others for h in range(2)])

    def out_step(t, carry):
        total = add_up(ysum_two[tile(t, 64)], [yrecv_two[e, tile(t, 64)] for e in range(3)])
        out_ref[tile(t, 64)] = (self_two[tile(t, 64)] + b_two[...] + total / FAN).astype(BF)
        return carry

    lax.fori_loop(0, rows_three // 64, out_step, 0)
    arrived(two_copies)
    two_copies = [send(two_all.at[u], two_all.at[u], u_dev(d)) for d in others]

    arrived([back_copy(d, t) for d in others for t in range(chunks)])

    def gtab_step(t, carry):
        gtab[tile(t, 128)] = add_up(
            gsum[0, tile(t, 128)], [grecv[d, tile(t, 128)] for d in range(SIDE - 1)]
        ).astype(BF)
        return carry

    lax.fori_loop(0, rows_one // 128, gtab_step, 0)
    pair_at = group(1)
    pair = describe(pair_at, pair_out, pair_in, feat_dev(0, 1))

    def outer_step(k, carry):
        block = slab[2 * (k % 4) + 1 - k // 4]
        wall[k, :, :256] = dot(block[:rows_two], glin[...], ((0,), (0,)))
        wall[k, :, 256:] = dot(block, gtab[...], ((0,), (0,)))

        @pl.when(k < 4)
        def _():
            pair_out[k] = wall[k].astype(BF)

        @pl.when(k == 3)
        def _():
            pair.start()

        return carry

    lax.fori_loop(0, FEATS, outer_step, 0)
    pair.wait_recv()

    def piece_step(dz, carry):
        value = (wall[4 + dz] + pair_in[dz].astype(F32)).astype(BF)
        for r in range(4):
            for q in range(4):
                a, b = place(r, q)
                w_out[a, b, tile(dz, 32)] = value[r * 32:r * 32 + 32, q * 128:q * 128 + 128]
        return carry

    lax.fori_loop(0, 4, piece_step, 0)

    sums = [send(w_out.at[(u + d) % SIDE], w_in.at[d - 1], u_dev(d)) for d in others]
    arrived(two_copies)

    def lay_two(r, carry):
        for q in range(4):
            a, b = place(r, q)
            gw_two_ref[tile(r, 64), q * 128:q * 128 + 128] = two_all[a, b, :64].astype(F32)
        return carry

    lax.fori_loop(0, 4, lay_two, 0)
    for q in range(2):
        a, b = place(0, q)
        gb_ref[:, q * 128:q * 128 + 128] = two_all[a, b, 64:].astype(F32)[:1]
    arrived(sums)

    def mid_step(b, carry):
        w_mid[b] = add_up(
            w_out[u, b].astype(F32), [w_in[d, b] for d in range(SIDE - 1)]
        ).astype(BF)
        return carry

    lax.fori_loop(0, SIDE, mid_step, 0)
    sums = [send(w_mid.at[(v + e) % SIDE], v_in.at[e - 1], v_dev(e)) for e in others]
    arrived(sums)
    z_out[...] = add_up(w_mid[v].astype(F32), [v_in[e] for e in range(SIDE - 1)]).astype(BF)
    sums = [
        send(z_out.at[pl.ds(dz * 32, 32)], z_in.at[dz - 1], feat_dev(-dz, 0)) for dz in others
    ]
    arrived(sums)
    piece_all[u, v] = add_up(
        z_out[:32].astype(F32), [z_in[dz] for dz in range(3)]
    ).astype(BF)
    sums = [send(piece_all.at[u, v], piece_all.at[u, v], v_dev(e)) for e in others]
    arrived(sums)
    sums = [send(piece_all.at[u], piece_all.at[u], u_dev(d)) for d in others]
    arrived(sums)

    def lay_one(r, carry):
        for q in range(4):
            a, b = place(r, q)
            gw_one_ref[tile(r, 32), q * 128:q * 128 + 128] = piece_all[a, b].astype(F32)
        return carry

    lax.fori_loop(0, 4, lay_one, 0)
    for copy in groups:
        copy.wait_send()
    pair.wait_send()

    def sent(c, carry):
        for i in range(1, FEATS):
            slab_copy(c, i).wait_send()
        for d in others:
            table_copy(c, d).wait_send()
            back_copy(d, c).wait_send()
        return carry

    lax.fori_loop(0, chunks, sent, 0)

    def sent_tiles(t, carry):
        for d in others:
            back_two(d, t).wait_send()
            y_copy(d, t).wait_send()
            msg_copy(t, d).wait_send()
        return carry

    lax.fori_loop(0, tiles, sent_tiles, 0)
    for e in others:
        two_v_copy(e).wait_send()
        for h in range(2):
            y_two_copy(e, h).wait_send()


def store_kernel(*refs):
    count = len(refs) // 2
    copies = [
        pltpu.make_async_copy(refs[i], refs[count + i], refs[-1].at[i]) for i in range(count)
    ]
    for copy in copies:
        copy.start()
    for copy in copies:
        copy.wait()


N_COPIES = 160


def on_device(
    features, w_one, w_two, b_one, b_two, owner_one, slot_one, owner_two, slot_two, cotangent
):
    r1, r2, r3 = features.shape[1], owner_one.shape[1], owner_two.shape[1]
    vm = pl.BlockSpec(memory_space=pltpu.VMEM)
    scratch = [
        ((FEATS, r1, 128), BF), ((FEATS, 4, 4, 32, 128), BF), ((1024, 512), BF),
        ((256, 512), BF), ((1, 256), F32), ((1, 256), F32),
        ((FAN, r2), I32), ((FAN, r2), I32), ((FAN, r3), I32), ((FAN, r3), I32),
        ((r3, 256), F32), ((SIDE, 8, r2 + r3), I32),
        ((SIDE, 8, r2 + r3), I32), ((SIDE, r2 + r3, 8), I32),
        ((SIDE, r3, 256), BF), ((r2, 256), F32), ((3, r2, 256), BF), ((3, r2, 256), BF),
        ((r2, 512), BF), ((r2, 256), F32), ((SIDE, r1, 256), BF), ((r2, 256), F32),
        ((SIDE, r2, 256), F32), ((3, r2, 256), BF), ((3, r2, 256), BF), ((r2, 256), BF),
        ((r3, 256), F32), ((SIDE, r2, 256), BF), ((r3, 256), F32), ((3, r3, 256), BF),
        ((3, r3, 256), BF), ((r2, 256), BF), ((SIDE, r2, 256), BF), ((SIDE, r1, 256), F32),
        ((3, r1, 256), BF), ((3, r1, 256), BF), ((1, 256), F32),
        ((4, 4, 80, 128), BF), ((3, 4, 80, 128), BF), ((4, 80, 128), BF), ((3, 80, 128), BF),
        ((FEATS, 80, 128), BF), ((4, 4, 80, 128), BF),
        ((FEATS, 128, 512), F32), ((r1, 256), BF), ((4, 128, 512), BF), ((4, 128, 512), BF),
        ((4, 4, 128, 128), BF), ((3, 4, 128, 128), BF),
        ((4, 128, 128), BF), ((3, 128, 128), BF), ((128, 128), BF), ((3, 32, 128), BF),
        ((4, 4, 32, 128), BF),
    ]
    outs = pl.pallas_call(
        step_kernel,
        out_shape=[
            jax.ShapeDtypeStruct((r3, 256), BF), jax.ShapeDtypeStruct((128, 512), F32),
            jax.ShapeDtypeStruct((256, 512), F32), jax.ShapeDtypeStruct((1, 256), F32),
        ],
        in_specs=[pl.BlockSpec(memory_space=pl.ANY)] * 10,
        out_specs=[vm] * 4,
        scratch_shapes=[pltpu.VMEM(s, t) for s, t in scratch] + [
            pltpu.SemaphoreType.DMA((N_COPIES,)), pltpu.SemaphoreType.DMA((N_COPIES,)),
            pltpu.SemaphoreType.DMA((10,)),
        ],
        compiler_params=pltpu.CompilerParams(
            collective_id=0, has_side_effects=True, vmem_limit_bytes=56 * 2**20
        ),
        cost_estimate=pl.CostEstimate(
            flops=14 * 10**9, bytes_accessed=8 * 2**20, transcendentals=512 * 256
        ),
        name="sage_step",
    )(features, w_one, w_two, b_one[None], b_two[None], owner_one[0].T, slot_one[0].T,
      owner_two[0].T, slot_two[0].T, cotangent[0])
    hbm = pl.BlockSpec(memory_space=pl.ANY)
    layer_out, gw_one, gw_two, gb = pl.pallas_call(
        store_kernel,
        out_shape=[jax.ShapeDtypeStruct(o.shape, o.dtype) for o in outs],
        in_specs=[hbm] * 4,
        out_specs=[hbm] * 4,
        scratch_shapes=[pltpu.SemaphoreType.DMA((4,))],
        compiler_params=pltpu.CompilerParams(vmem_limit_bytes=60 * 2**20),
        name="store_results",
    )(*outs)
    return layer_out[None], gw_one, gw_two, gb[0]


def solution(mesh):
    placed = (
        P(None, "node", "feat"),
        P("feat", None),
        P(),
        P(),
        P(),
        P("feat", "node", None),
        P("feat", "node", None),
        P("feat", "node", None),
        P("feat", "node", None),
        P("feat", "node", None),
    )
    return jax.shard_map(
        on_device,
        mesh=mesh,
        in_specs=placed,
        out_specs=(P("feat", "node", None), P("feat", None), P(), P()),
        check_vma=False,
    )
```

```python
import jax
import jax.numpy as jnp
from jax import lax
from jax.experimental import pallas as pl
from jax.experimental.pallas import tpu as pltpu
from jax.sharding import PartitionSpec as P

MESH = pl.DeviceIdType.MESH
PART = 256
FEATS = 8
SIDE = 4
FAN = 8
BF = jnp.bfloat16
F32 = jnp.float32
I32 = jnp.int32


def line_place(core, node):
    low, high = node % SIDE, node // SIDE
    return (1 - core) * low + core * high, (1 - core) * high + core * low


def node_at(core, u, v):
    return (1 - core) * (v * SIDE + u) + core * (u * SIDE + v)


def dot(a, b, dims=((1,), (0,))):
    return lax.dot_general(a, b, (dims, ((), ())), preferred_element_type=F32)


def add_up(first, others):
    total = first
    for other in others:
        total += other.astype(F32)
    return total


def step_kernel(
    feat_ref, w_one_ref, w_two_ref, b_one_ref, b_two_ref, owner_one_ref, slot_one_ref,
    owner_two_ref, slot_two_ref, cot_ref,
    out_ref, gw_one_ref, gw_two_ref, gb_ref,
    slab, w_parts, w_full, w_two, b_one, b_two, own_one, slo_one, own_two, slo_two, cot,
    asks_out, asks, asks_col, msg_two, gsum_two, gsend_two, grecv_two,
    gproj_two, ghid, table, self_one, ysum, ysend, yrecv, hidden, self_two,
    table_two, ysum_two, ysend_two, yrecv_two, glin, msg_one, gsum, gsend, grecv, bias,
    two_out, two_in, two_mid, two_v, two_z, two_all,
    wall, gtab, pair_out, pair_in, w_out, w_in, w_mid, v_in, z_out, z_in, piece_all,
    ssem, rsem, lsem,
):
    f, n = lax.axis_index("feat"), lax.axis_index("node")
    z, core = f // 2, f % 2
    u, v = line_place(core, n)
    rows_one = slab.shape[1]
    rows_two = own_one.shape[1]
    rows_three = own_two.shape[1]
    chunks = rows_one // PART
    tiles = rows_two // PART
    slots = [(dz, dc) for dz in range(4) for dc in range(2)]
    others = (2, 1, 3)

    def feat_dev(dz, dc):
        return (((z + dz + 4) % 4) * 2 + (core + dc) % 2, n)

    def u_dev(d):
        return (f, node_at(core, (u + d + SIDE) % SIDE, v))

    def v_dev(e):
        return (f, node_at(core, u, (v + e + SIDE) % SIDE))

    def place(r, q):
        return (1 - core) * q + core * r, (1 - core) * r + core * q

    def tile(j, size=PART):
        return pl.ds(pl.multiple_of(j * size, size), size)

    used = [0]
    groups = []

    def group(count):
        first = used[0]
        used[0] += count
        return first

    def describe(k, src, dst, dev):
        return pltpu.make_async_remote_copy(
            src_ref=src, dst_ref=dst, send_sem=ssem.at[k], recv_sem=rsem.at[k],
            device_id=dev, device_id_type=MESH,
        )

    def send(src, dst, dev):
        copy = describe(group(1), src, dst, dev)
        copy.start()
        groups.append(copy)
        return copy

    def arrived(copies):
        for copy in copies:
            copy.wait_recv()

    barrier = pltpu.get_barrier_semaphore()
    partners = [feat_dev(*s) for s in slots[1:]]
    partners += [u_dev(d) for d in range(1, SIDE)] + [v_dev(e) for e in range(1, SIDE)]
    for dev in partners:
        pl.semaphore_signal(barrier, inc=1, device_id=dev, device_id_type=MESH)

    loads = []

    def load(src, dst):
        copy = pltpu.make_async_copy(src, dst, lsem.at[len(loads)])
        copy.start()
        loads.append(copy)
        return copy

    index_loads = [
        load(owner_one_ref, own_one), load(slot_one_ref, slo_one),
        load(owner_two_ref, own_two), load(slot_two_ref, slo_two),
    ]
    cot_load = load(cot_ref, cot)
    w_one_load = load(w_one_ref, w_full.at[pl.ds(0, 128)])
    own_load = load(feat_ref.at[f], slab.at[0])
    small_loads = [load(w_two_ref, w_two), load(b_one_ref, b_one), load(b_two_ref, b_two)]

    for copy in index_loads:
        copy.wait()

    def ask_line(e, carry):
        for own, slo, lower in ((own_one, slo_one, 0), (own_two, slo_two, rows_two)):
            owner, slot = own[...], slo[...]
            found = []
            for d in range(SIDE):
                at = node_at(core, (u - d + SIDE) % SIDE, (v + e) % SIDE)
                found.append(jnp.max(jnp.where(owner == at, slot, -1), axis=0, keepdims=True))
            found.append(jnp.full((8 - SIDE, own.shape[1]), -1, I32))
            asks_out[e, :, lower:lower + own.shape[1]] = jnp.concatenate(found, axis=0)
        return carry

    lax.fori_loop(0, SIDE, ask_line, 0)
    cot_load.wait()
    msg_two[0] = (cot[...] / FAN).astype(BF)

    def clear(j, carry):
        ysum[j] = jnp.zeros((rows_two, 256), F32)
        gsum[j] = jnp.zeros((rows_one, 256), F32)
        return carry

    lax.fori_loop(0, SIDE, clear, 0)
    bias[...] = jnp.zeros((1, 256), F32)

    pl.semaphore_wait(barrier, len(partners))

    low, high = n % SIDE, n // SIDE
    w_copies = []
    for i, (dz, dc) in enumerate(slots):
        if i:
            their_u, their_v = line_place((core + dc) % 2, n)
            w_copies.append(send(
                w_one_ref.at[pl.ds(pl.multiple_of(high * 32, 32), 32),
                             pl.ds(pl.multiple_of(low * 128, 128), 128)],
                w_parts.at[i, their_u, their_v], feat_dev(dz, dc),
            ))
    slab_at = group(7 * chunks)

    def slab_copy(c, i):
        dev = feat_dev(*slots[i])
        return describe(slab_at + c * 7 + i - 1, feat_ref.at[dev[0], tile(c)],
                        slab.at[i, tile(c)], dev)

    def send_chunk(c, carry):
        for i in (4, 5, 2, 3, 6, 7, 1):
            slab_copy(c, i).start()
        return carry

    send_chunk(0, 0)
    ask_copies = [send(asks_out.at[e], asks.at[e], v_dev(e)) for e in range(1, SIDE)]
    msg_two_copies = [send(msg_two.at[0], msg_two.at[e], v_dev(e)) for e in range(1, SIDE)]
    lax.fori_loop(1, chunks, send_chunk, 0)

    arrived(w_copies)
    mine = w_parts.at[pl.ds(1, FEATS - 1), u, v]
    along_u = [send(mine, mine, u_dev(d)) for d in range(1, SIDE)]
    asks[0] = asks_out[0]
    arrived(ask_copies)

    def turn(e, carry):
        asks_col[e] = jnp.transpose(asks[e].astype(F32)).astype(I32)
        return carry

    lax.fori_loop(0, SIDE, turn, 0)

    arrived(along_u)
    mine = w_parts.at[pl.ds(1, FEATS - 1), :, v]
    along_v = [send(mine, mine, v_dev(e)) for e in range(1, SIDE)]

    arrived(msg_two_copies)
    back_two_at = group(3)

    def back_two(d):
        return describe(back_two_at + d - 1, gsend_two.at[d - 1], grecv_two.at[d - 1], u_dev(-d))

    def back_two_step(j, carry):
        d = (j + 1) % SIDE
        ids = lax.broadcasted_iota(I32, (rows_two, rows_three), 0)
        picks = jnp.concatenate(
            [(ids == asks[e, pl.ds(d, 1), rows_two:]).astype(BF) for e in range(SIDE)], axis=1
        )
        value = dot(picks, jnp.concatenate([msg_two[e] for e in range(SIDE)], axis=0))

        @pl.when(d > 0)
        def _():
            gsend_two[d - 1] = value.astype(BF)
            back_two(d).start()

        @pl.when(d == 0)
        def _():
            gsum_two[...] = value

        return carry

    lax.fori_loop(0, SIDE, back_two_step, 0)

    arrived(along_v)
    w_one_load.wait()

    def lay_w(i, carry):
        for r in range(4):
            for q in range(4):
                a, b = place(r, q)
                w_full[pl.ds(pl.multiple_of(i * 128 + r * 32, 32), 32),
                       q * 128:q * 128 + 128] = w_parts[i, a, b]
        return carry

    lax.fori_loop(1, FEATS, lay_w, 0)
    own_load.wait()

    table_at = group(3 * chunks)
    y_at = group(3 * tiles)

    def table_copy(c, d):
        return describe(table_at + c * 3 + d - 1, table.at[0, tile(c)], table.at[d, tile(c)],
                        u_dev(d))

    def y_copy(e, h):
        return describe(y_at + h * 3 + e - 1, ysend.at[e - 1, tile(h)], yrecv.at[e - 1, tile(h)],
                        v_dev(-e))

    def chunk_step(c, carry):
        @pl.when(c < chunks)
        def _():
            arrived([slab_copy(c, i) for i in range(1, FEATS)])
            block = jnp.concatenate([slab[i, tile(c)] for i in range(FEATS)], axis=1)
            table[0, tile(c)] = dot(block, w_full[:, 256:]).astype(BF)
            for d in others:
                table_copy(c, d).start()

            @pl.when(c < tiles)
            def _():
                self_one[tile(c)] = dot(block, w_full[:, :256])

        @pl.when(c > 1)
        def _():
            b = c - 2
            arrived([table_copy(b, d) for d in others])

            def sum_step(h, inner):
                ids = lax.broadcasted_iota(I32, (PART, PART), 1) + b * PART
                rows = jnp.concatenate([table[d, tile(b)] for d in range(SIDE)], axis=0)
                for e in (2, 1, 3, 0):
                    picks = jnp.concatenate(
                        [(ids == asks_col[e, tile(h), d:d + 1]).astype(BF)
                         for d in range(SIDE)], axis=1
                    )
                    ysum[e, tile(h)] += dot(picks, rows)

                @pl.when(b == chunks - 1)
                def _():
                    for e in others:
                        ysend[e - 1, tile(h)] = ysum[e, tile(h)].astype(BF)
                        y_copy(e, h).start()

                return inner

            lax.fori_loop(0, tiles, sum_step, 0)

        return carry

    lax.fori_loop(0, chunks + 2, chunk_step, 0)

    for copy in small_loads:
        copy.wait()
    arrived([back_two(d) for d in others])
    gproj_two[:rows_three, :256] = cot[...].astype(BF)
    gproj_two[rows_three:, :256] = jnp.zeros((rows_two - rows_three, 256), BF)

    total = add_up(gsum_two[...], [grecv_two[d] for d in range(SIDE - 1)])
    gproj_two[:, 256:] = total.astype(BF)
    ghid[...] = dot(gproj_two[...], w_two[...], ((1,), (1,)))

    msg_at = group(3 * tiles)

    def msg_copy(h, e):
        return describe(msg_at + h * 3 + e - 1, msg_one.at[0, tile(h)], msg_one.at[e, tile(h)],
                        v_dev(e))

    def act_step(h, carry):
        arrived([y_copy(e, h) for e in others])

        def rows_step(t, inner):
            rows = pl.ds(pl.multiple_of(h * PART + t * 128, 128), 128)
            total = add_up(ysum[0, rows], [yrecv[e, rows] for e in range(SIDE - 1)])
            linear = self_one[rows] + b_one[...] + total / FAN
            logistic = 1.0 / (1.0 + jnp.exp(-linear))
            grad = ghid[rows] * (logistic * (1.0 + linear * (1.0 - logistic)))
            msg_one[0, rows] = (grad / FAN).astype(BF)
            glin[rows] = grad.astype(BF)
            hidden[rows] = (linear * logistic).astype(BF)
            bias[...] += jnp.sum(grad, axis=0, keepdims=True)
            return inner

        lax.fori_loop(0, PART // 128, rows_step, 0)
        for e in others:
            msg_copy(h, e).start()
        return carry

    lax.fori_loop(0, tiles, act_step, 0)

    value = dot(hidden[...], gproj_two[...], ((0,), (0,))).astype(BF)
    for r in range(4):
        for q in range(4):
            a, b = place(r, q)
            two_out[a, b, :64] = value[r * 64:r * 64 + 64, q * 128:q * 128 + 128]
            two_out[a, b, 64:] = jnp.zeros((16, 128), BF)
    for q in range(2):
        a, b = place(0, q)
        two_out[a, b, 64:] = jnp.broadcast_to(bias[:, q * 128:q * 128 + 128], (16, 128)).astype(BF)
    two_u_copies = [
        send(two_out.at[(u + d) % SIDE], two_in.at[d - 1], u_dev(d)) for d in others
    ]

    proj = dot(hidden[...], w_two[...])
    table_two[0] = proj[:, 256:].astype(BF)
    self_two[...] = proj[:rows_three, :256]
    table_two_copies = [send(table_two.at[0], table_two.at[d], u_dev(d)) for d in others]

    two_v_at = group(3)
    back_at = group(3)

    def two_v_copy(e):
        return describe(two_v_at + e - 1, two_mid.at[(v + e) % SIDE], two_v.at[e - 1], v_dev(e))

    def back_copy(d):
        return describe(back_at + d - 1, gsend.at[d - 1], grecv.at[d - 1], u_dev(-d))

    def back_step(h, carry):
        @pl.when(h == tiles - 1)
        def _():
            arrived(two_u_copies)
            for b in range(SIDE):
                two_mid[b] = add_up(
                    two_out[u, b].astype(F32), [two_in[d, b] for d in range(SIDE - 1)]
                ).astype(BF)
            for e in others:
                two_v_copy(e).start()

        arrived([msg_copy(h, e) for e in others])

        def grad_step(j, inner):
            d = (j + 1) % SIDE
            ids = lax.broadcasted_iota(I32, (rows_one, PART), 0)
            picks = jnp.concatenate(
                [(ids == asks[e, pl.ds(d, 1), tile(h)]).astype(BF) for e in range(SIDE)], axis=1
            )
            rows = jnp.concatenate([msg_one[e, tile(h)] for e in range(SIDE)], axis=0)
            gsum[d] += dot(picks, rows)

            @pl.when((h == tiles - 1) & (d > 0))
            def _():
                gsend[d - 1] = gsum[d].astype(BF)
                back_copy(d).start()

            return inner

        lax.fori_loop(0, SIDE, grad_step, 0)
        return carry

    lax.fori_loop(0, tiles, back_step, 0)
    arrived([two_v_copy(e) for e in others])
    two_z[0] = add_up(two_mid[v].astype(F32), [two_v[e] for e in range(SIDE - 1)]).astype(BF)
    two_z_copies = [
        send(two_z.at[0], two_z.at[i], feat_dev(*slots[i])) for i in range(1, FEATS)
    ]

    arrived(table_two_copies)
    y_two_at = group(3)

    def y_two_copy(e):
        return describe(y_two_at + e - 1, ysend_two.at[e - 1], yrecv_two.at[e - 1], v_dev(-e))

    def y_two_step(j, carry):
        e = (j + 1) % SIDE
        ids = lax.broadcasted_iota(I32, (rows_three, rows_two), 1)
        picks = jnp.concatenate(
            [(ids == asks_col[e, rows_two:, d:d + 1]).astype(BF) for d in range(SIDE)], axis=1
        )
        value = dot(picks, jnp.concatenate([table_two[d] for d in range(SIDE)], axis=0))

        @pl.when(e > 0)
        def _():
            ysend_two[e - 1] = value.astype(BF)
            y_two_copy(e).start()

        @pl.when(e == 0)
        def _():
            ysum_two[...] = value

        return carry

    lax.fori_loop(0, SIDE, y_two_step, 0)

    arrived(two_z_copies)
    two_all[u, v] = add_up(
        two_z[0].astype(F32), [two_z[i] for i in range(1, FEATS)]
    ).astype(BF)
    two_copies = [send(two_all.at[u, v], two_all.at[u, v], v_dev(e)) for e in others]
    arrived([y_two_copy(e) for e in others])

    def out_step(t, carry):
        total = add_up(ysum_two[tile(t, 64)], [yrecv_two[e, tile(t, 64)] for e in range(3)])
        out_ref[tile(t, 64)] = (self_two[tile(t, 64)] + b_two[...] + total / FAN).astype(BF)
        return carry

    lax.fori_loop(0, rows_three // 64, out_step, 0)
    arrived(two_copies)
    two_copies = [send(two_all.at[u], two_all.at[u], u_dev(d)) for d in others]

    def outer(dc, grad):
        block = jnp.concatenate([slab[2 * dz + dc] for dz in range(4)], axis=1)
        return dot(block[:grad.shape[0]], grad[...], ((0,), (0,)))

    pair_out[0] = outer(1, glin).astype(BF)
    wall[0] = outer(0, glin)
    pairs = [send(pair_out.at[0], pair_in.at[0], feat_dev(0, 1))]
    arrived([back_copy(d) for d in others])
    gtab[...] = add_up(gsum[0], [grecv[d] for d in range(SIDE - 1)]).astype(BF)
    pair_out[1] = outer(1, gtab).astype(BF)
    pairs.append(send(pair_out.at[1], pair_in.at[1], feat_dev(0, 1)))
    wall[1] = outer(0, gtab)
    arrived(pairs)
    for k in range(2):
        value = (wall[k] + pair_in[k].astype(F32)).astype(BF)
        for dz in range(4):
            for r in range(4):
                for q in range(2):
                    a, b = place(r, 2 * k + q)
                    w_out[a, b, dz * 32:dz * 32 + 32] = value[
                        dz * 128 + r * 32:dz * 128 + r * 32 + 32, q * 128:q * 128 + 128]

    sums = [send(w_out.at[(u + d) % SIDE], w_in.at[d - 1], u_dev(d)) for d in others]
    arrived(two_copies)

    def lay_two(r, carry):
        for q in range(4):
            a, b = place(r, q)
            gw_two_ref[tile(r, 64), q * 128:q * 128 + 128] = two_all[a, b, :64].astype(F32)
        return carry

    lax.fori_loop(0, 4, lay_two, 0)
    for q in range(2):
        a, b = place(0, q)
        gb_ref[:, q * 128:q * 128 + 128] = two_all[a, b, 64:].astype(F32)[:1]
    arrived(sums)

    def mid_step(b, carry):
        w_mid[b] = add_up(
            w_out[u, b].astype(F32), [w_in[d, b] for d in range(SIDE - 1)]
        ).astype(BF)
        return carry

    lax.fori_loop(0, SIDE, mid_step, 0)
    sums = [send(w_mid.at[(v + e) % SIDE], v_in.at[e - 1], v_dev(e)) for e in others]
    arrived(sums)
    z_out[...] = add_up(w_mid[v].astype(F32), [v_in[e] for e in range(SIDE - 1)]).astype(BF)
    sums = [
        send(z_out.at[pl.ds(dz * 32, 32)], z_in.at[dz - 1], feat_dev(-dz, 0)) for dz in others
    ]
    arrived(sums)
    piece_all[u, v] = add_up(
        z_out[:32].astype(F32), [z_in[dz] for dz in range(3)]
    ).astype(BF)
    sums = [send(piece_all.at[u, v], piece_all.at[u, v], v_dev(e)) for e in others]
    arrived(sums)
    sums = [send(piece_all.at[u], piece_all.at[u], u_dev(d)) for d in others]
    arrived(sums)

    def lay_one(r, carry):
        for q in range(4):
            a, b = place(r, q)
            gw_one_ref[tile(r, 32), q * 128:q * 128 + 128] = piece_all[a, b].astype(F32)
        return carry

    lax.fori_loop(0, 4, lay_one, 0)
    for copy in groups:
        copy.wait_send()

    def sent(c, carry):
        for i in range(1, FEATS):
            slab_copy(c, i).wait_send()
        for d in others:
            table_copy(c, d).wait_send()
        return carry

    lax.fori_loop(0, chunks, sent, 0)

    def sent_tiles(t, carry):
        for d in others:
            y_copy(d, t).wait_send()
            msg_copy(t, d).wait_send()
        return carry

    lax.fori_loop(0, tiles, sent_tiles, 0)
    for e in others:
        two_v_copy(e).wait_send()
        y_two_copy(e).wait_send()
        back_two(e).wait_send()
        back_copy(e).wait_send()


N_COPIES = 160


def on_device(
    features, w_one, w_two, b_one, b_two, owner_one, slot_one, owner_two, slot_two, cotangent
):
    r1, r2, r3 = features.shape[1], owner_one.shape[1], owner_two.shape[1]
    vm = pl.BlockSpec(memory_space=pltpu.VMEM)
    scratch = [
        ((FEATS, r1, 128), BF), ((FEATS, 4, 4, 32, 128), BF), ((1024, 512), BF),
        ((256, 512), BF), ((1, 256), F32), ((1, 256), F32),
        ((FAN, r2), I32), ((FAN, r2), I32), ((FAN, r3), I32), ((FAN, r3), I32),
        ((r3, 256), F32), ((SIDE, 8, r2 + r3), I32),
        ((SIDE, 8, r2 + r3), I32), ((SIDE, r2 + r3, 8), I32),
        ((SIDE, r3, 256), BF), ((r2, 256), F32), ((3, r2, 256), BF), ((3, r2, 256), BF),
        ((r2, 512), BF), ((r2, 256), F32), ((SIDE, r1, 256), BF), ((r2, 256), F32),
        ((SIDE, r2, 256), F32), ((3, r2, 256), BF), ((3, r2, 256), BF), ((r2, 256), BF),
        ((r3, 256), F32), ((SIDE, r2, 256), BF), ((r3, 256), F32), ((3, r3, 256), BF),
        ((3, r3, 256), BF), ((r2, 256), BF), ((SIDE, r2, 256), BF), ((SIDE, r1, 256), F32),
        ((3, r1, 256), BF), ((3, r1, 256), BF), ((1, 256), F32),
        ((4, 4, 80, 128), BF), ((3, 4, 80, 128), BF), ((4, 80, 128), BF), ((3, 80, 128), BF),
        ((FEATS, 80, 128), BF), ((4, 4, 80, 128), BF),
        ((2, 512, 256), F32), ((r1, 256), BF), ((2, 512, 256), BF), ((2, 512, 256), BF),
        ((4, 4, 128, 128), BF), ((3, 4, 128, 128), BF),
        ((4, 128, 128), BF), ((3, 128, 128), BF), ((128, 128), BF), ((3, 32, 128), BF),
        ((4, 4, 32, 128), BF),
    ]
    layer_out, gw_one, gw_two, gb = pl.pallas_call(
        step_kernel,
        out_shape=[
            jax.ShapeDtypeStruct((r3, 256), BF), jax.ShapeDtypeStruct((128, 512), F32),
            jax.ShapeDtypeStruct((256, 512), F32), jax.ShapeDtypeStruct((1, 256), F32),
        ],
        in_specs=[pl.BlockSpec(memory_space=pl.ANY)] * 10,
        out_specs=[vm] * 4,
        scratch_shapes=[pltpu.VMEM(s, t) for s, t in scratch] + [
            pltpu.SemaphoreType.DMA((N_COPIES,)), pltpu.SemaphoreType.DMA((N_COPIES,)),
            pltpu.SemaphoreType.DMA((10,)),
        ],
        compiler_params=pltpu.CompilerParams(
            collective_id=0, has_side_effects=True, vmem_limit_bytes=56 * 2**20
        ),
        cost_estimate=pl.CostEstimate(
            flops=14 * 10**9, bytes_accessed=8 * 2**20, transcendentals=512 * 256
        ),
        name="sage_step",
    )(features, w_one, w_two, b_one[None], b_two[None], owner_one[0].T, slot_one[0].T,
      owner_two[0].T, slot_two[0].T, cotangent[0])
    return layer_out[None], gw_one, gw_two, gb[0]


def solution(mesh):
    placed = (
        P(None, "node", "feat"),
        P("feat", None),
        P(),
        P(),
        P(),
        P("feat", "node", None),
        P("feat", "node", None),
        P("feat", "node", None),
        P("feat", "node", None),
        P("feat", "node", None),
    )
    return jax.shard_map(
        on_device,
        mesh=mesh,
        in_specs=placed,
        out_specs=(P("feat", "node", None), P("feat", None), P(), P()),
        check_vma=False,
    )
```

```python
import jax
import jax.numpy as jnp
from jax import lax
from jax.experimental import pallas as pl
from jax.experimental.pallas import tpu as pltpu
from jax.sharding import PartitionSpec as P

MESH = pl.DeviceIdType.MESH
PART = 256
FEATS = 8
SIDE = 4
FAN = 8
BF = jnp.bfloat16
F32 = jnp.float32
I32 = jnp.int32


def line_place(core, node):
    low, high = node % SIDE, node // SIDE
    return (1 - core) * low + core * high, (1 - core) * high + core * low


def node_at(core, u, v):
    return (1 - core) * (v * SIDE + u) + core * (u * SIDE + v)


def dot(a, b, dims=((1,), (0,))):
    return lax.dot_general(a, b, (dims, ((), ())), preferred_element_type=F32)


def add_up(first, others):
    total = first
    for other in others:
        total += other.astype(F32)
    return total


def step_kernel(
    feat_ref, w_one_ref, w_two_ref, b_one_ref, b_two_ref, owner_one_ref, slot_one_ref,
    owner_two_ref, slot_two_ref, cot_ref,
    out_ref, gw_one_ref, gw_two_ref, gb_ref,
    slab, w_parts, w_full, w_two, b_one, b_two, own_one, slo_one, own_two, slo_two, cot,
    asks_out, asks, asks_col, msg_two, gsum_two, gsend_two, grecv_two,
    gproj_two, ghid, table, self_one, ysum, ysend, yrecv, hidden, self_two,
    table_two, ysum_two, ysend_two, yrecv_two, glin, msg_one, gsum, gsend, grecv, bias,
    two_out, two_in, two_mid, two_v, two_z, two_all,
    wall, gtab, pair_out, pair_in, w_out, w_in, w_mid, v_in, z_out, z_in, piece_all,
    ssem, rsem, lsem,
):
    f, n = lax.axis_index("feat"), lax.axis_index("node")
    z, core = f // 2, f % 2
    u, v = line_place(core, n)
    rows_one = slab.shape[1]
    rows_two = own_one.shape[1]
    rows_three = own_two.shape[1]
    chunks = rows_one // PART
    tiles = rows_two // PART
    slots = [(dz, dc) for dz in range(4) for dc in range(2)]
    others = (2, 1, 3)

    def feat_dev(dz, dc):
        return (((z + dz + 4) % 4) * 2 + (core + dc) % 2, n)

    def u_dev(d):
        return (f, node_at(core, (u + d + SIDE) % SIDE, v))

    def v_dev(e):
        return (f, node_at(core, u, (v + e + SIDE) % SIDE))

    def place(r, q):
        return (1 - core) * q + core * r, (1 - core) * r + core * q

    def tile(j, size=PART):
        return pl.ds(pl.multiple_of(j * size, size), size)

    used = [0]
    groups = []

    def group(count):
        first = used[0]
        used[0] += count
        return first

    def describe(k, src, dst, dev):
        return pltpu.make_async_remote_copy(
            src_ref=src, dst_ref=dst, send_sem=ssem.at[k], recv_sem=rsem.at[k],
            device_id=dev, device_id_type=MESH,
        )

    def send(src, dst, dev):
        copy = describe(group(1), src, dst, dev)
        copy.start()
        groups.append(copy)
        return copy

    def arrived(copies):
        for copy in copies:
            copy.wait_recv()

    barrier = pltpu.get_barrier_semaphore()
    partners = [feat_dev(*s) for s in slots[1:]]
    partners += [u_dev(d) for d in range(1, SIDE)] + [v_dev(e) for e in range(1, SIDE)]
    for dev in partners:
        pl.semaphore_signal(barrier, inc=1, device_id=dev, device_id_type=MESH)

    loads = []

    def load(src, dst):
        copy = pltpu.make_async_copy(src, dst, lsem.at[len(loads)])
        copy.start()
        loads.append(copy)
        return copy

    index_loads = [
        load(owner_one_ref, own_one), load(slot_one_ref, slo_one),
        load(owner_two_ref, own_two), load(slot_two_ref, slo_two),
    ]
    cot_load = load(cot_ref, cot)
    w_one_load = load(w_one_ref, w_full.at[pl.ds(0, 128)])
    own_load = load(feat_ref.at[f], slab.at[0])
    small_loads = [load(w_two_ref, w_two), load(b_one_ref, b_one), load(b_two_ref, b_two)]

    pl.semaphore_wait(barrier, len(partners))

    low, high = n % SIDE, n // SIDE
    w_piece = w_one_ref.at[pl.ds(pl.multiple_of(high * 32, 32), 32),
                           pl.ds(pl.multiple_of(low * 128, 128), 128)]
    w_copies = [send(w_piece, w_parts.at[dz - 1, u, v], feat_dev(dz, 0)) for dz in others]
    slab_at = group(7 * chunks)

    def slab_copy(c, i):
        dev = feat_dev(*slots[i])
        return describe(slab_at + c * 7 + i - 1, feat_ref.at[dev[0], tile(c)],
                        slab.at[i, tile(c)], dev)

    def send_chunk(c, carry):
        for i in (4, 5, 2, 3, 6, 7, 1):
            slab_copy(c, i).start()
        return carry

    send_chunk(0, 0)
    w_pairs = [send(w_one_ref, w_full.at[pl.ds(128, 128)], feat_dev(0, 1))]

    for copy in index_loads:
        copy.wait()

    def ask_line(e, carry):
        for own, slo, lower in ((own_one, slo_one, 0), (own_two, slo_two, rows_two)):
            owner, slot = own[...], slo[...]
            found = []
            for d in range(SIDE):
                at = node_at(core, (u - d + SIDE) % SIDE, (v + e) % SIDE)
                found.append(jnp.max(jnp.where(owner == at, slot, -1), axis=0, keepdims=True))
            found.append(jnp.full((8 - SIDE, own.shape[1]), -1, I32))
            asks_out[e, :, lower:lower + own.shape[1]] = jnp.concatenate(found, axis=0)
        return carry

    lax.fori_loop(0, SIDE, ask_line, 0)
    cot_load.wait()
    msg_two[0] = (cot[...] / FAN).astype(BF)

    ask_copies = [send(asks_out.at[e], asks.at[e], v_dev(e)) for e in range(1, SIDE)]
    msg_two_copies = [send(msg_two.at[0], msg_two.at[e], v_dev(e)) for e in range(1, SIDE)]
    send_chunk(1, 0)

    arrived(w_copies)
    mine = w_parts.at[:, u, v]
    along_u = [send(mine, mine, u_dev(d)) for d in range(1, SIDE)]
    lax.fori_loop(2, chunks, send_chunk, 0)
    asks[0] = asks_out[0]
    arrived(ask_copies)

    def turn(e, carry):
        asks_col[e] = jnp.transpose(asks[e].astype(F32)).astype(I32)
        return carry

    lax.fori_loop(0, SIDE, turn, 0)
    arrived(along_u)
    mine = w_parts.at[:, :, v]
    along_v = [send(mine, mine, v_dev(e)) for e in range(1, SIDE)]

    def clear(j, carry):
        ysum[j] = jnp.zeros((rows_two, 256), F32)
        return carry

    lax.fori_loop(0, SIDE, clear, 0)
    bias[...] = jnp.zeros((1, 256), F32)

    arrived(msg_two_copies)
    back_two_at = group(3)

    def back_two(d):
        return describe(back_two_at + d - 1, gsend_two.at[d - 1], grecv_two.at[d - 1], u_dev(-d))

    def back_two_step(j, carry):
        d = (j + 1) % SIDE
        ids = lax.broadcasted_iota(I32, (rows_two, rows_three), 0)
        picks = jnp.concatenate(
            [(ids == asks[e, pl.ds(d, 1), rows_two:]).astype(BF) for e in range(SIDE)], axis=1
        )
        value = dot(picks, jnp.concatenate([msg_two[e] for e in range(SIDE)], axis=0))

        @pl.when(d > 0)
        def _():
            gsend_two[d - 1] = value.astype(BF)
            back_two(d).start()

        @pl.when(d == 0)
        def _():
            gsum_two[...] = value

        return carry

    lax.fori_loop(0, SIDE, back_two_step, 0)

    arrived(along_v)
    w_one_load.wait()

    for dz in range(1, SIDE):
        for r in range(4):
            for q in range(4):
                a, b = place(r, q)
                w_full[dz * 256 + r * 32:dz * 256 + r * 32 + 32, q * 128:q * 128 + 128] = (
                    w_parts[dz - 1, a, b]
                )
        w_pairs.append(send(w_full.at[pl.ds(dz * 256, 128)],
                            w_full.at[pl.ds(dz * 256 + 128, 128)], feat_dev(0, 1)))
    arrived(w_pairs)
    own_load.wait()

    table_at = group(3 * chunks)
    y_at = group(3 * tiles)

    def table_copy(c, d):
        return describe(table_at + c * 3 + d - 1, table.at[0, tile(c)], table.at[d, tile(c)],
                        u_dev(d))

    def y_copy(e, h):
        return describe(y_at + h * 3 + e - 1, ysend.at[e - 1, tile(h)], yrecv.at[e - 1, tile(h)],
                        v_dev(-e))

    def chunk_step(c, carry):
        @pl.when(c < chunks)
        def _():
            arrived([slab_copy(c, i) for i in range(1, FEATS)])
            block = jnp.concatenate([slab[i, tile(c)] for i in range(FEATS)], axis=1)
            table[0, tile(c)] = dot(block, w_full[:, 256:]).astype(BF)
            for d in others:
                table_copy(c, d).start()

            @pl.when(c < tiles)
            def _():
                self_one[tile(c)] = dot(block, w_full[:, :256])

        @pl.when(c > 1)
        def _():
            b = c - 2
            arrived([table_copy(b, d) for d in others])

            def sum_step(h, inner):
                ids = lax.broadcasted_iota(I32, (PART, PART), 1) + b * PART
                rows = jnp.concatenate([table[d, tile(b)] for d in range(SIDE)], axis=0)
                for e in (2, 1, 3, 0):
                    picks = jnp.concatenate(
                        [(ids == asks_col[e, tile(h), d:d + 1]).astype(BF)
                         for d in range(SIDE)], axis=1
                    )
                    ysum[e, tile(h)] += dot(picks, rows)

                @pl.when(b == chunks - 1)
                def _():
                    for e in others:
                        ysend[e - 1, tile(h)] = ysum[e, tile(h)].astype(BF)
                        y_copy(e, h).start()

                return inner

            lax.fori_loop(0, tiles, sum_step, 0)

        return carry

    lax.fori_loop(0, chunks + 2, chunk_step, 0)

    for copy in small_loads:
        copy.wait()
    arrived([back_two(d) for d in others])
    gproj_two[:rows_three, :256] = cot[...].astype(BF)
    gproj_two[rows_three:, :256] = jnp.zeros((rows_two - rows_three, 256), BF)

    total = add_up(gsum_two[...], [grecv_two[d] for d in range(SIDE - 1)])
    gproj_two[:, 256:] = total.astype(BF)
    ghid[...] = dot(gproj_two[...], w_two[...], ((1,), (1,)))

    msg_at = group(3 * tiles)

    def msg_copy(h, e):
        return describe(msg_at + h * 3 + e - 1, msg_one.at[0, tile(h)], msg_one.at[e, tile(h)],
                        v_dev(e))

    def act_step(h, carry):
        arrived([y_copy(e, h) for e in others])

        def rows_step(t, inner):
            rows = pl.ds(pl.multiple_of(h * PART + t * 128, 128), 128)
            total = add_up(ysum[0, rows], [yrecv[e, rows] for e in range(SIDE - 1)])
            linear = self_one[rows] + b_one[...] + total / FAN
            logistic = 1.0 / (1.0 + jnp.exp(-linear))
            grad = ghid[rows] * (logistic * (1.0 + linear * (1.0 - logistic)))
            msg_one[0, rows] = (grad / FAN).astype(BF)
            glin[rows] = grad.astype(BF)
            hidden[rows] = (linear * logistic).astype(BF)
            bias[...] += jnp.sum(grad, axis=0, keepdims=True)
            return inner

        lax.fori_loop(0, PART // 128, rows_step, 0)
        for e in others:
            msg_copy(h, e).start()
        return carry

    lax.fori_loop(0, tiles, act_step, 0)

    value = dot(hidden[...], gproj_two[...], ((0,), (0,))).astype(BF)
    for r in range(4):
        for q in range(4):
            a, b = place(r, q)
            two_out[a, b, :64] = value[r * 64:r * 64 + 64, q * 128:q * 128 + 128]
            two_out[a, b, 64:] = jnp.zeros((16, 128), BF)
    for q in range(2):
        a, b = place(0, q)
        two_out[a, b, 64:] = jnp.broadcast_to(bias[:, q * 128:q * 128 + 128], (16, 128)).astype(BF)
    two_u_copies = [
        send(two_out.at[(u + d) % SIDE], two_in.at[d - 1], u_dev(d)) for d in others
    ]

    proj = dot(hidden[...], w_two[...])
    table_two[0] = proj[:, 256:].astype(BF)
    self_two[...] = proj[:rows_three, :256]
    table_two_copies = [send(table_two.at[0], table_two.at[d], u_dev(d)) for d in others]

    two_v_at = group(3)
    back_at = group(3)

    def two_v_copy(e):
        return describe(two_v_at + e - 1, two_mid.at[(v + e) % SIDE], two_v.at[e - 1], v_dev(e))

    def back_copy(d):
        return describe(back_at + d - 1, gsend.at[d - 1], grecv.at[d - 1], u_dev(-d))

    def line_grads(e, d):
        ids = lax.broadcasted_iota(I32, (rows_one, rows_two), 0)
        return dot((ids == asks[e, pl.ds(d, 1), :rows_two]).astype(BF), msg_one[e])

    def own_step(d, carry):
        gsum[d] = line_grads(0, d)
        return carry

    lax.fori_loop(0, SIDE, own_step, 0)
    arrived(two_u_copies)
    for b in range(SIDE):
        two_mid[b] = add_up(
            two_out[u, b].astype(F32), [two_in[d, b] for d in range(SIDE - 1)]
        ).astype(BF)
    for e in others:
        two_v_copy(e).start()
    arrived([msg_copy(h, e) for h in range(tiles) for e in others])

    def back_step(j, carry):
        d = (j + 1) % SIDE
        value = gsum[d]
        for e in range(1, SIDE):
            value += line_grads(e, d)

        @pl.when(d > 0)
        def _():
            gsend[d - 1] = value.astype(BF)
            back_copy(d).start()

        @pl.when(d == 0)
        def _():
            gsum[0] = value

        return carry

    lax.fori_loop(0, SIDE, back_step, 0)
    arrived([two_v_copy(e) for e in others])
    two_z[0] = add_up(two_mid[v].astype(F32), [two_v[e] for e in range(SIDE - 1)]).astype(BF)
    two_z_copies = [
        send(two_z.at[0], two_z.at[i], feat_dev(*slots[i])) for i in range(1, FEATS)
    ]

    arrived(table_two_copies)
    y_two_at = group(3)

    def y_two_copy(e):
        return describe(y_two_at + e - 1, ysend_two.at[e - 1], yrecv_two.at[e - 1], v_dev(-e))

    def y_two_step(j, carry):
        e = (j + 1) % SIDE
        ids = lax.broadcasted_iota(I32, (rows_three, rows_two), 1)
        picks = jnp.concatenate(
            [(ids == asks_col[e, rows_two:, d:d + 1]).astype(BF) for d in range(SIDE)], axis=1
        )
        value = dot(picks, jnp.concatenate([table_two[d] for d in range(SIDE)], axis=0))

        @pl.when(e > 0)
        def _():
            ysend_two[e - 1] = value.astype(BF)
            y_two_copy(e).start()

        @pl.when(e == 0)
        def _():
            ysum_two[...] = value

        return carry

    lax.fori_loop(0, SIDE, y_two_step, 0)

    arrived(two_z_copies)
    two_all[u, v] = add_up(
        two_z[0].astype(F32), [two_z[i] for i in range(1, FEATS)]
    ).astype(BF)
    two_copies = [send(two_all.at[u, v], two_all.at[u, v], v_dev(e)) for e in others]
    arrived([y_two_copy(e) for e in others])

    def out_step(t, carry):
        total = add_up(ysum_two[tile(t, 64)], [yrecv_two[e, tile(t, 64)] for e in range(3)])
        out_ref[tile(t, 64)] = (self_two[tile(t, 64)] + b_two[...] + total / FAN).astype(BF)
        return carry

    lax.fori_loop(0, rows_three // 64, out_step, 0)
    arrived(two_copies)
    two_copies = [send(two_all.at[u], two_all.at[u], u_dev(d)) for d in others]

    def outer(dc, grad):
        block = jnp.concatenate([slab[2 * dz + dc] for dz in range(4)], axis=1)
        return dot(block[:grad.shape[0]], grad[...], ((0,), (0,)))

    pair_out[0] = outer(1, glin).astype(BF)
    wall[0] = outer(0, glin)
    pairs = [send(pair_out.at[0], pair_in.at[0], feat_dev(0, 1))]
    arrived([back_copy(d) for d in others])
    gtab[...] = add_up(gsum[0], [grecv[d] for d in range(SIDE - 1)]).astype(BF)
    pair_out[1] = outer(1, gtab).astype(BF)
    pairs.append(send(pair_out.at[1], pair_in.at[1], feat_dev(0, 1)))
    wall[1] = outer(0, gtab)
    arrived(pairs)
    for k in range(2):
        value = (wall[k] + pair_in[k].astype(F32)).astype(BF)
        for dz in range(4):
            for r in range(4):
                for q in range(2):
                    a, b = place(r, 2 * k + q)
                    w_out[a, b, dz * 32:dz * 32 + 32] = value[
                        dz * 128 + r * 32:dz * 128 + r * 32 + 32, q * 128:q * 128 + 128]

    sums = [send(w_out.at[(u + d) % SIDE], w_in.at[d - 1], u_dev(d)) for d in others]
    arrived(two_copies)

    def lay_two(r, carry):
        for q in range(4):
            a, b = place(r, q)
            gw_two_ref[tile(r, 64), q * 128:q * 128 + 128] = two_all[a, b, :64].astype(F32)
        return carry

    lax.fori_loop(0, 4, lay_two, 0)
    for q in range(2):
        a, b = place(0, q)
        gb_ref[:, q * 128:q * 128 + 128] = two_all[a, b, 64:].astype(F32)[:1]
    arrived(sums)

    def mid_step(b, carry):
        w_mid[b] = add_up(
            w_out[u, b].astype(F32), [w_in[d, b] for d in range(SIDE - 1)]
        ).astype(BF)
        return carry

    lax.fori_loop(0, SIDE, mid_step, 0)
    sums = [send(w_mid.at[(v + e) % SIDE], v_in.at[e - 1], v_dev(e)) for e in others]
    arrived(sums)
    z_out[...] = add_up(w_mid[v].astype(F32), [v_in[e] for e in range(SIDE - 1)]).astype(BF)
    sums = [
        send(z_out.at[pl.ds(dz * 32, 32)], z_in.at[dz - 1], feat_dev(-dz, 0)) for dz in others
    ]
    arrived(sums)
    piece_all[u, v] = add_up(
        z_out[:32].astype(F32), [z_in[dz] for dz in range(3)]
    ).astype(BF)
    sums = [send(piece_all.at[u, v], piece_all.at[u, v], v_dev(e)) for e in others]
    arrived(sums)
    sums = [send(piece_all.at[u], piece_all.at[u], u_dev(d)) for d in others]
    arrived(sums)

    def lay_one(r, carry):
        for q in range(4):
            a, b = place(r, q)
            gw_one_ref[tile(r, 32), q * 128:q * 128 + 128] = piece_all[a, b].astype(F32)
        return carry

    lax.fori_loop(0, 4, lay_one, 0)
    for copy in groups:
        copy.wait_send()

    def sent(c, carry):
        for i in range(1, FEATS):
            slab_copy(c, i).wait_send()
        for d in others:
            table_copy(c, d).wait_send()
        return carry

    lax.fori_loop(0, chunks, sent, 0)

    def sent_tiles(t, carry):
        for d in others:
            y_copy(d, t).wait_send()
            msg_copy(t, d).wait_send()
        return carry

    lax.fori_loop(0, tiles, sent_tiles, 0)
    for e in others:
        two_v_copy(e).wait_send()
        y_two_copy(e).wait_send()
        back_two(e).wait_send()
        back_copy(e).wait_send()


N_COPIES = 160


def on_device(
    features, w_one, w_two, b_one, b_two, owner_one, slot_one, owner_two, slot_two, cotangent
):
    r1, r2, r3 = features.shape[1], owner_one.shape[1], owner_two.shape[1]
    vm = pl.BlockSpec(memory_space=pltpu.VMEM)
    scratch = [
        ((FEATS, r1, 128), BF), ((3, 4, 4, 32, 128), BF), ((1024, 512), BF),
        ((256, 512), BF), ((1, 256), F32), ((1, 256), F32),
        ((FAN, r2), I32), ((FAN, r2), I32), ((FAN, r3), I32), ((FAN, r3), I32),
        ((r3, 256), F32), ((SIDE, 8, r2 + r3), I32),
        ((SIDE, 8, r2 + r3), I32), ((SIDE, r2 + r3, 8), I32),
        ((SIDE, r3, 256), BF), ((r2, 256), F32), ((3, r2, 256), BF), ((3, r2, 256), BF),
        ((r2, 512), BF), ((r2, 256), F32), ((SIDE, r1, 256), BF), ((r2, 256), F32),
        ((SIDE, r2, 256), F32), ((3, r2, 256), BF), ((3, r2, 256), BF), ((r2, 256), BF),
        ((r3, 256), F32), ((SIDE, r2, 256), BF), ((r3, 256), F32), ((3, r3, 256), BF),
        ((3, r3, 256), BF), ((r2, 256), BF), ((SIDE, r2, 256), BF), ((SIDE, r1, 256), F32),
        ((3, r1, 256), BF), ((3, r1, 256), BF), ((1, 256), F32),
        ((4, 4, 80, 128), BF), ((3, 4, 80, 128), BF), ((4, 80, 128), BF), ((3, 80, 128), BF),
        ((FEATS, 80, 128), BF), ((4, 4, 80, 128), BF),
        ((2, 512, 256), F32), ((r1, 256), BF), ((2, 512, 256), BF), ((2, 512, 256), BF),
        ((4, 4, 128, 128), BF), ((3, 4, 128, 128), BF),
        ((4, 128, 128), BF), ((3, 128, 128), BF), ((128, 128), BF), ((3, 32, 128), BF),
        ((4, 4, 32, 128), BF),
    ]
    layer_out, gw_one, gw_two, gb = pl.pallas_call(
        step_kernel,
        out_shape=[
            jax.ShapeDtypeStruct((r3, 256), BF), jax.ShapeDtypeStruct((128, 512), F32),
            jax.ShapeDtypeStruct((256, 512), F32), jax.ShapeDtypeStruct((1, 256), F32),
        ],
        in_specs=[pl.BlockSpec(memory_space=pl.ANY)] * 10,
        out_specs=[vm] * 4,
        scratch_shapes=[pltpu.VMEM(s, t) for s, t in scratch] + [
            pltpu.SemaphoreType.DMA((N_COPIES,)), pltpu.SemaphoreType.DMA((N_COPIES,)),
            pltpu.SemaphoreType.DMA((10,)),
        ],
        compiler_params=pltpu.CompilerParams(
            collective_id=0, has_side_effects=True, vmem_limit_bytes=56 * 2**20
        ),
        cost_estimate=pl.CostEstimate(
            flops=14 * 10**9, bytes_accessed=8 * 2**20, transcendentals=512 * 256
        ),
        name="sage_step",
    )(features, w_one, w_two, b_one[None], b_two[None], owner_one[0].T, slot_one[0].T,
      owner_two[0].T, slot_two[0].T, cotangent[0])
    return layer_out[None], gw_one, gw_two, gb[0]


def solution(mesh):
    placed = (
        P(None, "node", "feat"),
        P("feat", None),
        P(),
        P(),
        P(),
        P("feat", "node", None),
        P("feat", "node", None),
        P("feat", "node", None),
        P("feat", "node", None),
        P("feat", "node", None),
    )
    return jax.shard_map(
        on_device,
        mesh=mesh,
        in_specs=placed,
        out_specs=(P("feat", "node", None), P("feat", None), P(), P()),
        check_vma=False,
    )
```

```python
import jax
import jax.numpy as jnp
from jax import lax
from jax.experimental import pallas as pl
from jax.experimental.pallas import tpu as pltpu
from jax.sharding import PartitionSpec as P

MESH = pl.DeviceIdType.MESH
PART = 256
FEATS = 8
SIDE = 4
FAN = 8
BF = jnp.bfloat16
F32 = jnp.float32
I32 = jnp.int32


def line_place(core, node):
    low, high = node % SIDE, node // SIDE
    return (1 - core) * low + core * high, (1 - core) * high + core * low


def node_at(core, u, v):
    return (1 - core) * (v * SIDE + u) + core * (u * SIDE + v)


def dot(a, b, dims=((1,), (0,))):
    return lax.dot_general(a, b, (dims, ((), ())), preferred_element_type=F32)


def add_up(first, others):
    total = first
    for other in others:
        total += other.astype(F32)
    return total


def step_kernel(
    feat_ref, w_one_ref, w_two_ref, b_one_ref, b_two_ref, owner_one_ref, slot_one_ref,
    owner_two_ref, slot_two_ref, cot_ref,
    out_ref, gw_one_ref, gw_two_ref, gb_ref,
    slab, w_parts, w_full, w_two, b_one, b_two, own_one, slo_one, own_two, slo_two, cot,
    asks_out, asks, asks_col, msg_two, gsum_two, gsend_two, grecv_two,
    gproj_two, ghid, table, self_one, ysum, ysend, yrecv, hidden, self_two,
    table_two, ysum_two, ysend_two, yrecv_two, glin, msg_one, gsum, gsend, grecv, bias,
    two_out, two_in, two_mid, two_v, two_z, two_all,
    wall, gtab, pair_out, pair_in, w_out, w_in, w_mid, v_in, z_out, z_in, piece_all,
    ssem, rsem, lsem,
):
    f, n = lax.axis_index("feat"), lax.axis_index("node")
    z, core = f // 2, f % 2
    u, v = line_place(core, n)
    rows_one = slab.shape[1]
    rows_two = own_one.shape[1]
    rows_three = own_two.shape[1]
    chunks = rows_one // PART
    tiles = rows_two // PART
    slots = [(dz, dc) for dz in range(4) for dc in range(2)]
    others = (2, 1, 3)

    def feat_dev(dz, dc):
        return (((z + dz + 4) % 4) * 2 + (core + dc) % 2, n)

    def u_dev(d):
        return (f, node_at(core, (u + d + SIDE) % SIDE, v))

    def v_dev(e):
        return (f, node_at(core, u, (v + e + SIDE) % SIDE))

    def place(r, q):
        return (1 - core) * q + core * r, (1 - core) * r + core * q

    def tile(j, size=PART):
        return pl.ds(pl.multiple_of(j * size, size), size)

    used = [0]
    groups = []

    def group(count):
        first = used[0]
        used[0] += count
        return first

    def describe(k, src, dst, dev):
        return pltpu.make_async_remote_copy(
            src_ref=src, dst_ref=dst, send_sem=ssem.at[k], recv_sem=rsem.at[k],
            device_id=dev, device_id_type=MESH,
        )

    def send(src, dst, dev):
        copy = describe(group(1), src, dst, dev)
        copy.start()
        groups.append(copy)
        return copy

    def arrived(copies):
        for copy in copies:
            copy.wait_recv()

    barrier = pltpu.get_barrier_semaphore()
    partners = [feat_dev(*s) for s in slots[1:]]
    partners += [u_dev(d) for d in range(1, SIDE)] + [v_dev(e) for e in range(1, SIDE)]
    for dev in partners:
        pl.semaphore_signal(barrier, inc=1, device_id=dev, device_id_type=MESH)

    loads = []

    def load(src, dst):
        copy = pltpu.make_async_copy(src, dst, lsem.at[len(loads)])
        copy.start()
        loads.append(copy)
        return copy

    index_loads = [
        load(owner_one_ref, own_one), load(slot_one_ref, slo_one),
        load(owner_two_ref, own_two), load(slot_two_ref, slo_two),
    ]
    cot_load = load(cot_ref, cot)
    w_one_load = load(w_one_ref, w_full.at[pl.ds(0, 128)])
    own_load = load(feat_ref.at[f], slab.at[0])
    small_loads = [load(w_two_ref, w_two), load(b_one_ref, b_one), load(b_two_ref, b_two)]

    pl.semaphore_wait(barrier, len(partners))

    low, high = n % SIDE, n // SIDE
    w_piece = w_one_ref.at[pl.ds(pl.multiple_of(high * 32, 32), 32),
                           pl.ds(pl.multiple_of(low * 128, 128), 128)]
    w_copies = [send(w_piece, w_parts.at[dz - 1, u, v], feat_dev(dz, 0)) for dz in others]
    slab_at = group(7 * chunks)

    def slab_copy(c, i):
        dev = feat_dev(*slots[i])
        return describe(slab_at + c * 7 + i - 1, feat_ref.at[dev[0], tile(c)],
                        slab.at[i, tile(c)], dev)

    def send_chunk(c, carry):
        for i in (4, 5, 2, 3, 6, 7, 1):
            slab_copy(c, i).start()
        return carry

    send_chunk(0, 0)
    w_pairs = [send(w_one_ref, w_full.at[pl.ds(128, 128)], feat_dev(0, 1))]

    for copy in index_loads:
        copy.wait()

    def ask_line(e, carry):
        for own, slo, lower in ((own_one, slo_one, 0), (own_two, slo_two, rows_two)):
            owner, slot = own[...], slo[...]
            found = []
            for d in range(SIDE):
                at = node_at(core, (u - d + SIDE) % SIDE, (v + e) % SIDE)
                found.append(jnp.max(jnp.where(owner == at, slot, -1), axis=0, keepdims=True))
            found.append(jnp.full((8 - SIDE, own.shape[1]), -1, I32))
            asks_out[e, :, lower:lower + own.shape[1]] = jnp.concatenate(found, axis=0)
        return carry

    lax.fori_loop(0, SIDE, ask_line, 0)
    cot_load.wait()
    msg_two[0] = (cot[...] / FAN).astype(BF)

    ask_copies = [send(asks_out.at[e], asks.at[e], v_dev(e)) for e in range(1, SIDE)]
    msg_two_copies = [send(msg_two.at[0], msg_two.at[e], v_dev(e)) for e in range(1, SIDE)]
    send_chunk(1, 0)

    arrived(w_copies)
    mine = w_parts.at[:, u, v]
    along_u = [send(mine, mine, u_dev(d)) for d in range(1, SIDE)]
    lax.fori_loop(2, chunks, send_chunk, 0)
    asks[0] = asks_out[0]
    arrived(ask_copies)

    def turn(e, carry):
        asks_col[e] = jnp.transpose(asks[e].astype(F32)).astype(I32)
        return carry

    lax.fori_loop(0, SIDE, turn, 0)
    arrived(along_u)
    mine = w_parts.at[:, :, v]
    along_v = [send(mine, mine, v_dev(e)) for e in range(1, SIDE)]

    def clear(j, carry):
        ysum[j] = jnp.zeros((rows_two, 256), F32)
        return carry

    lax.fori_loop(0, SIDE, clear, 0)
    bias[...] = jnp.zeros((1, 256), F32)

    arrived(msg_two_copies)
    back_two_at = group(3)

    def back_two(d):
        return describe(back_two_at + d - 1, gsend_two.at[d - 1], grecv_two.at[d - 1], u_dev(-d))

    def back_two_step(j, carry):
        d = (j + 1) % SIDE
        ids = lax.broadcasted_iota(I32, (rows_two, rows_three), 0)
        picks = jnp.concatenate(
            [(ids == asks[e, pl.ds(d, 1), rows_two:]).astype(BF) for e in range(SIDE)], axis=1
        )
        value = dot(picks, jnp.concatenate([msg_two[e] for e in range(SIDE)], axis=0))

        @pl.when(d > 0)
        def _():
            gsend_two[d - 1] = value.astype(BF)
            back_two(d).start()

        @pl.when(d == 0)
        def _():
            gsum_two[...] = value

        return carry

    lax.fori_loop(0, SIDE, back_two_step, 0)

    arrived(along_v)
    w_one_load.wait()

    for dz in range(1, SIDE):
        for r in range(4):
            for q in range(4):
                a, b = place(r, q)
                w_full[dz * 256 + r * 32:dz * 256 + r * 32 + 32, q * 128:q * 128 + 128] = (
                    w_parts[dz - 1, a, b]
                )
        w_pairs.append(send(w_full.at[pl.ds(dz * 256, 128)],
                            w_full.at[pl.ds(dz * 256 + 128, 128)], feat_dev(0, 1)))
    arrived(w_pairs)
    own_load.wait()

    table_at = group(3 * chunks)
    y_at = group(3 * tiles)

    def table_copy(c, d):
        return describe(table_at + c * 3 + d - 1, table.at[0, tile(c)], table.at[d, tile(c)],
                        u_dev(d))

    def y_copy(e, h):
        return describe(y_at + h * 3 + e - 1, ysend.at[e - 1, tile(h)], yrecv.at[e - 1, tile(h)],
                        v_dev(-e))

    def chunk_step(c, carry):
        @pl.when(c < chunks)
        def _():
            arrived([slab_copy(c, i) for i in range(1, FEATS)])
            block = jnp.concatenate([slab[i, tile(c)] for i in range(FEATS)], axis=1)
            table[0, tile(c)] = dot(block, w_full[:, 256:]).astype(BF)
            for d in others:
                table_copy(c, d).start()

            @pl.when(c < tiles)
            def _():
                self_one[tile(c)] = dot(block, w_full[:, :256])

        @pl.when(c > 1)
        def _():
            b = c - 2
            arrived([table_copy(b, d) for d in others])

            def sum_step(h, inner):
                ids = lax.broadcasted_iota(I32, (PART, PART), 1) + b * PART
                rows = jnp.concatenate([table[d, tile(b)] for d in range(SIDE)], axis=0)
                for e in (2, 1, 3, 0):
                    picks = jnp.concatenate(
                        [(ids == asks_col[e, tile(h), d:d + 1]).astype(BF)
                         for d in range(SIDE)], axis=1
                    )
                    ysum[e, tile(h)] += dot(picks, rows)

                @pl.when(b == chunks - 1)
                def _():
                    for e in others:
                        ysend[e - 1, tile(h)] = ysum[e, tile(h)].astype(BF)
                        y_copy(e, h).start()

                return inner

            lax.fori_loop(0, tiles, sum_step, 0)

        return carry

    lax.fori_loop(0, chunks + 2, chunk_step, 0)

    for copy in small_loads:
        copy.wait()
    arrived([back_two(d) for d in others])
    gproj_two[:rows_three, :256] = cot[...].astype(BF)
    gproj_two[rows_three:, :256] = jnp.zeros((rows_two - rows_three, 256), BF)

    total = add_up(gsum_two[...], [grecv_two[d] for d in range(SIDE - 1)])
    gproj_two[:, 256:] = total.astype(BF)
    ghid[...] = dot(gproj_two[...], w_two[...], ((1,), (1,)))

    msg_at = group(3 * tiles)

    def msg_copy(h, e):
        return describe(msg_at + h * 3 + e - 1, msg_one.at[0, tile(h)], msg_one.at[e, tile(h)],
                        v_dev(e))

    def act_step(h, carry):
        arrived([y_copy(e, h) for e in others])

        def rows_step(t, inner):
            rows = pl.ds(pl.multiple_of(h * PART + t * 128, 128), 128)
            total = add_up(ysum[0, rows], [yrecv[e, rows] for e in range(SIDE - 1)])
            linear = self_one[rows] + b_one[...] + total / FAN
            logistic = 1.0 / (1.0 + jnp.exp(-linear))
            grad = ghid[rows] * (logistic * (1.0 + linear * (1.0 - logistic)))
            msg_one[0, rows] = (grad / FAN).astype(BF)
            glin[rows] = grad.astype(BF)
            hidden[rows] = (linear * logistic).astype(BF)
            bias[...] += jnp.sum(grad, axis=0, keepdims=True)
            return inner

        lax.fori_loop(0, PART // 128, rows_step, 0)
        for e in others:
            msg_copy(h, e).start()
        return carry

    lax.fori_loop(0, tiles, act_step, 0)

    value = dot(hidden[...], gproj_two[...], ((0,), (0,))).astype(BF)
    for r in range(4):
        for q in range(4):
            a, b = place(r, q)
            two_out[a, b, :64] = value[r * 64:r * 64 + 64, q * 128:q * 128 + 128]
            two_out[a, b, 64:] = jnp.zeros((16, 128), BF)
    for q in range(2):
        a, b = place(0, q)
        two_out[a, b, 64:] = jnp.broadcast_to(bias[:, q * 128:q * 128 + 128], (16, 128)).astype(BF)
    two_u_copies = [
        send(two_out.at[(u + d) % SIDE], two_in.at[d - 1], u_dev(d)) for d in others
    ]

    proj = dot(hidden[...], w_two[...])
    table_two[0] = proj[:, 256:].astype(BF)
    self_two[...] = proj[:rows_three, :256]
    table_two_copies = [send(table_two.at[0], table_two.at[d], u_dev(d)) for d in others]

    two_v_at = group(3)
    back_at = group(3)

    def two_v_copy(e):
        return describe(two_v_at + e - 1, two_mid.at[(v + e) % SIDE], two_v.at[e - 1], v_dev(e))

    def back_copy(d):
        return describe(back_at + d - 1, gsend.at[d - 1], grecv.at[d - 1], u_dev(-d))

    def line_grads(e, d):
        ids = lax.broadcasted_iota(I32, (rows_one, rows_two), 0)
        return dot((ids == asks[e, pl.ds(d, 1), :rows_two]).astype(BF), msg_one[e])

    def own_step(d, carry):
        gsum[d] = line_grads(0, d)
        return carry

    lax.fori_loop(0, SIDE, own_step, 0)
    arrived([msg_copy(h, e) for h in range(tiles) for e in others])

    def back_step(j, carry):
        d = (j + 1) % SIDE
        value = gsum[d]
        for e in range(1, SIDE):
            value += line_grads(e, d)

        @pl.when(d > 0)
        def _():
            gsend[d - 1] = value.astype(BF)
            back_copy(d).start()

        @pl.when(d == 0)
        def _():
            gsum[0] = value

        return carry

    lax.fori_loop(0, SIDE, back_step, 0)
    arrived(two_u_copies)
    for b in range(SIDE):
        two_mid[b] = add_up(
            two_out[u, b].astype(F32), [two_in[d, b] for d in range(SIDE - 1)]
        ).astype(BF)
    for e in others:
        two_v_copy(e).start()

    arrived(table_two_copies)
    y_two_at = group(3)

    def y_two_copy(e):
        return describe(y_two_at + e - 1, ysend_two.at[e - 1], yrecv_two.at[e - 1], v_dev(-e))

    def y_two_step(j, carry):
        e = (j + 1) % SIDE
        ids = lax.broadcasted_iota(I32, (rows_three, rows_two), 1)
        picks = jnp.concatenate(
            [(ids == asks_col[e, rows_two:, d:d + 1]).astype(BF) for d in range(SIDE)], axis=1
        )
        value = dot(picks, jnp.concatenate([table_two[d] for d in range(SIDE)], axis=0))

        @pl.when(e > 0)
        def _():
            ysend_two[e - 1] = value.astype(BF)
            y_two_copy(e).start()

        @pl.when(e == 0)
        def _():
            ysum_two[...] = value

        return carry

    lax.fori_loop(0, SIDE, y_two_step, 0)

    arrived([two_v_copy(e) for e in others])
    two_z[0] = add_up(two_mid[v].astype(F32), [two_v[e] for e in range(SIDE - 1)]).astype(BF)
    two_z_copies = [
        send(two_z.at[0], two_z.at[i], feat_dev(*slots[i])) for i in range(1, FEATS)
    ]

    def outer(dc, grad):
        block = jnp.concatenate([slab[2 * dz + dc] for dz in range(4)], axis=1)
        return dot(block[:grad.shape[0]], grad[...], ((0,), (0,)))

    pair_out[0] = outer(1, glin).astype(BF)
    wall[0] = outer(0, glin)
    pairs = [send(pair_out.at[0], pair_in.at[0], feat_dev(0, 1))]
    arrived([y_two_copy(e) for e in others])

    def out_step(t, carry):
        total = add_up(ysum_two[tile(t, 64)], [yrecv_two[e, tile(t, 64)] for e in range(3)])
        out_ref[tile(t, 64)] = (self_two[tile(t, 64)] + b_two[...] + total / FAN).astype(BF)
        return carry

    lax.fori_loop(0, rows_three // 64, out_step, 0)

    arrived(two_z_copies)
    two_all[u, v] = add_up(
        two_z[0].astype(F32), [two_z[i] for i in range(1, FEATS)]
    ).astype(BF)
    two_copies = [send(two_all.at[u, v], two_all.at[u, v], v_dev(e)) for e in others]
    arrived([back_copy(d) for d in others])
    gtab[...] = add_up(gsum[0], [grecv[d] for d in range(SIDE - 1)]).astype(BF)
    pair_out[1] = outer(1, gtab).astype(BF)
    pairs.append(send(pair_out.at[1], pair_in.at[1], feat_dev(0, 1)))
    wall[1] = outer(0, gtab)
    arrived(two_copies)
    two_copies = [send(two_all.at[u], two_all.at[u], u_dev(d)) for d in others]
    arrived(pairs)
    for k in range(2):
        value = (wall[k] + pair_in[k].astype(F32)).astype(BF)
        for dz in range(4):
            for r in range(4):
                for q in range(2):
                    a, b = place(r, 2 * k + q)
                    w_out[a, b, dz * 32:dz * 32 + 32] = value[
                        dz * 128 + r * 32:dz * 128 + r * 32 + 32, q * 128:q * 128 + 128]

    sums = [send(w_out.at[(u + d) % SIDE], w_in.at[d - 1], u_dev(d)) for d in others]
    arrived(two_copies)

    def lay_two(r, carry):
        for q in range(4):
            a, b = place(r, q)
            gw_two_ref[tile(r, 64), q * 128:q * 128 + 128] = two_all[a, b, :64].astype(F32)
        return carry

    lax.fori_loop(0, 4, lay_two, 0)
    for q in range(2):
        a, b = place(0, q)
        gb_ref[:, q * 128:q * 128 + 128] = two_all[a, b, 64:].astype(F32)[:1]
    arrived(sums)

    def mid_step(b, carry):
        w_mid[b] = add_up(
            w_out[u, b].astype(F32), [w_in[d, b] for d in range(SIDE - 1)]
        ).astype(BF)
        return carry

    lax.fori_loop(0, SIDE, mid_step, 0)
    sums = [send(w_mid.at[(v + e) % SIDE], v_in.at[e - 1], v_dev(e)) for e in others]
    arrived(sums)
    z_out[...] = add_up(w_mid[v].astype(F32), [v_in[e] for e in range(SIDE - 1)]).astype(BF)
    sums = [
        send(z_out.at[pl.ds(dz * 32, 32)], z_in.at[dz - 1], feat_dev(-dz, 0)) for dz in others
    ]
    arrived(sums)
    piece_all[u, v] = add_up(
        z_out[:32].astype(F32), [z_in[dz] for dz in range(3)]
    ).astype(BF)
    sums = [send(piece_all.at[u, v], piece_all.at[u, v], v_dev(e)) for e in others]
    arrived(sums)
    sums = [send(piece_all.at[u], piece_all.at[u], u_dev(d)) for d in others]
    arrived(sums)

    def lay_one(r, carry):
        for q in range(4):
            a, b = place(r, q)
            gw_one_ref[tile(r, 32), q * 128:q * 128 + 128] = piece_all[a, b].astype(F32)
        return carry

    lax.fori_loop(0, 4, lay_one, 0)
    for copy in groups:
        copy.wait_send()

    def sent(c, carry):
        for i in range(1, FEATS):
            slab_copy(c, i).wait_send()
        for d in others:
            table_copy(c, d).wait_send()
        return carry

    lax.fori_loop(0, chunks, sent, 0)

    def sent_tiles(t, carry):
        for d in others:
            y_copy(d, t).wait_send()
            msg_copy(t, d).wait_send()
        return carry

    lax.fori_loop(0, tiles, sent_tiles, 0)
    for e in others:
        two_v_copy(e).wait_send()
        y_two_copy(e).wait_send()
        back_two(e).wait_send()
        back_copy(e).wait_send()


def store_kernel(*refs):
    src, dst, held, sem = refs[:4], refs[4:8], refs[8:12], refs[12]
    reads = [pltpu.make_async_copy(src[i], held[i], sem.at[i]) for i in range(4)]
    writes = [pltpu.make_async_copy(held[i], dst[i], sem.at[4 + i]) for i in range(4)]
    for copy in reads:
        copy.start()
    for read, write in zip(reads, writes):
        read.wait()
        write.start()
    for copy in writes:
        copy.wait()


N_COPIES = 160


def on_device(
    features, w_one, w_two, b_one, b_two, owner_one, slot_one, owner_two, slot_two, cotangent
):
    r1, r2, r3 = features.shape[1], owner_one.shape[1], owner_two.shape[1]
    vm = pl.BlockSpec(memory_space=pltpu.VMEM)
    scratch = [
        ((FEATS, r1, 128), BF), ((3, 4, 4, 32, 128), BF), ((1024, 512), BF),
        ((256, 512), BF), ((1, 256), F32), ((1, 256), F32),
        ((FAN, r2), I32), ((FAN, r2), I32), ((FAN, r3), I32), ((FAN, r3), I32),
        ((r3, 256), F32), ((SIDE, 8, r2 + r3), I32),
        ((SIDE, 8, r2 + r3), I32), ((SIDE, r2 + r3, 8), I32),
        ((SIDE, r3, 256), BF), ((r2, 256), F32), ((3, r2, 256), BF), ((3, r2, 256), BF),
        ((r2, 512), BF), ((r2, 256), F32), ((SIDE, r1, 256), BF), ((r2, 256), F32),
        ((SIDE, r2, 256), F32), ((3, r2, 256), BF), ((3, r2, 256), BF), ((r2, 256), BF),
        ((r3, 256), F32), ((SIDE, r2, 256), BF), ((r3, 256), F32), ((3, r3, 256), BF),
        ((3, r3, 256), BF), ((r2, 256), BF), ((SIDE, r2, 256), BF), ((SIDE, r1, 256), F32),
        ((3, r1, 256), BF), ((3, r1, 256), BF), ((1, 256), F32),
        ((4, 4, 80, 128), BF), ((3, 4, 80, 128), BF), ((4, 80, 128), BF), ((3, 80, 128), BF),
        ((FEATS, 80, 128), BF), ((4, 4, 80, 128), BF),
        ((2, 512, 256), F32), ((r1, 256), BF), ((2, 512, 256), BF), ((2, 512, 256), BF),
        ((4, 4, 128, 128), BF), ((3, 4, 128, 128), BF),
        ((4, 128, 128), BF), ((3, 128, 128), BF), ((128, 128), BF), ((3, 32, 128), BF),
        ((4, 4, 32, 128), BF),
    ]
    outs = pl.pallas_call(
        step_kernel,
        out_shape=[
            jax.ShapeDtypeStruct((r3, 256), BF), jax.ShapeDtypeStruct((128, 512), F32),
            jax.ShapeDtypeStruct((256, 512), F32), jax.ShapeDtypeStruct((1, 256), F32),
        ],
        in_specs=[pl.BlockSpec(memory_space=pl.ANY)] * 10,
        out_specs=[vm] * 4,
        scratch_shapes=[pltpu.VMEM(s, t) for s, t in scratch] + [
            pltpu.SemaphoreType.DMA((N_COPIES,)), pltpu.SemaphoreType.DMA((N_COPIES,)),
            pltpu.SemaphoreType.DMA((10,)),
        ],
        compiler_params=pltpu.CompilerParams(
            collective_id=0, has_side_effects=True, vmem_limit_bytes=56 * 2**20
        ),
        cost_estimate=pl.CostEstimate(
            flops=14 * 10**9, bytes_accessed=8 * 2**20, transcendentals=512 * 256
        ),
        name="sage_step",
    )(features, w_one, w_two, b_one[None], b_two[None], owner_one[0].T, slot_one[0].T,
      owner_two[0].T, slot_two[0].T, cotangent[0])
    anywhere = pl.BlockSpec(memory_space=pl.ANY)
    layer_out, gw_one, gw_two, gb = pl.pallas_call(
        store_kernel,
        out_shape=[jax.ShapeDtypeStruct(o.shape, o.dtype) for o in outs],
        in_specs=[anywhere] * 4,
        out_specs=[anywhere] * 4,
        scratch_shapes=[pltpu.VMEM(o.shape, o.dtype) for o in outs]
        + [pltpu.SemaphoreType.DMA((8,))],
        compiler_params=pltpu.CompilerParams(vmem_limit_bytes=56 * 2**20),
        name="store_results",
    )(*outs)
    return layer_out[None], gw_one, gw_two, gb[0]


def solution(mesh):
    placed = (
        P(None, "node", "feat"),
        P("feat", None),
        P(),
        P(),
        P(),
        P("feat", "node", None),
        P("feat", "node", None),
        P("feat", "node", None),
        P("feat", "node", None),
        P("feat", "node", None),
    )
    return jax.shard_map(
        on_device,
        mesh=mesh,
        in_specs=placed,
        out_specs=(P("feat", "node", None), P("feat", None), P(), P()),
        check_vma=False,
    )
```

```python
import jax
import jax.numpy as jnp
from jax import lax
from jax.experimental import pallas as pl
from jax.experimental.pallas import tpu as pltpu
from jax.sharding import PartitionSpec as P

MESH = pl.DeviceIdType.MESH
PART = 256
FEATS = 8
SIDE = 4
FAN = 8
BF = jnp.bfloat16
F32 = jnp.float32
I32 = jnp.int32


def line_place(core, node):
    low, high = node % SIDE, node // SIDE
    return (1 - core) * low + core * high, (1 - core) * high + core * low


def node_at(core, u, v):
    return (1 - core) * (v * SIDE + u) + core * (u * SIDE + v)


def dot(a, b, dims=((1,), (0,))):
    return lax.dot_general(a, b, (dims, ((), ())), preferred_element_type=F32)


def add_up(first, others):
    total = first
    for other in others:
        total += other.astype(F32)
    return total


def step_kernel(
    feat_ref, w_one_ref, w_two_ref, b_one_ref, b_two_ref, owner_one_ref, slot_one_ref,
    owner_two_ref, slot_two_ref, cot_ref,
    out_ref, gw_one_ref, gw_two_ref, gb_ref,
    slab, w_parts, w_full, w_two, b_one, b_two, own_one, slo_one, own_two, slo_two, cot,
    asks_out, asks, asks_col, msg_two, gsum_two, gsend_two, grecv_two,
    gproj_two, ghid, table, self_one, ysum, ysend, yrecv, hidden, self_two,
    table_two, ysum_two, ysend_two, yrecv_two, glin, msg_one, gsum, gsend, grecv, bias,
    two_out, two_in, two_mid, two_v, two_z, two_all,
    wall, gtab, pair_out, pair_in, w_out, w_in, w_mid, v_in, z_out, z_in, piece_all,
    ssem, rsem, lsem,
):
    f, n = lax.axis_index("feat"), lax.axis_index("node")
    z, core = f // 2, f % 2
    u, v = line_place(core, n)
    rows_one = slab.shape[1]
    rows_two = own_one.shape[1]
    rows_three = own_two.shape[1]
    chunks = rows_one // PART
    tiles = rows_two // PART
    slots = [(dz, dc) for dz in range(4) for dc in range(2)]
    others = (2, 1, 3)

    def feat_dev(dz, dc):
        return (((z + dz + 4) % 4) * 2 + (core + dc) % 2, n)

    def u_dev(d):
        return (f, node_at(core, (u + d + SIDE) % SIDE, v))

    def v_dev(e):
        return (f, node_at(core, u, (v + e + SIDE) % SIDE))

    def place(r, q):
        return (1 - core) * q + core * r, (1 - core) * r + core * q

    def tile(j, size=PART):
        return pl.ds(pl.multiple_of(j * size, size), size)

    used = [0]
    groups = []

    def group(count):
        first = used[0]
        used[0] += count
        return first

    def describe(k, src, dst, dev):
        return pltpu.make_async_remote_copy(
            src_ref=src, dst_ref=dst, send_sem=ssem.at[k], recv_sem=rsem.at[k],
            device_id=dev, device_id_type=MESH,
        )

    def send(src, dst, dev):
        copy = describe(group(1), src, dst, dev)
        copy.start()
        groups.append(copy)
        return copy

    def arrived(copies):
        for copy in copies:
            copy.wait_recv()

    barrier = pltpu.get_barrier_semaphore()
    partners = [feat_dev(*s) for s in slots[1:]]
    partners += [u_dev(d) for d in range(1, SIDE)] + [v_dev(e) for e in range(1, SIDE)]
    for dev in partners:
        pl.semaphore_signal(barrier, inc=1, device_id=dev, device_id_type=MESH)

    loads = []

    def load(src, dst):
        copy = pltpu.make_async_copy(src, dst, lsem.at[len(loads)])
        copy.start()
        loads.append(copy)
        return copy

    index_loads = [
        load(owner_one_ref, own_one), load(slot_one_ref, slo_one),
        load(owner_two_ref, own_two), load(slot_two_ref, slo_two),
    ]
    cot_load = load(cot_ref, cot)
    w_one_load = load(w_one_ref, w_full.at[pl.ds(0, 128)])
    own_load = load(feat_ref.at[f], slab.at[0])
    small_loads = [load(w_two_ref, w_two), load(b_one_ref, b_one), load(b_two_ref, b_two)]

    pl.semaphore_wait(barrier, len(partners))

    low, high = n % SIDE, n // SIDE
    w_piece = w_one_ref.at[pl.ds(pl.multiple_of(high * 32, 32), 32),
                           pl.ds(pl.multiple_of(low * 128, 128), 128)]
    w_copies = [send(w_piece, w_parts.at[dz - 1, u, v], feat_dev(dz, 0)) for dz in others]
    slab_at = group(7 * chunks)

    def slab_copy(c, i):
        dev = feat_dev(*slots[i])
        return describe(slab_at + c * 7 + i - 1, feat_ref.at[dev[0], tile(c)],
                        slab.at[i, tile(c)], dev)

    def send_chunk(c, carry):
        for i in (4, 5, 2, 3, 6, 7, 1):
            slab_copy(c, i).start()
        return carry

    send_chunk(0, 0)
    w_pairs = [send(w_one_ref, w_full.at[pl.ds(128, 128)], feat_dev(0, 1))]

    for copy in index_loads:
        copy.wait()

    def ask_line(e, carry):
        for own, slo, lower in ((own_one, slo_one, 0), (own_two, slo_two, rows_two)):
            owner, slot = own[...], slo[...]
            found = []
            for d in range(SIDE):
                at = node_at(core, (u - d + SIDE) % SIDE, (v + e) % SIDE)
                found.append(jnp.max(jnp.where(owner == at, slot, -1), axis=0, keepdims=True))
            found.append(jnp.full((8 - SIDE, own.shape[1]), -1, I32))
            asks_out[e, :, lower:lower + own.shape[1]] = jnp.concatenate(found, axis=0)
        return carry

    lax.fori_loop(0, SIDE, ask_line, 0)
    cot_load.wait()
    msg_two[0] = (cot[...] / FAN).astype(BF)

    ask_copies = [send(asks_out.at[e], asks.at[e], v_dev(e)) for e in range(1, SIDE)]
    msg_two_copies = [send(msg_two.at[0], msg_two.at[e], v_dev(e)) for e in range(1, SIDE)]
    send_chunk(1, 0)

    arrived(w_copies)
    mine = w_parts.at[:, u, v]
    along_u = [send(mine, mine, u_dev(d)) for d in range(1, SIDE)]
    lax.fori_loop(2, chunks, send_chunk, 0)
    asks[0] = asks_out[0]
    arrived(ask_copies)

    def turn(e, carry):
        asks_col[e] = jnp.transpose(asks[e].astype(F32)).astype(I32)
        return carry

    lax.fori_loop(0, SIDE, turn, 0)
    arrived(along_u)
    mine = w_parts.at[:, :, v]
    along_v = [send(mine, mine, v_dev(e)) for e in range(1, SIDE)]

    def clear(j, carry):
        ysum[j] = jnp.zeros((rows_two, 256), F32)
        return carry

    lax.fori_loop(0, SIDE, clear, 0)
    bias[...] = jnp.zeros((1, 256), F32)

    arrived(msg_two_copies)
    back_two_at = group(3)

    def back_two(d):
        return describe(back_two_at + d - 1, gsend_two.at[d - 1], grecv_two.at[d - 1], u_dev(-d))

    def back_two_step(j, carry):
        d = (j + 1) % SIDE
        ids = lax.broadcasted_iota(I32, (rows_two, rows_three), 0)
        picks = jnp.concatenate(
            [(ids == asks[e, pl.ds(d, 1), rows_two:]).astype(BF) for e in range(SIDE)], axis=1
        )
        value = dot(picks, jnp.concatenate([msg_two[e] for e in range(SIDE)], axis=0))

        @pl.when(d > 0)
        def _():
            gsend_two[d - 1] = value.astype(BF)
            back_two(d).start()

        @pl.when(d == 0)
        def _():
            gsum_two[...] = value

        return carry

    lax.fori_loop(0, SIDE, back_two_step, 0)

    arrived(along_v)
    w_one_load.wait()

    for dz in range(1, SIDE):
        for r in range(4):
            for q in range(4):
                a, b = place(r, q)
                w_full[dz * 256 + r * 32:dz * 256 + r * 32 + 32, q * 128:q * 128 + 128] = (
                    w_parts[dz - 1, a, b]
                )
        w_pairs.append(send(w_full.at[pl.ds(dz * 256, 128)],
                            w_full.at[pl.ds(dz * 256 + 128, 128)], feat_dev(0, 1)))
    arrived(w_pairs)
    own_load.wait()

    table_at = group(3 * chunks)
    y_at = group(3 * tiles)

    def table_copy(c, d):
        return describe(table_at + c * 3 + d - 1, table.at[0, tile(c)], table.at[d, tile(c)],
                        u_dev(d))

    def y_copy(e, h):
        return describe(y_at + h * 3 + e - 1, ysend.at[e - 1, tile(h)], yrecv.at[e - 1, tile(h)],
                        v_dev(-e))

    def chunk_step(c, carry):
        @pl.when(c < chunks)
        def _():
            arrived([slab_copy(c, i) for i in range(1, FEATS)])
            block = jnp.concatenate([slab[i, tile(c)] for i in range(FEATS)], axis=1)
            table[0, tile(c)] = dot(block, w_full[:, 256:]).astype(BF)
            for d in others:
                table_copy(c, d).start()

            @pl.when(c < tiles)
            def _():
                self_one[tile(c)] = dot(block, w_full[:, :256])

        @pl.when(c > 1)
        def _():
            b = c - 2
            arrived([table_copy(b, d) for d in others])

            def sum_step(h, inner):
                ids = lax.broadcasted_iota(I32, (PART, PART), 1) + b * PART
                rows = jnp.concatenate([table[d, tile(b)] for d in range(SIDE)], axis=0)
                for e in (2, 1, 3, 0):
                    picks = jnp.concatenate(
                        [(ids == asks_col[e, tile(h), d:d + 1]).astype(BF)
                         for d in range(SIDE)], axis=1
                    )
                    ysum[e, tile(h)] += dot(picks, rows)

                @pl.when(b == chunks - 1)
                def _():
                    for e in others:
                        ysend[e - 1, tile(h)] = ysum[e, tile(h)].astype(BF)
                        y_copy(e, h).start()

                return inner

            lax.fori_loop(0, tiles, sum_step, 0)

        return carry

    lax.fori_loop(0, chunks + 2, chunk_step, 0)

    for copy in small_loads:
        copy.wait()
    arrived([back_two(d) for d in others])
    gproj_two[:rows_three, :256] = cot[...].astype(BF)
    gproj_two[rows_three:, :256] = jnp.zeros((rows_two - rows_three, 256), BF)

    total = add_up(gsum_two[...], [grecv_two[d] for d in range(SIDE - 1)])
    gproj_two[:, 256:] = total.astype(BF)
    ghid[...] = dot(gproj_two[...], w_two[...], ((1,), (1,)))

    msg_at = group(3 * tiles)

    def msg_copy(h, e):
        return describe(msg_at + h * 3 + e - 1, msg_one.at[0, tile(h)], msg_one.at[e, tile(h)],
                        v_dev(e))

    def act_step(h, carry):
        arrived([y_copy(e, h) for e in others])

        def rows_step(t, inner):
            rows = pl.ds(pl.multiple_of(h * PART + t * 128, 128), 128)
            total = add_up(ysum[0, rows], [yrecv[e, rows] for e in range(SIDE - 1)])
            linear = self_one[rows] + b_one[...] + total / FAN
            logistic = 1.0 / (1.0 + jnp.exp(-linear))
            grad = ghid[rows] * (logistic * (1.0 + linear * (1.0 - logistic)))
            msg_one[0, rows] = (grad / FAN).astype(BF)
            glin[rows] = grad.astype(BF)
            hidden[rows] = (linear * logistic).astype(BF)
            bias[...] += jnp.sum(grad, axis=0, keepdims=True)
            return inner

        lax.fori_loop(0, PART // 128, rows_step, 0)
        for e in others:
            msg_copy(h, e).start()
        return carry

    lax.fori_loop(0, tiles, act_step, 0)

    value = dot(hidden[...], gproj_two[...], ((0,), (0,))).astype(BF)
    for r in range(4):
        for q in range(4):
            a, b = place(r, q)
            two_out[a, b, :64] = value[r * 64:r * 64 + 64, q * 128:q * 128 + 128]
            two_out[a, b, 64:] = jnp.zeros((16, 128), BF)
    for q in range(2):
        a, b = place(0, q)
        two_out[a, b, 64:] = jnp.broadcast_to(bias[:, q * 128:q * 128 + 128], (16, 128)).astype(BF)
    two_u_copies = [
        send(two_out.at[(u + d) % SIDE], two_in.at[d - 1], u_dev(d)) for d in others
    ]

    proj = dot(hidden[...], w_two[...])
    table_two[0] = proj[:, 256:].astype(BF)
    self_two[...] = proj[:rows_three, :256]

    two_v_at = group(3)
    back_at = group(3)

    def two_v_copy(e):
        return describe(two_v_at + e - 1, two_mid.at[(v + e) % SIDE], two_v.at[e - 1], v_dev(e))

    def back_copy(d):
        return describe(back_at + d - 1, gsend.at[d - 1], grecv.at[d - 1], u_dev(-d))

    def line_grads(e, d):
        ids = lax.broadcasted_iota(I32, (rows_one, rows_two), 0)
        return dot((ids == asks[e, pl.ds(d, 1), :rows_two]).astype(BF), msg_one[e])

    def own_step(d, carry):
        gsum[d] = line_grads(0, d)
        return carry

    lax.fori_loop(0, SIDE, own_step, 0)
    arrived([msg_copy(h, e) for h in range(tiles) for e in others])

    def back_step(j, carry):
        d = (j + 1) % SIDE
        value = gsum[d]
        for e in range(1, SIDE):
            value += line_grads(e, d)

        @pl.when(d > 0)
        def _():
            gsend[d - 1] = value.astype(BF)
            back_copy(d).start()

        @pl.when(d == 0)
        def _():
            gsum[0] = value

        return carry

    lax.fori_loop(0, SIDE, back_step, 0)
    arrived(two_u_copies)
    for b in range(SIDE):
        two_mid[b] = add_up(
            two_out[u, b].astype(F32), [two_in[d, b] for d in range(SIDE - 1)]
        ).astype(BF)
    for e in others:
        two_v_copy(e).start()

    def outer(dc, grad):
        block = jnp.concatenate([slab[2 * dz + dc] for dz in range(4)], axis=1)
        return dot(block[:grad.shape[0]], grad[...], ((0,), (0,)))

    pair_out[0] = outer(1, glin).astype(BF)
    wall[0] = outer(0, glin)
    pairs = [send(pair_out.at[0], pair_in.at[0], feat_dev(0, 1))]
    arrived([two_v_copy(e) for e in others])
    two_z[0] = add_up(two_mid[v].astype(F32), [two_v[e] for e in range(SIDE - 1)]).astype(BF)
    two_z_copies = [
        send(two_z.at[0], two_z.at[i], feat_dev(*slots[i])) for i in range(1, FEATS)
    ]
    arrived(two_z_copies)
    two_all[u, v] = add_up(
        two_z[0].astype(F32), [two_z[i] for i in range(1, FEATS)]
    ).astype(BF)
    two_copies = [send(two_all.at[u, v], two_all.at[u, v], v_dev(e)) for e in others]
    arrived([back_copy(d) for d in others])
    table_two_copies = [send(table_two.at[0], table_two.at[d], u_dev(d)) for d in others]
    gtab[...] = add_up(gsum[0], [grecv[d] for d in range(SIDE - 1)]).astype(BF)
    pair_out[1] = outer(1, gtab).astype(BF)
    pairs.append(send(pair_out.at[1], pair_in.at[1], feat_dev(0, 1)))
    wall[1] = outer(0, gtab)
    arrived(two_copies)
    two_copies = [send(two_all.at[u], two_all.at[u], u_dev(d)) for d in others]
    arrived(pairs)
    for k in range(2):
        value = (wall[k] + pair_in[k].astype(F32)).astype(BF)
        for dz in range(4):
            for r in range(4):
                for q in range(2):
                    a, b = place(r, 2 * k + q)
                    w_out[a, b, dz * 32:dz * 32 + 32] = value[
                        dz * 128 + r * 32:dz * 128 + r * 32 + 32, q * 128:q * 128 + 128]

    sums = [send(w_out.at[(u + d) % SIDE], w_in.at[d - 1], u_dev(d)) for d in others]

    arrived(table_two_copies)
    y_two_at = group(3)

    def y_two_copy(e):
        return describe(y_two_at + e - 1, ysend_two.at[e - 1], yrecv_two.at[e - 1], v_dev(-e))

    def y_two_step(j, carry):
        e = (j + 1) % SIDE
        ids = lax.broadcasted_iota(I32, (rows_three, rows_two), 1)
        picks = jnp.concatenate(
            [(ids == asks_col[e, rows_two:, d:d + 1]).astype(BF) for d in range(SIDE)], axis=1
        )
        value = dot(picks, jnp.concatenate([table_two[d] for d in range(SIDE)], axis=0))

        @pl.when(e > 0)
        def _():
            ysend_two[e - 1] = value.astype(BF)
            y_two_copy(e).start()

        @pl.when(e == 0)
        def _():
            ysum_two[...] = value

        return carry

    lax.fori_loop(0, SIDE, y_two_step, 0)

    arrived(two_copies)

    def lay_two(r, carry):
        for q in range(4):
            a, b = place(r, q)
            gw_two_ref[tile(r, 64), q * 128:q * 128 + 128] = two_all[a, b, :64].astype(F32)
        return carry

    lax.fori_loop(0, 4, lay_two, 0)
    for q in range(2):
        a, b = place(0, q)
        gb_ref[:, q * 128:q * 128 + 128] = two_all[a, b, 64:].astype(F32)[:1]
    arrived(sums)

    def mid_step(b, carry):
        w_mid[b] = add_up(
            w_out[u, b].astype(F32), [w_in[d, b] for d in range(SIDE - 1)]
        ).astype(BF)
        return carry

    lax.fori_loop(0, SIDE, mid_step, 0)
    sums = [send(w_mid.at[(v + e) % SIDE], v_in.at[e - 1], v_dev(e)) for e in others]
    arrived(sums)
    z_out[...] = add_up(w_mid[v].astype(F32), [v_in[e] for e in range(SIDE - 1)]).astype(BF)
    sums = [
        send(z_out.at[pl.ds(dz * 32, 32)], z_in.at[dz - 1], feat_dev(-dz, 0)) for dz in others
    ]
    arrived([y_two_copy(e) for e in others])

    def out_step(t, carry):
        total = add_up(ysum_two[tile(t, 64)], [yrecv_two[e, tile(t, 64)] for e in range(3)])
        out_ref[tile(t, 64)] = (self_two[tile(t, 64)] + b_two[...] + total / FAN).astype(BF)
        return carry

    lax.fori_loop(0, rows_three // 64, out_step, 0)

    arrived(sums)
    piece_all[u, v] = add_up(
        z_out[:32].astype(F32), [z_in[dz] for dz in range(3)]
    ).astype(BF)
    sums = [send(piece_all.at[u, v], piece_all.at[u, v], v_dev(e)) for e in others]
    arrived(sums)
    sums = [send(piece_all.at[u], piece_all.at[u], u_dev(d)) for d in others]
    arrived(sums)

    def lay_one(r, carry):
        for q in range(4):
            a, b = place(r, q)
            gw_one_ref[tile(r, 32), q * 128:q * 128 + 128] = piece_all[a, b].astype(F32)
        return carry

    lax.fori_loop(0, 4, lay_one, 0)
    for copy in groups:
        copy.wait_send()

    def sent(c, carry):
        for i in range(1, FEATS):
            slab_copy(c, i).wait_send()
        for d in others:
            table_copy(c, d).wait_send()
        return carry

    lax.fori_loop(0, chunks, sent, 0)

    def sent_tiles(t, carry):
        for d in others:
            y_copy(d, t).wait_send()
            msg_copy(t, d).wait_send()
        return carry

    lax.fori_loop(0, tiles, sent_tiles, 0)
    for e in others:
        two_v_copy(e).wait_send()
        y_two_copy(e).wait_send()
        back_two(e).wait_send()
        back_copy(e).wait_send()


def store_kernel(*refs):
    src, dst, held, sem = refs[:4], refs[4:8], refs[8:12], refs[12]
    reads = [pltpu.make_async_copy(src[i], held[i], sem.at[i]) for i in range(4)]
    writes = [pltpu.make_async_copy(held[i], dst[i], sem.at[4 + i]) for i in range(4)]
    for copy in reads:
        copy.start()
    for read, write in zip(reads, writes):
        read.wait()
        write.start()
    for copy in writes:
        copy.wait()


N_COPIES = 160


def on_device(
    features, w_one, w_two, b_one, b_two, owner_one, slot_one, owner_two, slot_two, cotangent
):
    r1, r2, r3 = features.shape[1], owner_one.shape[1], owner_two.shape[1]
    vm = pl.BlockSpec(memory_space=pltpu.VMEM)
    scratch = [
        ((FEATS, r1, 128), BF), ((3, 4, 4, 32, 128), BF), ((1024, 512), BF),
        ((256, 512), BF), ((1, 256), F32), ((1, 256), F32),
        ((FAN, r2), I32), ((FAN, r2), I32), ((FAN, r3), I32), ((FAN, r3), I32),
        ((r3, 256), F32), ((SIDE, 8, r2 + r3), I32),
        ((SIDE, 8, r2 + r3), I32), ((SIDE, r2 + r3, 8), I32),
        ((SIDE, r3, 256), BF), ((r2, 256), F32), ((3, r2, 256), BF), ((3, r2, 256), BF),
        ((r2, 512), BF), ((r2, 256), F32), ((SIDE, r1, 256), BF), ((r2, 256), F32),
        ((SIDE, r2, 256), F32), ((3, r2, 256), BF), ((3, r2, 256), BF), ((r2, 256), BF),
        ((r3, 256), F32), ((SIDE, r2, 256), BF), ((r3, 256), F32), ((3, r3, 256), BF),
        ((3, r3, 256), BF), ((r2, 256), BF), ((SIDE, r2, 256), BF), ((SIDE, r1, 256), F32),
        ((3, r1, 256), BF), ((3, r1, 256), BF), ((1, 256), F32),
        ((4, 4, 80, 128), BF), ((3, 4, 80, 128), BF), ((4, 80, 128), BF), ((3, 80, 128), BF),
        ((FEATS, 80, 128), BF), ((4, 4, 80, 128), BF),
        ((2, 512, 256), F32), ((r1, 256), BF), ((2, 512, 256), BF), ((2, 512, 256), BF),
        ((4, 4, 128, 128), BF), ((3, 4, 128, 128), BF),
        ((4, 128, 128), BF), ((3, 128, 128), BF), ((128, 128), BF), ((3, 32, 128), BF),
        ((4, 4, 32, 128), BF),
    ]
    outs = pl.pallas_call(
        step_kernel,
        out_shape=[
            jax.ShapeDtypeStruct((r3, 256), BF), jax.ShapeDtypeStruct((128, 512), F32),
            jax.ShapeDtypeStruct((256, 512), F32), jax.ShapeDtypeStruct((1, 256), F32),
        ],
        in_specs=[pl.BlockSpec(memory_space=pl.ANY)] * 10,
        out_specs=[vm] * 4,
        scratch_shapes=[pltpu.VMEM(s, t) for s, t in scratch] + [
            pltpu.SemaphoreType.DMA((N_COPIES,)), pltpu.SemaphoreType.DMA((N_COPIES,)),
            pltpu.SemaphoreType.DMA((10,)),
        ],
        compiler_params=pltpu.CompilerParams(
            collective_id=0, has_side_effects=True, vmem_limit_bytes=56 * 2**20
        ),
        cost_estimate=pl.CostEstimate(
            flops=14 * 10**9, bytes_accessed=8 * 2**20, transcendentals=512 * 256
        ),
        name="sage_step",
    )(features, w_one, w_two, b_one[None], b_two[None], owner_one[0].T, slot_one[0].T,
      owner_two[0].T, slot_two[0].T, cotangent[0])
    anywhere = pl.BlockSpec(memory_space=pl.ANY)
    layer_out, gw_one, gw_two, gb = pl.pallas_call(
        store_kernel,
        out_shape=[jax.ShapeDtypeStruct(o.shape, o.dtype) for o in outs],
        in_specs=[anywhere] * 4,
        out_specs=[anywhere] * 4,
        scratch_shapes=[pltpu.VMEM(o.shape, o.dtype) for o in outs]
        + [pltpu.SemaphoreType.DMA((8,))],
        compiler_params=pltpu.CompilerParams(vmem_limit_bytes=56 * 2**20),
        name="store_results",
    )(*outs)
    return layer_out[None], gw_one, gw_two, gb[0]


def solution(mesh):
    placed = (
        P(None, "node", "feat"),
        P("feat", None),
        P(),
        P(),
        P(),
        P("feat", "node", None),
        P("feat", "node", None),
        P("feat", "node", None),
        P("feat", "node", None),
        P("feat", "node", None),
    )
    return jax.shard_map(
        on_device,
        mesh=mesh,
        in_specs=placed,
        out_specs=(P("feat", "node", None), P("feat", None), P(), P()),
        check_vma=False,
    )
```

```python
import jax
import jax.numpy as jnp
from jax import lax
from jax.experimental import pallas as pl
from jax.experimental.pallas import tpu as pltpu
from jax.sharding import PartitionSpec as P

MESH = pl.DeviceIdType.MESH
PART = 256
FEATS = 8
SIDE = 4
FAN = 8
BF = jnp.bfloat16
F32 = jnp.float32
I32 = jnp.int32


def line_place(core, node):
    low, high = node % SIDE, node // SIDE
    return (1 - core) * low + core * high, (1 - core) * high + core * low


def node_at(core, u, v):
    return (1 - core) * (v * SIDE + u) + core * (u * SIDE + v)


def dot(a, b, dims=((1,), (0,))):
    return lax.dot_general(a, b, (dims, ((), ())), preferred_element_type=F32)


def add_up(first, others):
    total = first
    for other in others:
        total += other.astype(F32)
    return total


def step_kernel(
    feat_ref, w_one_ref, w_two_ref, b_one_ref, b_two_ref, owner_one_ref, slot_one_ref,
    owner_two_ref, slot_two_ref, cot_ref,
    out_ref, gw_one_ref, gw_two_ref, gb_ref,
    slab, w_parts, w_full, w_two, b_one, b_two, own_one, slo_one, own_two, slo_two, cot,
    asks_out, asks, asks_col, msg_two, gsum_two, gsend_two, grecv_two,
    gproj_two, ghid, table, self_one, ysum, ysend, yrecv, hidden, self_two,
    table_two, ysum_two, ysend_two, yrecv_two, glin, msg_one, gsum, gsend, grecv, bias,
    two_out, two_in, two_mid, two_v, two_z, two_all,
    wall, gtab, pair_out, pair_in, w_out, w_in, w_mid, v_in, z_out, z_in, piece_all,
    ssem, rsem, lsem,
):
    f, n = lax.axis_index("feat"), lax.axis_index("node")
    z, core = f // 2, f % 2
    u, v = line_place(core, n)
    rows_one = slab.shape[1]
    rows_two = own_one.shape[1]
    rows_three = own_two.shape[1]
    chunks = rows_one // PART
    tiles = rows_two // PART
    slots = [(dz, dc) for dz in range(4) for dc in range(2)]
    others = (2, 1, 3)

    def feat_dev(dz, dc):
        return (((z + dz + 4) % 4) * 2 + (core + dc) % 2, n)

    def u_dev(d):
        return (f, node_at(core, (u + d + SIDE) % SIDE, v))

    def v_dev(e):
        return (f, node_at(core, u, (v + e + SIDE) % SIDE))

    def place(r, q):
        return (1 - core) * q + core * r, (1 - core) * r + core * q

    def tile(j, size=PART):
        return pl.ds(pl.multiple_of(j * size, size), size)

    used = [0]
    groups = []

    def group(count):
        first = used[0]
        used[0] += count
        return first

    def describe(k, src, dst, dev):
        return pltpu.make_async_remote_copy(
            src_ref=src, dst_ref=dst, send_sem=ssem.at[k], recv_sem=rsem.at[k],
            device_id=dev, device_id_type=MESH,
        )

    def send(src, dst, dev):
        copy = describe(group(1), src, dst, dev)
        copy.start()
        groups.append(copy)
        return copy

    def arrived(copies):
        for copy in copies:
            copy.wait_recv()

    barrier = pltpu.get_barrier_semaphore()
    partners = [feat_dev(*s) for s in slots[1:]]
    partners += [u_dev(d) for d in range(1, SIDE)] + [v_dev(e) for e in range(1, SIDE)]
    for dev in partners:
        pl.semaphore_signal(barrier, inc=1, device_id=dev, device_id_type=MESH)

    loads = []

    def load(src, dst):
        copy = pltpu.make_async_copy(src, dst, lsem.at[len(loads)])
        copy.start()
        loads.append(copy)
        return copy

    index_loads = [
        load(owner_one_ref, own_one), load(slot_one_ref, slo_one),
        load(owner_two_ref, own_two), load(slot_two_ref, slo_two),
    ]
    cot_load = load(cot_ref, cot)
    w_one_load = load(w_one_ref, w_full.at[pl.ds(0, 128)])
    own_load = load(feat_ref.at[f], slab.at[0])
    small_loads = [load(w_two_ref, w_two), load(b_one_ref, b_one), load(b_two_ref, b_two)]

    pl.semaphore_wait(barrier, len(partners))

    low, high = n % SIDE, n // SIDE
    w_piece = w_one_ref.at[pl.ds(pl.multiple_of(high * 32, 32), 32),
                           pl.ds(pl.multiple_of(low * 128, 128), 128)]
    w_copies = [send(w_piece, w_parts.at[dz - 1, u, v], feat_dev(dz, 0)) for dz in others]
    slab_at = group(7 * chunks)

    def slab_copy(c, i):
        dev = feat_dev(*slots[i])
        return describe(slab_at + c * 7 + i - 1, feat_ref.at[dev[0], tile(c)],
                        slab.at[i, tile(c)], dev)

    def send_chunk(c, carry):
        for i in (4, 5, 2, 3, 6, 7, 1):
            slab_copy(c, i).start()
        return carry

    send_chunk(0, 0)
    w_pairs = [send(w_one_ref, w_full.at[pl.ds(128, 128)], feat_dev(0, 1))]

    for copy in index_loads:
        copy.wait()

    def ask_line(e, carry):
        for own, slo, lower in ((own_one, slo_one, 0), (own_two, slo_two, rows_two)):
            owner, slot = own[...], slo[...]
            found = []
            for d in range(SIDE):
                at = node_at(core, (u - d + SIDE) % SIDE, (v + e) % SIDE)
                found.append(jnp.max(jnp.where(owner == at, slot, -1), axis=0, keepdims=True))
            found.append(jnp.full((8 - SIDE, own.shape[1]), -1, I32))
            asks_out[e, :, lower:lower + own.shape[1]] = jnp.concatenate(found, axis=0)
        return carry

    lax.fori_loop(0, SIDE, ask_line, 0)
    cot_load.wait()
    msg_two[0] = (cot[...] / FAN).astype(BF)

    ask_copies = [send(asks_out.at[e], asks.at[e], v_dev(e)) for e in range(1, SIDE)]
    msg_two_copies = [send(msg_two.at[0], msg_two.at[e], v_dev(e)) for e in range(1, SIDE)]
    send_chunk(1, 0)

    arrived(w_copies)
    mine = w_parts.at[:, u, v]
    along_u = [send(mine, mine, u_dev(d)) for d in range(1, SIDE)]
    lax.fori_loop(2, chunks, send_chunk, 0)
    asks[0] = asks_out[0]
    arrived(ask_copies)

    def turn(e, carry):
        asks_col[e] = jnp.transpose(asks[e].astype(F32)).astype(I32)
        return carry

    lax.fori_loop(0, SIDE, turn, 0)
    arrived(along_u)
    mine = w_parts.at[:, :, v]
    along_v = [send(mine, mine, v_dev(e)) for e in range(1, SIDE)]

    def clear(j, carry):
        ysum[j] = jnp.zeros((rows_two, 256), F32)
        return carry

    lax.fori_loop(0, SIDE, clear, 0)
    bias[...] = jnp.zeros((1, 256), F32)

    arrived(msg_two_copies)
    back_two_at = group(3)

    def back_two(d):
        return describe(back_two_at + d - 1, gsend_two.at[d - 1], grecv_two.at[d - 1], u_dev(-d))

    def back_two_step(j, carry):
        d = (j + 1) % SIDE
        ids = lax.broadcasted_iota(I32, (rows_two, rows_three), 0)
        picks = jnp.concatenate(
            [(ids == asks[e, pl.ds(d, 1), rows_two:]).astype(BF) for e in range(SIDE)], axis=1
        )
        value = dot(picks, jnp.concatenate([msg_two[e] for e in range(SIDE)], axis=0))

        @pl.when(d > 0)
        def _():
            gsend_two[d - 1] = value.astype(BF)
            back_two(d).start()

        @pl.when(d == 0)
        def _():
            gsum_two[...] = value

        return carry

    lax.fori_loop(0, SIDE, back_two_step, 0)

    arrived(along_v)
    w_one_load.wait()

    for dz in range(1, SIDE):
        for r in range(4):
            for q in range(4):
                a, b = place(r, q)
                w_full[dz * 256 + r * 32:dz * 256 + r * 32 + 32, q * 128:q * 128 + 128] = (
                    w_parts[dz - 1, a, b]
                )
        w_pairs.append(send(w_full.at[pl.ds(dz * 256, 128)],
                            w_full.at[pl.ds(dz * 256 + 128, 128)], feat_dev(0, 1)))
    arrived(w_pairs)
    own_load.wait()

    table_at = group(3 * chunks)
    y_at = group(3 * tiles)

    def table_copy(c, d):
        return describe(table_at + c * 3 + d - 1, table.at[0, tile(c)], table.at[d, tile(c)],
                        u_dev(d))

    def y_copy(e, h):
        return describe(y_at + h * 3 + e - 1, ysend.at[e - 1, tile(h)], yrecv.at[e - 1, tile(h)],
                        v_dev(-e))

    def chunk_step(c, carry):
        @pl.when(c < chunks)
        def _():
            arrived([slab_copy(c, i) for i in range(1, FEATS)])
            block = jnp.concatenate([slab[i, tile(c)] for i in range(FEATS)], axis=1)
            table[0, tile(c)] = dot(block, w_full[:, 256:]).astype(BF)
            for d in others:
                table_copy(c, d).start()

            @pl.when(c < tiles)
            def _():
                self_one[tile(c)] = dot(block, w_full[:, :256])

        @pl.when(c > 1)
        def _():
            b = c - 2
            arrived([table_copy(b, d) for d in others])

            def sum_step(h, inner):
                ids = lax.broadcasted_iota(I32, (PART, PART), 1) + b * PART
                rows = jnp.concatenate([table[d, tile(b)] for d in range(SIDE)], axis=0)
                for e in (2, 1, 3, 0):
                    picks = jnp.concatenate(
                        [(ids == asks_col[e, tile(h), d:d + 1]).astype(BF)
                         for d in range(SIDE)], axis=1
                    )
                    ysum[e, tile(h)] += dot(picks, rows)

                @pl.when(b == chunks - 1)
                def _():
                    for e in others:
                        ysend[e - 1, tile(h)] = ysum[e, tile(h)].astype(BF)
                        y_copy(e, h).start()

                return inner

            lax.fori_loop(0, tiles, sum_step, 0)

        return carry

    lax.fori_loop(0, chunks + 2, chunk_step, 0)

    for copy in small_loads:
        copy.wait()
    arrived([back_two(d) for d in others])
    gproj_two[:rows_three, :256] = cot[...].astype(BF)
    gproj_two[rows_three:, :256] = jnp.zeros((rows_two - rows_three, 256), BF)

    total = add_up(gsum_two[...], [grecv_two[d] for d in range(SIDE - 1)])
    gproj_two[:, 256:] = total.astype(BF)
    ghid[...] = dot(gproj_two[...], w_two[...], ((1,), (1,)))

    msg_at = group(3 * tiles)

    def msg_copy(h, e):
        return describe(msg_at + h * 3 + e - 1, msg_one.at[0, tile(h)], msg_one.at[e, tile(h)],
                        v_dev(e))

    def act_step(h, carry):
        arrived([y_copy(e, h) for e in others])

        def rows_step(t, inner):
            rows = pl.ds(pl.multiple_of(h * PART + t * 128, 128), 128)
            total = add_up(ysum[0, rows], [yrecv[e, rows] for e in range(SIDE - 1)])
            linear = self_one[rows] + b_one[...] + total / FAN
            logistic = 1.0 / (1.0 + jnp.exp(-linear))
            grad = ghid[rows] * (logistic * (1.0 + linear * (1.0 - logistic)))
            msg_one[0, rows] = (grad / FAN).astype(BF)
            glin[rows] = grad.astype(BF)
            hidden[rows] = (linear * logistic).astype(BF)
            bias[...] += jnp.sum(grad, axis=0, keepdims=True)
            return inner

        lax.fori_loop(0, PART // 128, rows_step, 0)
        for e in others:
            msg_copy(h, e).start()
        return carry

    lax.fori_loop(0, tiles, act_step, 0)

    value = dot(hidden[...], gproj_two[...], ((0,), (0,))).astype(BF)
    for r in range(4):
        for q in range(4):
            a, b = place(r, q)
            two_out[a, b, :64] = value[r * 64:r * 64 + 64, q * 128:q * 128 + 128]
            two_out[a, b, 64:] = jnp.zeros((16, 128), BF)
    for q in range(2):
        a, b = place(0, q)
        two_out[a, b, 64:] = jnp.broadcast_to(bias[:, q * 128:q * 128 + 128], (16, 128)).astype(BF)
    two_u_copies = [
        send(two_out.at[(u + d) % SIDE], two_in.at[d - 1], u_dev(d)) for d in others
    ]

    proj = dot(hidden[...], w_two[...])
    table_two[0] = proj[:, 256:].astype(BF)
    self_two[...] = proj[:rows_three, :256]

    two_v_at = group(3)
    back_at = group(3)

    def two_v_copy(e):
        return describe(two_v_at + e - 1, two_mid.at[(v + e) % SIDE], two_v.at[e - 1], v_dev(e))

    def back_copy(d):
        return describe(back_at + d - 1, gsend.at[d - 1], grecv.at[d - 1], u_dev(-d))

    def line_grads(e, d):
        ids = lax.broadcasted_iota(I32, (rows_one, rows_two), 0)
        return dot((ids == asks[e, pl.ds(d, 1), :rows_two]).astype(BF), msg_one[e])

    def own_step(d, carry):
        gsum[d] = line_grads(0, d)
        return carry

    lax.fori_loop(0, SIDE, own_step, 0)
    arrived([msg_copy(h, e) for h in range(tiles) for e in others])

    def back_step(j, carry):
        d = (j + 1) % SIDE
        value = gsum[d]
        for e in range(1, SIDE):
            value += line_grads(e, d)

        @pl.when(d > 0)
        def _():
            gsend[d - 1] = value.astype(BF)
            back_copy(d).start()

        @pl.when(d == 0)
        def _():
            gsum[0] = value

        return carry

    lax.fori_loop(0, SIDE, back_step, 0)
    arrived(two_u_copies)
    for b in range(SIDE):
        two_mid[b] = add_up(
            two_out[u, b].astype(F32), [two_in[d, b] for d in range(SIDE - 1)]
        ).astype(BF)
    for e in others:
        two_v_copy(e).start()

    def outer(dc, grad):
        block = jnp.concatenate([slab[2 * dz + dc] for dz in range(4)], axis=1)
        return dot(block[:grad.shape[0]], grad[...], ((0,), (0,)))

    pair_out[0] = outer(1, glin).astype(BF)
    wall[0] = outer(0, glin)
    pairs = [send(pair_out.at[0], pair_in.at[0], feat_dev(0, 1))]
    arrived([two_v_copy(e) for e in others])
    two_z[0] = add_up(two_mid[v].astype(F32), [two_v[e] for e in range(SIDE - 1)]).astype(BF)
    two_z_copies = [
        send(two_z.at[0], two_z.at[i], feat_dev(*slots[i])) for i in range(1, FEATS)
    ]
    arrived(two_z_copies)
    two_all[u, v] = add_up(
        two_z[0].astype(F32), [two_z[i] for i in range(1, FEATS)]
    ).astype(BF)
    two_copies = [send(two_all.at[u, v], two_all.at[u, v], v_dev(e)) for e in others]
    for d in others:
        back_copy(d).wait_send()
    table_two_copies = [send(table_two.at[0], table_two.at[d], u_dev(d)) for d in others]
    arrived([back_copy(d) for d in others])
    gtab[...] = add_up(gsum[0], [grecv[d] for d in range(SIDE - 1)]).astype(BF)
    pair_out[1] = outer(1, gtab).astype(BF)
    pairs.append(send(pair_out.at[1], pair_in.at[1], feat_dev(0, 1)))
    wall[1] = outer(0, gtab)
    arrived(two_copies)
    two_copies = [send(two_all.at[u], two_all.at[u], u_dev(d)) for d in others]
    arrived(pairs)
    for k in range(2):
        value = (wall[k] + pair_in[k].astype(F32)).astype(BF)
        for dz in range(4):
            for r in range(4):
                for q in range(2):
                    a, b = place(r, 2 * k + q)
                    w_out[a, b, dz * 32:dz * 32 + 32] = value[
                        dz * 128 + r * 32:dz * 128 + r * 32 + 32, q * 128:q * 128 + 128]

    sums = [send(w_out.at[(u + d) % SIDE], w_in.at[d - 1], u_dev(d)) for d in others]

    arrived(two_copies)

    def lay_two(r, carry):
        for q in range(4):
            a, b = place(r, q)
            gw_two_ref[tile(r, 64), q * 128:q * 128 + 128] = two_all[a, b, :64].astype(F32)
        return carry

    lax.fori_loop(0, 4, lay_two, 0)
    for q in range(2):
        a, b = place(0, q)
        gb_ref[:, q * 128:q * 128 + 128] = two_all[a, b, 64:].astype(F32)[:1]
    arrived(sums)

    def mid_step(b, carry):
        w_mid[b] = add_up(
            w_out[u, b].astype(F32), [w_in[d, b] for d in range(SIDE - 1)]
        ).astype(BF)
        return carry

    lax.fori_loop(0, SIDE, mid_step, 0)
    sums = [send(w_mid.at[(v + e) % SIDE], v_in.at[e - 1], v_dev(e)) for e in others]

    arrived(table_two_copies)
    y_two_at = group(3)

    def y_two_copy(e):
        return describe(y_two_at + e - 1, ysend_two.at[e - 1], yrecv_two.at[e - 1], v_dev(-e))

    def y_two_step(j, carry):
        e = (j + 1) % SIDE
        ids = lax.broadcasted_iota(I32, (rows_three, rows_two), 1)
        picks = jnp.concatenate(
            [(ids == asks_col[e, rows_two:, d:d + 1]).astype(BF) for d in range(SIDE)], axis=1
        )
        value = dot(picks, jnp.concatenate([table_two[d] for d in range(SIDE)], axis=0))

        @pl.when(e > 0)
        def _():
            ysend_two[e - 1] = value.astype(BF)
            y_two_copy(e).start()

        @pl.when(e == 0)
        def _():
            ysum_two[...] = value

        return carry

    lax.fori_loop(0, SIDE, y_two_step, 0)

    arrived(sums)
    z_out[...] = add_up(w_mid[v].astype(F32), [v_in[e] for e in range(SIDE - 1)]).astype(BF)
    sums = [
        send(z_out.at[pl.ds(dz * 32, 32)], z_in.at[dz - 1], feat_dev(-dz, 0)) for dz in others
    ]
    arrived(sums)
    piece_all[u, v] = add_up(
        z_out[:32].astype(F32), [z_in[dz] for dz in range(3)]
    ).astype(BF)
    sums = [send(piece_all.at[u, v], piece_all.at[u, v], v_dev(e)) for e in others]
    arrived(sums)
    sums = [send(piece_all.at[u], piece_all.at[u], u_dev(d)) for d in others]
    arrived([y_two_copy(e) for e in others])

    def out_step(t, carry):
        total = add_up(ysum_two[tile(t, 64)], [yrecv_two[e, tile(t, 64)] for e in range(3)])
        out_ref[tile(t, 64)] = (self_two[tile(t, 64)] + b_two[...] + total / FAN).astype(BF)
        return carry

    lax.fori_loop(0, rows_three // 64, out_step, 0)

    arrived(sums)

    def lay_one(r, carry):
        for q in range(4):
            a, b = place(r, q)
            gw_one_ref[tile(r, 32), q * 128:q * 128 + 128] = piece_all[a, b].astype(F32)
        return carry

    lax.fori_loop(0, 4, lay_one, 0)
    for copy in groups:
        copy.wait_send()

    def sent(c, carry):
        for i in range(1, FEATS):
            slab_copy(c, i).wait_send()
        for d in others:
            table_copy(c, d).wait_send()
        return carry

    lax.fori_loop(0, chunks, sent, 0)

    def sent_tiles(t, carry):
        for d in others:
            y_copy(d, t).wait_send()
            msg_copy(t, d).wait_send()
        return carry

    lax.fori_loop(0, tiles, sent_tiles, 0)
    for e in others:
        two_v_copy(e).wait_send()
        y_two_copy(e).wait_send()
        back_two(e).wait_send()


def store_kernel(*refs):
    src, dst, held, sem = refs[:4], refs[4:8], refs[8:12], refs[12]
    reads = [pltpu.make_async_copy(src[i], held[i], sem.at[i]) for i in range(4)]
    writes = [pltpu.make_async_copy(held[i], dst[i], sem.at[4 + i]) for i in range(4)]
    for copy in reads:
        copy.start()
    for read, write in zip(reads, writes):
        read.wait()
        write.start()
    for copy in writes:
        copy.wait()


N_COPIES = 160


def on_device(
    features, w_one, w_two, b_one, b_two, owner_one, slot_one, owner_two, slot_two, cotangent
):
    r1, r2, r3 = features.shape[1], owner_one.shape[1], owner_two.shape[1]
    vm = pl.BlockSpec(memory_space=pltpu.VMEM)
    scratch = [
        ((FEATS, r1, 128), BF), ((3, 4, 4, 32, 128), BF), ((1024, 512), BF),
        ((256, 512), BF), ((1, 256), F32), ((1, 256), F32),
        ((FAN, r2), I32), ((FAN, r2), I32), ((FAN, r3), I32), ((FAN, r3), I32),
        ((r3, 256), F32), ((SIDE, 8, r2 + r3), I32),
        ((SIDE, 8, r2 + r3), I32), ((SIDE, r2 + r3, 8), I32),
        ((SIDE, r3, 256), BF), ((r2, 256), F32), ((3, r2, 256), BF), ((3, r2, 256), BF),
        ((r2, 512), BF), ((r2, 256), F32), ((SIDE, r1, 256), BF), ((r2, 256), F32),
        ((SIDE, r2, 256), F32), ((3, r2, 256), BF), ((3, r2, 256), BF), ((r2, 256), BF),
        ((r3, 256), F32), ((SIDE, r2, 256), BF), ((r3, 256), F32), ((3, r3, 256), BF),
        ((3, r3, 256), BF), ((r2, 256), BF), ((SIDE, r2, 256), BF), ((SIDE, r1, 256), F32),
        ((3, r1, 256), BF), ((3, r1, 256), BF), ((1, 256), F32),
        ((4, 4, 80, 128), BF), ((3, 4, 80, 128), BF), ((4, 80, 128), BF), ((3, 80, 128), BF),
        ((FEATS, 80, 128), BF), ((4, 4, 80, 128), BF),
        ((2, 512, 256), F32), ((r1, 256), BF), ((2, 512, 256), BF), ((2, 512, 256), BF),
        ((4, 4, 128, 128), BF), ((3, 4, 128, 128), BF),
        ((4, 128, 128), BF), ((3, 128, 128), BF), ((128, 128), BF), ((3, 32, 128), BF),
        ((4, 4, 32, 128), BF),
    ]
    outs = pl.pallas_call(
        step_kernel,
        out_shape=[
            jax.ShapeDtypeStruct((r3, 256), BF), jax.ShapeDtypeStruct((128, 512), F32),
            jax.ShapeDtypeStruct((256, 512), F32), jax.ShapeDtypeStruct((1, 256), F32),
        ],
        in_specs=[pl.BlockSpec(memory_space=pl.ANY)] * 10,
        out_specs=[vm] * 4,
        scratch_shapes=[pltpu.VMEM(s, t) for s, t in scratch] + [
            pltpu.SemaphoreType.DMA((N_COPIES,)), pltpu.SemaphoreType.DMA((N_COPIES,)),
            pltpu.SemaphoreType.DMA((10,)),
        ],
        compiler_params=pltpu.CompilerParams(
            collective_id=0, has_side_effects=True, vmem_limit_bytes=56 * 2**20
        ),
        cost_estimate=pl.CostEstimate(
            flops=14 * 10**9, bytes_accessed=8 * 2**20, transcendentals=512 * 256
        ),
        name="sage_step",
    )(features, w_one, w_two, b_one[None], b_two[None], owner_one[0].T, slot_one[0].T,
      owner_two[0].T, slot_two[0].T, cotangent[0])
    anywhere = pl.BlockSpec(memory_space=pl.ANY)
    layer_out, gw_one, gw_two, gb = pl.pallas_call(
        store_kernel,
        out_shape=[jax.ShapeDtypeStruct(o.shape, o.dtype) for o in outs],
        in_specs=[anywhere] * 4,
        out_specs=[anywhere] * 4,
        scratch_shapes=[pltpu.VMEM(o.shape, o.dtype) for o in outs]
        + [pltpu.SemaphoreType.DMA((8,))],
        compiler_params=pltpu.CompilerParams(vmem_limit_bytes=56 * 2**20),
        name="store_results",
    )(*outs)
    return layer_out[None], gw_one, gw_two, gb[0]


def solution(mesh):
    placed = (
        P(None, "node", "feat"),
        P("feat", None),
        P(),
        P(),
        P(),
        P("feat", "node", None),
        P("feat", "node", None),
        P("feat", "node", None),
        P("feat", "node", None),
        P("feat", "node", None),
    )
    return jax.shard_map(
        on_device,
        mesh=mesh,
        in_specs=placed,
        out_specs=(P("feat", "node", None), P("feat", None), P(), P()),
        check_vma=False,
    )
```

```python
import jax
import jax.numpy as jnp
from jax import lax
from jax.experimental import pallas as pl
from jax.experimental.pallas import tpu as pltpu
from jax.sharding import PartitionSpec as P

MESH = pl.DeviceIdType.MESH
PART = 256
FEATS = 8
SIDE = 4
FAN = 8
BF = jnp.bfloat16
F32 = jnp.float32
I32 = jnp.int32


def line_place(core, node):
    low, high = node % SIDE, node // SIDE
    return (1 - core) * low + core * high, (1 - core) * high + core * low


def node_at(core, u, v):
    return (1 - core) * (v * SIDE + u) + core * (u * SIDE + v)


def dot(a, b, dims=((1,), (0,))):
    return lax.dot_general(a, b, (dims, ((), ())), preferred_element_type=F32)


def add_up(first, others):
    total = first
    for other in others:
        total += other.astype(F32)
    return total


def step_kernel(
    feat_ref, w_one_ref, w_two_ref, b_one_ref, b_two_ref, owner_one_ref, slot_one_ref,
    owner_two_ref, slot_two_ref, cot_ref,
    out_ref, gw_one_ref, gw_two_ref, gb_ref,
    slab, w_parts, w_full, w_two, b_one, b_two, own_one, slo_one, own_two, slo_two, cot,
    asks_out, asks, asks_col, msg_two, gsum_two, gsend_two, grecv_two,
    gproj_two, ghid, table, self_one, ysum, ysend, yrecv, hidden, self_two,
    table_two, ysum_two, ysend_two, yrecv_two, glin, msg_one, gsum, gsend, grecv, bias,
    two_out, two_in, two_mid, two_v, two_z, two_all,
    wall, gtab, pair_out, pair_in, w_out, w_in, w_mid, v_in, z_out, z_in, piece_all,
    ssem, rsem, lsem,
):
    f, n = lax.axis_index("feat"), lax.axis_index("node")
    z, core = f // 2, f % 2
    u, v = line_place(core, n)
    rows_one = slab.shape[1]
    rows_two = own_one.shape[1]
    rows_three = own_two.shape[1]
    chunks = rows_one // PART
    tiles = rows_two // PART
    slots = [(dz, dc) for dz in range(4) for dc in range(2)]
    others = (2, 1, 3)

    def feat_dev(dz, dc):
        return (((z + dz + 4) % 4) * 2 + (core + dc) % 2, n)

    def u_dev(d):
        return (f, node_at(core, (u + d + SIDE) % SIDE, v))

    def v_dev(e):
        return (f, node_at(core, u, (v + e + SIDE) % SIDE))

    def place(r, q):
        return (1 - core) * q + core * r, (1 - core) * r + core * q

    def tile(j, size=PART):
        return pl.ds(pl.multiple_of(j * size, size), size)

    used = [0]
    groups = []

    def group(count):
        first = used[0]
        used[0] += count
        return first

    def describe(k, src, dst, dev):
        return pltpu.make_async_remote_copy(
            src_ref=src, dst_ref=dst, send_sem=ssem.at[k], recv_sem=rsem.at[k],
            device_id=dev, device_id_type=MESH,
        )

    def send(src, dst, dev):
        copy = describe(group(1), src, dst, dev)
        copy.start()
        groups.append(copy)
        return copy

    def arrived(copies):
        for copy in copies:
            copy.wait_recv()

    barrier = pltpu.get_barrier_semaphore()
    partners = [feat_dev(*s) for s in slots[1:]]
    partners += [u_dev(d) for d in range(1, SIDE)] + [v_dev(e) for e in range(1, SIDE)]
    for dev in partners:
        pl.semaphore_signal(barrier, inc=1, device_id=dev, device_id_type=MESH)

    loads = []

    def load(src, dst):
        copy = pltpu.make_async_copy(src, dst, lsem.at[len(loads)])
        copy.start()
        loads.append(copy)
        return copy

    index_loads = [
        load(owner_one_ref, own_one), load(slot_one_ref, slo_one),
        load(owner_two_ref, own_two), load(slot_two_ref, slo_two),
    ]
    cot_load = load(cot_ref, cot)
    w_one_load = load(w_one_ref, w_full.at[pl.ds(0, 128)])
    own_load = load(feat_ref.at[f], slab.at[0])
    small_loads = [load(w_two_ref, w_two), load(b_one_ref, b_one), load(b_two_ref, b_two)]

    pl.semaphore_wait(barrier, len(partners))

    low, high = n % SIDE, n // SIDE
    w_piece = w_one_ref.at[pl.ds(pl.multiple_of(high * 32, 32), 32),
                           pl.ds(pl.multiple_of(low * 128, 128), 128)]
    w_copies = [send(w_piece, w_parts.at[dz - 1, u, v], feat_dev(dz, 0)) for dz in others]
    slab_at = group(7 * chunks)

    def slab_copy(c, i):
        dev = feat_dev(*slots[i])
        return describe(slab_at + c * 7 + i - 1, feat_ref.at[dev[0], tile(c)],
                        slab.at[i, tile(c)], dev)

    def send_chunk(c, carry):
        for i in (4, 5, 2, 3, 6, 7, 1):
            slab_copy(c, i).start()
        return carry

    send_chunk(0, 0)
    w_pairs = [send(w_one_ref, w_full.at[pl.ds(128, 128)], feat_dev(0, 1))]

    for copy in index_loads:
        copy.wait()

    def ask_line(e, carry):
        for own, slo, lower in ((own_one, slo_one, 0), (own_two, slo_two, rows_two)):
            owner, slot = own[...], slo[...]
            found = []
            for d in range(SIDE):
                at = node_at(core, (u - d + SIDE) % SIDE, (v + e) % SIDE)
                found.append(jnp.max(jnp.where(owner == at, slot, -1), axis=0, keepdims=True))
            found.append(jnp.full((8 - SIDE, own.shape[1]), -1, I32))
            asks_out[e, :, lower:lower + own.shape[1]] = jnp.concatenate(found, axis=0)
        return carry

    lax.fori_loop(0, SIDE, ask_line, 0)
    cot_load.wait()
    msg_two[0] = (cot[...] / FAN).astype(BF)

    ask_copies = [send(asks_out.at[e], asks.at[e], v_dev(e)) for e in range(1, SIDE)]
    msg_two_copies = [send(msg_two.at[0], msg_two.at[e], v_dev(e)) for e in range(1, SIDE)]
    send_chunk(1, 0)

    arrived(w_copies)
    mine = w_parts.at[:, u, v]
    along_u = [send(mine, mine, u_dev(d)) for d in range(1, SIDE)]
    lax.fori_loop(2, chunks, send_chunk, 0)
    asks[0] = asks_out[0]
    arrived(ask_copies)

    def turn(e, carry):
        asks_col[e] = jnp.transpose(asks[e].astype(F32)).astype(I32)
        return carry

    lax.fori_loop(0, SIDE, turn, 0)
    arrived(along_u)
    mine = w_parts.at[:, :, v]
    along_v = [send(mine, mine, v_dev(e)) for e in range(1, SIDE)]

    def clear(j, carry):
        ysum[j] = jnp.zeros((rows_two, 256), F32)
        return carry

    lax.fori_loop(0, SIDE, clear, 0)
    bias[...] = jnp.zeros((1, 256), F32)

    arrived(msg_two_copies)
    back_two_at = group(3)

    def back_two(d):
        return describe(back_two_at + d - 1, gsend_two.at[d - 1], grecv_two.at[d - 1], u_dev(-d))

    def back_two_step(j, carry):
        d = (j + 1) % SIDE
        ids = lax.broadcasted_iota(I32, (rows_two, rows_three), 0)
        picks = jnp.concatenate(
            [(ids == asks[e, pl.ds(d, 1), rows_two:]).astype(BF) for e in range(SIDE)], axis=1
        )
        value = dot(picks, jnp.concatenate([msg_two[e] for e in range(SIDE)], axis=0))

        @pl.when(d > 0)
        def _():
            gsend_two[d - 1] = value.astype(BF)
            back_two(d).start()

        @pl.when(d == 0)
        def _():
            gsum_two[...] = value

        return carry

    lax.fori_loop(0, SIDE, back_two_step, 0)

    arrived(along_v)
    w_one_load.wait()

    for dz in range(1, SIDE):
        for r in range(4):
            for q in range(4):
                a, b = place(r, q)
                w_full[dz * 256 + r * 32:dz * 256 + r * 32 + 32, q * 128:q * 128 + 128] = (
                    w_parts[dz - 1, a, b]
                )
        w_pairs.append(send(w_full.at[pl.ds(dz * 256, 128)],
                            w_full.at[pl.ds(dz * 256 + 128, 128)], feat_dev(0, 1)))
    arrived(w_pairs)
    own_load.wait()

    table_at = group(3 * chunks)
    y_at = group(3 * tiles)

    def table_copy(c, d):
        return describe(table_at + c * 3 + d - 1, table.at[0, tile(c)], table.at[d, tile(c)],
                        u_dev(d))

    def y_copy(e, h):
        return describe(y_at + h * 3 + e - 1, ysend.at[e - 1, tile(h)], yrecv.at[e - 1, tile(h)],
                        v_dev(-e))

    def chunk_step(c, carry):
        @pl.when(c < chunks)
        def _():
            arrived([slab_copy(c, i) for i in range(1, FEATS)])
            block = jnp.concatenate([slab[i, tile(c)] for i in range(FEATS)], axis=1)
            table[0, tile(c)] = dot(block, w_full[:, 256:]).astype(BF)
            for d in others:
                table_copy(c, d).start()

            @pl.when(c < tiles)
            def _():
                self_one[tile(c)] = dot(block, w_full[:, :256])

        @pl.when(c > 1)
        def _():
            b = c - 2
            arrived([table_copy(b, d) for d in others])

            def sum_step(h, inner):
                ids = lax.broadcasted_iota(I32, (PART, PART), 1) + b * PART
                rows = jnp.concatenate([table[d, tile(b)] for d in range(SIDE)], axis=0)
                for e in (2, 1, 3, 0):
                    picks = jnp.concatenate(
                        [(ids == asks_col[e, tile(h), d:d + 1]).astype(BF)
                         for d in range(SIDE)], axis=1
                    )
                    ysum[e, tile(h)] += dot(picks, rows)

                @pl.when(b == chunks - 1)
                def _():
                    for e in others:
                        ysend[e - 1, tile(h)] = ysum[e, tile(h)].astype(BF)
                        y_copy(e, h).start()

                return inner

            lax.fori_loop(0, tiles, sum_step, 0)

        return carry

    lax.fori_loop(0, chunks + 2, chunk_step, 0)

    for copy in small_loads:
        copy.wait()
    arrived([back_two(d) for d in others])
    gproj_two[:rows_three, :256] = cot[...].astype(BF)
    gproj_two[rows_three:, :256] = jnp.zeros((rows_two - rows_three, 256), BF)

    total = add_up(gsum_two[...], [grecv_two[d] for d in range(SIDE - 1)])
    gproj_two[:, 256:] = total.astype(BF)
    ghid[...] = dot(gproj_two[...], w_two[...], ((1,), (1,)))

    msg_at = group(3 * tiles)

    def msg_copy(h, e):
        return describe(msg_at + h * 3 + e - 1, msg_one.at[0, tile(h)], msg_one.at[e, tile(h)],
                        v_dev(e))

    def act_step(h, carry):
        arrived([y_copy(e, h) for e in others])

        def rows_step(t, inner):
            rows = pl.ds(pl.multiple_of(h * PART + t * 128, 128), 128)
            total = add_up(ysum[0, rows], [yrecv[e, rows] for e in range(SIDE - 1)])
            linear = self_one[rows] + b_one[...] + total / FAN
            logistic = 1.0 / (1.0 + jnp.exp(-linear))
            grad = ghid[rows] * (logistic * (1.0 + linear * (1.0 - logistic)))
            msg_one[0, rows] = (grad / FAN).astype(BF)
            glin[rows] = grad.astype(BF)
            hidden[rows] = (linear * logistic).astype(BF)
            bias[...] += jnp.sum(grad, axis=0, keepdims=True)
            return inner

        lax.fori_loop(0, PART // 128, rows_step, 0)
        for e in others:
            msg_copy(h, e).start()
        return carry

    lax.fori_loop(0, tiles, act_step, 0)

    value = dot(hidden[...], gproj_two[...], ((0,), (0,))).astype(BF)
    for r in range(4):
        for q in range(4):
            a, b = place(r, q)
            two_out[a, b, :64] = value[r * 64:r * 64 + 64, q * 128:q * 128 + 128]
            two_out[a, b, 64:] = jnp.zeros((16, 128), BF)
    for q in range(2):
        a, b = place(0, q)
        two_out[a, b, 64:] = jnp.broadcast_to(bias[:, q * 128:q * 128 + 128], (16, 128)).astype(BF)

    proj = dot(hidden[...], w_two[...])
    table_two[0] = proj[:, 256:].astype(BF)
    self_two[...] = proj[:rows_three, :256]

    two_v_at = group(3)
    back_at = group(3)

    def two_v_copy(e):
        return describe(two_v_at + e - 1, two_mid.at[(v + e) % SIDE], two_v.at[e - 1], v_dev(e))

    def back_copy(d):
        return describe(back_at + d - 1, gsend.at[d - 1], grecv.at[d - 1], u_dev(-d))

    def line_grads(e, d):
        ids = lax.broadcasted_iota(I32, (rows_one, rows_two), 0)
        return dot((ids == asks[e, pl.ds(d, 1), :rows_two]).astype(BF), msg_one[e])

    def own_step(d, carry):
        gsum[d] = line_grads(0, d)
        return carry

    lax.fori_loop(0, SIDE, own_step, 0)
    arrived([msg_copy(h, e) for h in range(tiles) for e in others])
    two_u_copies = [
        send(two_out.at[(u + d) % SIDE], two_in.at[d - 1], u_dev(d)) for d in others
    ]

    def back_step(j, carry):
        d = (j + 1) % SIDE
        value = gsum[d]
        for e in range(1, SIDE):
            value += line_grads(e, d)

        @pl.when(d > 0)
        def _():
            gsend[d - 1] = value.astype(BF)
            back_copy(d).start()

        @pl.when(d == 0)
        def _():
            gsum[0] = value

        return carry

    lax.fori_loop(0, SIDE, back_step, 0)
    arrived(two_u_copies)
    for b in range(SIDE):
        two_mid[b] = add_up(
            two_out[u, b].astype(F32), [two_in[d, b] for d in range(SIDE - 1)]
        ).astype(BF)
    for e in others:
        two_v_copy(e).start()

    def outer(dc, grad):
        block = jnp.concatenate([slab[2 * dz + dc] for dz in range(4)], axis=1)
        return dot(block[:grad.shape[0]], grad[...], ((0,), (0,)))

    pair_out[0] = outer(1, glin).astype(BF)
    wall[0] = outer(0, glin)
    pairs = [send(pair_out.at[0], pair_in.at[0], feat_dev(0, 1))]
    arrived([two_v_copy(e) for e in others])
    two_z[0] = add_up(two_mid[v].astype(F32), [two_v[e] for e in range(SIDE - 1)]).astype(BF)
    two_z_copies = [
        send(two_z.at[0], two_z.at[i], feat_dev(*slots[i])) for i in range(1, FEATS)
    ]
    arrived(two_z_copies)
    two_all[u, v] = add_up(
        two_z[0].astype(F32), [two_z[i] for i in range(1, FEATS)]
    ).astype(BF)
    two_copies = [send(two_all.at[u, v], two_all.at[u, v], v_dev(e)) for e in others]
    for d in others:
        back_copy(d).wait_send()
    table_two_copies = [send(table_two.at[0], table_two.at[d], u_dev(d)) for d in others]
    arrived([back_copy(d) for d in others])
    gtab[...] = add_up(gsum[0], [grecv[d] for d in range(SIDE - 1)]).astype(BF)
    pair_out[1] = outer(1, gtab).astype(BF)
    pairs.append(send(pair_out.at[1], pair_in.at[1], feat_dev(0, 1)))
    wall[1] = outer(0, gtab)
    arrived(two_copies)
    two_copies = [send(two_all.at[u], two_all.at[u], u_dev(d)) for d in others]
    arrived(pairs)
    for k in range(2):
        value = (wall[k] + pair_in[k].astype(F32)).astype(BF)
        for dz in range(4):
            for r in range(4):
                for q in range(2):
                    a, b = place(r, 2 * k + q)
                    w_out[a, b, dz * 32:dz * 32 + 32] = value[
                        dz * 128 + r * 32:dz * 128 + r * 32 + 32, q * 128:q * 128 + 128]

    sums = [send(w_out.at[(u + d) % SIDE], w_in.at[d - 1], u_dev(d)) for d in others]

    arrived(two_copies)

    def lay_two(r, carry):
        for q in range(4):
            a, b = place(r, q)
            gw_two_ref[tile(r, 64), q * 128:q * 128 + 128] = two_all[a, b, :64].astype(F32)
        return carry

    lax.fori_loop(0, 4, lay_two, 0)
    for q in range(2):
        a, b = place(0, q)
        gb_ref[:, q * 128:q * 128 + 128] = two_all[a, b, 64:].astype(F32)[:1]
    arrived(sums)

    def mid_step(b, carry):
        w_mid[b] = add_up(
            w_out[u, b].astype(F32), [w_in[d, b] for d in range(SIDE - 1)]
        ).astype(BF)
        return carry

    lax.fori_loop(0, SIDE, mid_step, 0)
    sums = [send(w_mid.at[(v + e) % SIDE], v_in.at[e - 1], v_dev(e)) for e in others]

    arrived(table_two_copies)
    y_two_at = group(3)

    def y_two_copy(e):
        return describe(y_two_at + e - 1, ysend_two.at[e - 1], yrecv_two.at[e - 1], v_dev(-e))

    def y_two_step(j, carry):
        e = (j + 1) % SIDE
        ids = lax.broadcasted_iota(I32, (rows_three, rows_two), 1)
        picks = jnp.concatenate(
            [(ids == asks_col[e, rows_two:, d:d + 1]).astype(BF) for d in range(SIDE)], axis=1
        )
        value = dot(picks, jnp.concatenate([table_two[d] for d in range(SIDE)], axis=0))

        @pl.when(e > 0)
        def _():
            ysend_two[e - 1] = value.astype(BF)
            y_two_copy(e).start()

        @pl.when(e == 0)
        def _():
            ysum_two[...] = value

        return carry

    lax.fori_loop(0, SIDE, y_two_step, 0)

    arrived(sums)
    z_out[...] = add_up(w_mid[v].astype(F32), [v_in[e] for e in range(SIDE - 1)]).astype(BF)
    sums = [
        send(z_out.at[pl.ds(dz * 32, 32)], z_in.at[dz - 1], feat_dev(-dz, 0)) for dz in others
    ]
    arrived(sums)
    piece_all[u, v] = add_up(
        z_out[:32].astype(F32), [z_in[dz] for dz in range(3)]
    ).astype(BF)
    sums = [send(piece_all.at[u, v], piece_all.at[u, v], v_dev(e)) for e in others]
    arrived(sums)
    sums = [send(piece_all.at[u], piece_all.at[u], u_dev(d)) for d in others]
    arrived([y_two_copy(e) for e in others])

    def out_step(t, carry):
        total = add_up(ysum_two[tile(t, 64)], [yrecv_two[e, tile(t, 64)] for e in range(3)])
        out_ref[tile(t, 64)] = (self_two[tile(t, 64)] + b_two[...] + total / FAN).astype(BF)
        return carry

    lax.fori_loop(0, rows_three // 64, out_step, 0)

    arrived(sums)

    def lay_one(r, carry):
        for q in range(4):
            a, b = place(r, q)
            gw_one_ref[tile(r, 32), q * 128:q * 128 + 128] = piece_all[a, b].astype(F32)
        return carry

    lax.fori_loop(0, 4, lay_one, 0)
    for copy in groups:
        copy.wait_send()

    def sent(c, carry):
        for i in range(1, FEATS):
            slab_copy(c, i).wait_send()
        for d in others:
            table_copy(c, d).wait_send()
        return carry

    lax.fori_loop(0, chunks, sent, 0)

    def sent_tiles(t, carry):
        for d in others:
            y_copy(d, t).wait_send()
            msg_copy(t, d).wait_send()
        return carry

    lax.fori_loop(0, tiles, sent_tiles, 0)
    for e in others:
        two_v_copy(e).wait_send()
        y_two_copy(e).wait_send()
        back_two(e).wait_send()


def store_kernel(*refs):
    src, dst, held, sem = refs[:4], refs[4:8], refs[8:12], refs[12]
    reads = [pltpu.make_async_copy(src[i], held[i], sem.at[i]) for i in range(4)]
    writes = [pltpu.make_async_copy(held[i], dst[i], sem.at[4 + i]) for i in range(4)]
    for copy in reads:
        copy.start()
    for read, write in zip(reads, writes):
        read.wait()
        write.start()
    for copy in writes:
        copy.wait()


N_COPIES = 160


def on_device(
    features, w_one, w_two, b_one, b_two, owner_one, slot_one, owner_two, slot_two, cotangent
):
    r1, r2, r3 = features.shape[1], owner_one.shape[1], owner_two.shape[1]
    vm = pl.BlockSpec(memory_space=pltpu.VMEM)
    scratch = [
        ((FEATS, r1, 128), BF), ((3, 4, 4, 32, 128), BF), ((1024, 512), BF),
        ((256, 512), BF), ((1, 256), F32), ((1, 256), F32),
        ((FAN, r2), I32), ((FAN, r2), I32), ((FAN, r3), I32), ((FAN, r3), I32),
        ((r3, 256), F32), ((SIDE, 8, r2 + r3), I32),
        ((SIDE, 8, r2 + r3), I32), ((SIDE, r2 + r3, 8), I32),
        ((SIDE, r3, 256), BF), ((r2, 256), F32), ((3, r2, 256), BF), ((3, r2, 256), BF),
        ((r2, 512), BF), ((r2, 256), F32), ((SIDE, r1, 256), BF), ((r2, 256), F32),
        ((SIDE, r2, 256), F32), ((3, r2, 256), BF), ((3, r2, 256), BF), ((r2, 256), BF),
        ((r3, 256), F32), ((SIDE, r2, 256), BF), ((r3, 256), F32), ((3, r3, 256), BF),
        ((3, r3, 256), BF), ((r2, 256), BF), ((SIDE, r2, 256), BF), ((SIDE, r1, 256), F32),
        ((3, r1, 256), BF), ((3, r1, 256), BF), ((1, 256), F32),
        ((4, 4, 80, 128), BF), ((3, 4, 80, 128), BF), ((4, 80, 128), BF), ((3, 80, 128), BF),
        ((FEATS, 80, 128), BF), ((4, 4, 80, 128), BF),
        ((2, 512, 256), F32), ((r1, 256), BF), ((2, 512, 256), BF), ((2, 512, 256), BF),
        ((4, 4, 128, 128), BF), ((3, 4, 128, 128), BF),
        ((4, 128, 128), BF), ((3, 128, 128), BF), ((128, 128), BF), ((3, 32, 128), BF),
        ((4, 4, 32, 128), BF),
    ]
    outs = pl.pallas_call(
        step_kernel,
        out_shape=[
            jax.ShapeDtypeStruct((r3, 256), BF), jax.ShapeDtypeStruct((128, 512), F32),
            jax.ShapeDtypeStruct((256, 512), F32), jax.ShapeDtypeStruct((1, 256), F32),
        ],
        in_specs=[pl.BlockSpec(memory_space=pl.ANY)] * 10,
        out_specs=[vm] * 4,
        scratch_shapes=[pltpu.VMEM(s, t) for s, t in scratch] + [
            pltpu.SemaphoreType.DMA((N_COPIES,)), pltpu.SemaphoreType.DMA((N_COPIES,)),
            pltpu.SemaphoreType.DMA((10,)),
        ],
        compiler_params=pltpu.CompilerParams(
            collective_id=0, has_side_effects=True, vmem_limit_bytes=56 * 2**20
        ),
        cost_estimate=pl.CostEstimate(
            flops=14 * 10**9, bytes_accessed=8 * 2**20, transcendentals=512 * 256
        ),
        name="sage_step",
    )(features, w_one, w_two, b_one[None], b_two[None], owner_one[0].T, slot_one[0].T,
      owner_two[0].T, slot_two[0].T, cotangent[0])
    anywhere = pl.BlockSpec(memory_space=pl.ANY)
    layer_out, gw_one, gw_two, gb = pl.pallas_call(
        store_kernel,
        out_shape=[jax.ShapeDtypeStruct(o.shape, o.dtype) for o in outs],
        in_specs=[anywhere] * 4,
        out_specs=[anywhere] * 4,
        scratch_shapes=[pltpu.VMEM(o.shape, o.dtype) for o in outs]
        + [pltpu.SemaphoreType.DMA((8,))],
        compiler_params=pltpu.CompilerParams(vmem_limit_bytes=56 * 2**20),
        name="store_results",
    )(*outs)
    return layer_out[None], gw_one, gw_two, gb[0]


def solution(mesh):
    placed = (
        P(None, "node", "feat"),
        P("feat", None),
        P(),
        P(),
        P(),
        P("feat", "node", None),
        P("feat", "node", None),
        P("feat", "node", None),
        P("feat", "node", None),
        P("feat", "node", None),
    )
    return jax.shard_map(
        on_device,
        mesh=mesh,
        in_specs=placed,
        out_specs=(P("feat", "node", None), P("feat", None), P(), P()),
        check_vma=False,
    )
```
